512 devices in a mesh: layer: 4 (over x), row: 8 (over z), col: 16 (over y, core).
Axes of the slice: x: 4, y: 8, z: 8, core: 2. Of those that a mesh axis runs over, the one named last changes fastest.
Arguments:
- a_vals: bfloat16 [4, 8, 16, 12, 128, 128], P('layer', 'row', 'col'), may hold values from -0.109375 to 0.109375
- a_rows: int32 [4, 8, 16, 12], P('layer', 'row', 'col'), may hold values from 0 to 31, as said below
- a_ks: int32 [4, 8, 16, 12], P('layer', 'row', 'col'), may hold values from 0 to 7
- a_live: int32 [4, 8, 16], P('layer', 'row', 'col'), may hold values from 6 to 12, as said below
- b_vals: bfloat16 [512, 16, 2, 128, 128], P(('layer', 'row'), 'col'), may hold values from -6 to 6
- b_cols: int32 [512, 16, 2], P(('layer', 'row'), 'col'), may hold values from 0 to 1, as said below
Outputs:
- product: float32 [128, 256, 32, 128], P('layer', 'row', 'col')
The draws below stay inside these ranges and needn't reach their ends.
Inputs may be any that keep to these rules, and one draw needn't show every extreme that they name: On each device the pairs (a_rows, a_ks) of the 12 slots are all different. `a_live`: in every draw some device has all 12 slots live. `b_cols`: the 2 block columns of one block row and col index are all different.
All inputs are finite; a program needn't handle non-finite values.
Results may differ from the reference program's by a relative error of at most 0.0003.
Values may be sent and summed in bfloat16 or wider, within the bound.
No kernel may reach another device: no remote copies, remote signals or barrier semaphores. Data moves between devices by JAX's collectives and lax.ppermute only.
A program may use at most 64 MiB of HBM per device.

```python
import jax
import jax.numpy as jnp
from jax import lax

BS = 128
BLK_DEV = 8
SA = 12
PB = 2
RB_DEV = 32
CB_DEV = 2
NBLK = 512
RB = 256
CB = 32
N_LAYER = 4
N_ROW = 8
N_COL = 16


def slot_pattern(key):
    count = N_LAYER * N_ROW * N_COL
    keys = jax.random.split(key, count)
    perms = jax.vmap(lambda one: jax.random.permutation(one, RB_DEV * BLK_DEV))(keys)[:, :SA]
    return perms.reshape(N_LAYER, N_ROW, N_COL, SA).astype(jnp.int32)


def draw_a_rows(key, part):
    return slot_pattern(key) // BLK_DEV


def draw_a_ks(key, part):
    return slot_pattern(key) % BLK_DEV


def draw_a_live(key, part):
    key = jax.random.fold_in(key, 11)
    first, second = jax.random.split(key)
    count = N_LAYER * N_ROW * N_COL
    live = jax.random.randint(first, (count,), SA // 2, SA + 1)
    fullest = jax.random.randint(second, (), 0, count)
    live = jnp.where(jnp.arange(count) == fullest, SA, live)
    return live.reshape(N_LAYER, N_ROW, N_COL).astype(jnp.int32)


def draw_b_cols(key, part):
    key = jax.random.fold_in(key, 23)
    count = NBLK * N_COL
    keys = jax.random.split(key, count)
    perms = jax.vmap(lambda one: jax.random.permutation(one, CB_DEV))(keys)[:, :PB]
    return perms.reshape(NBLK, N_COL, PB).astype(jnp.int32)


def steps_of(stream_key, shape, pieces, low, high):
    loudness, own = 1.0, jax.random.fold_in(stream_key, 6)
    for position, shards_of in pieces:
        steps = jnp.exp(jax.random.uniform(jax.random.fold_in(own, position), (shards_of,), jnp.float32, low / len(pieces), high / len(pieces)))
        loudness = loudness * jnp.repeat(steps, shape[position] // shards_of).reshape([-1 if axis == position else 1 for axis in range(len(shape))])
    return loudness


def scatter_about(own_key, shape, scale, bound, pieces=(), kind=jnp.bfloat16):
    gain = steps_of(own_key, shape, pieces, -0.22, 0.18) if pieces else 1.0
    values = jax.random.normal(own_key, shape, jnp.float32) * scale * gain
    return jnp.minimum(jnp.maximum(values, -bound), bound).astype(kind)


def setup_inputs(seed: int = 0) -> dict:
    streams_of = jax.random.split(jax.random.key(seed), 7)
    a_vals = scatter_about(streams_of[0], (N_LAYER, N_ROW, N_COL, SA, BS, BS), (BS * N_LAYER * N_COL * SA * PB // (RB_DEV * CB_DEV)) ** -0.5, 0.109375, ((0, 4), (1, 8), (2, 16)))
    a_rows = draw_a_rows(jax.random.fold_in(streams_of[6], 71), 0)
    a_ks = draw_a_ks(jax.random.fold_in(streams_of[6], 71), 0)
    a_live = draw_a_live(jax.random.fold_in(streams_of[6], 71), 0)
    b_vals = scatter_about(streams_of[4], (NBLK, N_COL, PB, BS, BS), 1.0, 6.0, ((0, 32), (1, 16)))
    b_cols = draw_b_cols(jax.random.fold_in(streams_of[6], 71), 0)
    return dict(a_vals=a_vals, a_rows=a_rows, a_ks=a_ks, a_live=a_live, b_vals=b_vals, b_cols=b_cols)


def reference(a_vals, a_rows, a_ks, a_live, b_vals, b_cols):
    count = N_LAYER * N_ROW * N_COL
    layer_width = BLK_DEV * N_COL
    all_vals = a_vals.reshape(count, SA, BS, BS)
    all_rows = a_rows.reshape(count, SA)
    all_ks = a_ks.reshape(count, SA)
    all_live = a_live.reshape(count)
    slot_index = jnp.arange(SA, dtype=jnp.int32)
    col_index = jnp.arange(N_COL, dtype=jnp.int32)

    def step(total, which):
        layer_now = which // (N_ROW * N_COL)
        row_now = (which // N_COL) % N_ROW
        col_now = which % N_COL
        keep = (slot_index < all_live[which]).astype(jnp.float32)
        values = all_vals[which].astype(jnp.float32) * keep[:, None, None]
        global_k = (layer_now * layer_width + col_now * BLK_DEV + all_ks[which]).astype(jnp.int32)
        chosen = b_vals[global_k].astype(jnp.float32)
        prods = jnp.einsum("sxz,scpzy->xscpy", values, chosen, precision=lax.Precision.HIGHEST)
        row_global = row_now * RB_DEV + all_rows[which]
        col_global = col_index[None, :, None] * CB_DEV + b_cols[global_k]
        target = (row_global[:, None, None] * CB + col_global).reshape(-1)
        return total.at[:, target].add(prods.reshape(BS, SA * N_COL * PB, BS)), None

    start = jnp.zeros((BS, RB * CB, BS), jnp.float32)
    total, unused = lax.scan(step, start, jnp.arange(count, dtype=jnp.int32))
    return total.reshape(BS, RB, CB, BS)
```

```python
import jax
import jax.numpy as jnp
from jax import lax
from jax.experimental import pallas as pl
from jax.experimental.pallas import tpu as pltpu
from jax.sharding import PartitionSpec as P

BS = 128
BLK_DEV = 8
SA = 12
PB = 2
RB_DEV = 32
CB_DEV = 2
N_LAYER = 4
N_ROW = 8
N_COL = 16
K_DEV = 16
XQ = BS // N_LAYER
A_ROWS = SA * BS
POS_ROWS = 16
MSG_ROWS = RB_DEV * XQ + RB_DEV
BITS = 13.0
LN2 = 0.6931471805599453


def piece_of(me, place):
    return lax.rem(me + place, N_ROW)


def products_kernel(me_ref, rows_ref, ks_ref, a_ref, *refs):
    b_refs = refs[:N_ROW]
    own_ref = refs[N_ROW]
    msg_refs = refs[N_ROW + 1 : N_ROW + N_LAYER]
    a_in, b_in, acc, top, a_sem, b_sem = refs[N_ROW + N_LAYER :]
    row = me_ref[0]
    layer = me_ref[1]

    def a_copy(place):
        first = 2 * piece_of(row, place)
        return pltpu.make_async_copy(
            a_ref.at[pl.ds(first, 2), pl.ds(0, A_ROWS)], a_in.at[place], a_sem.at[place]
        )

    def b_copy(place):
        return pltpu.make_async_copy(b_refs[place], b_in.at[place], b_sem.at[place])

    for place in range(N_ROW):
        a_copy(place).start()
        b_copy(place).start()

    def clear(i, carry):
        acc[i] = jnp.zeros((BS, BS), jnp.float32)
        return carry

    lax.fori_loop(0, RB_DEV, clear, 0)

    for place in range(N_ROW):
        a_copy(place).wait()
        b_copy(place).wait()

        def half(h, carry):
            base = (2 * piece_of(row, place) + h) * SA
            for s in range(SA):
                target = rows_ref[base + s]
                k = ks_ref[base + s]
                acc[target] += jnp.dot(
                    a_in[place, h, pl.ds(s * BS, BS), :],
                    b_in[place, h * BLK_DEV + k],
                    preferred_element_type=jnp.float32,
                )
            return carry

        lax.fori_loop(0, 2, half, 0)

    def keep(i, carry):
        own_ref[i] = acc[i, pl.ds(layer * XQ, XQ), :]
        for q in range(1, N_LAYER):
            start = lax.rem(layer + q, N_LAYER) * XQ
            part = acc[i, pl.ds(start, XQ), :]
            top[q - 1, pl.ds(i, 1), :] = jnp.max(jnp.abs(part), axis=0, keepdims=True)
        return carry

    lax.fori_loop(0, RB_DEV, keep, 0)
    for q in range(1, N_LAYER):
        power = jnp.floor(jnp.log(jnp.maximum(top[q - 1], 1e-30)) * (1.0 / LN2))
        msg_refs[q - 1][pl.ds(RB_DEV * XQ, RB_DEV), :] = power.astype(jnp.int32).astype(jnp.int16)
        top[q - 1] = jnp.exp((BITS - power) * LN2)

    def pack(i, carry):
        for q in range(1, N_LAYER):
            start = lax.rem(layer + q, N_LAYER) * XQ
            part = acc[i, pl.ds(start, XQ), :] * top[q - 1, pl.ds(i, 1), :]
            msg_refs[q - 1][pl.ds(pl.multiple_of(i * XQ, XQ), XQ), :] = (
                jnp.round(part).astype(jnp.int32).astype(jnp.int16)
            )
        return carry

    lax.fori_loop(0, RB_DEV, pack, 0)


def products(me, rows, ks, a_all, pieces):
    any_spec = pl.BlockSpec(memory_space=pl.ANY)
    smem = pl.BlockSpec(memory_space=pltpu.SMEM)
    vmem = pl.BlockSpec(memory_space=pltpu.VMEM)
    return pl.pallas_call(
        products_kernel,
        out_shape=[jax.ShapeDtypeStruct((RB_DEV, XQ, BS), jnp.float32)]
        + [jax.ShapeDtypeStruct((MSG_ROWS, BS), jnp.int16)] * (N_LAYER - 1),
        in_specs=[smem] * 3 + [any_spec] * (1 + N_ROW),
        out_specs=[vmem] * N_LAYER,
        scratch_shapes=[
            pltpu.VMEM((N_ROW, 2, A_ROWS, BS), jnp.bfloat16),
            pltpu.VMEM((N_ROW, K_DEV, BS, BS), jnp.bfloat16),
            pltpu.VMEM((RB_DEV + 1, BS, BS), jnp.float32),
            pltpu.VMEM((N_LAYER - 1, RB_DEV, BS), jnp.float32),
            pltpu.SemaphoreType.DMA((N_ROW,)),
            pltpu.SemaphoreType.DMA((N_ROW,)),
        ],
        compiler_params=pltpu.CompilerParams(vmem_limit_bytes=40 * 2**20),
        cost_estimate=pl.CostEstimate(
            flops=2 * N_COL * SA * BS**3, bytes_accessed=16 * 2**20, transcendentals=0
        ),
        name="products",
    )(me, rows, ks, a_all, *pieces)


def combine_kernel(*refs):
    out_ref = refs[-2]
    scale = refs[-1]
    for j in range(CB_DEV):
        own = refs[j * N_LAYER]
        msgs = refs[j * N_LAYER + 1 : (j + 1) * N_LAYER]
        for q in range(N_LAYER - 1):
            power = msgs[q][pl.ds(RB_DEV * XQ, RB_DEV), :].astype(jnp.int32).astype(jnp.float32)
            scale[q] = jnp.exp((power - BITS) * LN2)

        def step(i, carry):
            total = own[i]
            for q in range(N_LAYER - 1):
                part = msgs[q][pl.ds(pl.multiple_of(i * XQ, XQ), XQ), :]
                total = total + part.astype(jnp.int32).astype(jnp.float32) * scale[q, pl.ds(i, 1), :]
            out_ref[pl.ds(CB_DEV * i + j, XQ, stride=RB_DEV * CB_DEV), :] = total
            return carry

        lax.fori_loop(0, RB_DEV, step, 0)


def combine(parts):
    vmem = pl.BlockSpec(memory_space=pltpu.VMEM)
    return pl.pallas_call(
        combine_kernel,
        out_shape=jax.ShapeDtypeStruct((XQ * RB_DEV * CB_DEV, BS), jnp.float32),
        in_specs=[vmem] * len(parts),
        out_specs=vmem,
        scratch_shapes=[pltpu.VMEM((N_LAYER - 1, RB_DEV, BS), jnp.float32)],
        compiler_params=pltpu.CompilerParams(vmem_limit_bytes=24 * 2**20),
        name="combine",
    )(*parts)


def shifted(value, axis, size, by):
    return lax.ppermute(value, axis, [(i, (i + by) % size) for i in range(size)])


def around(first, forward, backward):
    pieces = [first] + [None] * (N_ROW - 1)
    moving = first
    for step in range(1, forward + 1):
        moving = shifted(moving, "row", N_ROW, 1)
        pieces[N_ROW - step] = moving
    moving = first
    for step in range(1, backward + 1):
        moving = shifted(moving, "row", N_ROW, -1)
        pieces[step] = moving
    return pieces


def send_sums(parts):
    own, msgs = parts[0], parts[1:]
    return [own] + [shifted(msgs[q - 1], "layer", N_LAYER, q) for q in range(1, N_LAYER)]


def body(a_vals, a_rows, a_ks, a_live, b_vals, b_cols):
    me = jnp.stack([lax.axis_index("row"), lax.axis_index("layer")]).astype(jnp.int32)
    live = jnp.arange(SA, dtype=jnp.int32) < a_live.reshape(())
    target = jnp.where(live, a_rows.reshape(SA), RB_DEV)
    position = jnp.zeros((POS_ROWS, BS), jnp.bfloat16)
    position = position.at[0, :SA].set(target.astype(jnp.bfloat16))
    position = position.at[1, :SA].set(a_ks.reshape(SA).astype(jnp.bfloat16))
    a_send = jnp.concatenate([a_vals.reshape(A_ROWS, BS), position], axis=0)
    a_all = lax.all_gather(a_send, "col", axis=0)
    positions = a_all[:, A_ROWS : A_ROWS + 2, :SA].astype(jnp.int32)
    rows = positions[:, 0].reshape(N_COL * SA)
    ks = positions[:, 1].reshape(N_COL * SA)

    b_vals = b_vals.reshape(K_DEV, PB, BS, BS)
    straight = (b_cols.reshape(K_DEV, PB)[:, 0] == 0)[:, None, None]
    b_zero = jnp.where(straight, b_vals[:, 0], b_vals[:, 1])
    b_one = jnp.where(straight, b_vals[:, 1], b_vals[:, 0])

    pieces_zero = around(b_zero, 4, 3)
    b_one, unused = lax.optimization_barrier((b_one, pieces_zero[3]))
    pieces_one = around(b_one, 3, 4)
    parts = send_sums(products(me, rows, ks, a_all, pieces_zero))
    parts += send_sums(products(me, rows, ks, a_all, pieces_one))
    return combine(parts).reshape(XQ, RB_DEV, CB_DEV, BS)


def solution(mesh):
    return jax.shard_map(
        body,
        mesh=mesh,
        in_specs=(
            P("layer", "row", "col", None, None, None),
            P("layer", "row", "col", None),
            P("layer", "row", "col", None),
            P("layer", "row", "col"),
            P(("layer", "row"), "col", None, None, None),
            P(("layer", "row"), "col", None),
        ),
        out_specs=P("layer", "row", "col", None),
        check_vma=False,
    )
```

```python
import jax
import jax.numpy as jnp
from jax import lax
from jax.experimental import pallas as pl
from jax.experimental.pallas import tpu as pltpu
from jax.sharding import PartitionSpec as P

BS = 128
BLK_DEV = 8
SA = 12
PB = 2
RB_DEV = 32
CB_DEV = 2
N_LAYER = 4
N_ROW = 8
N_COL = 16
K_DEV = 16
XQ = BS // N_LAYER
A_ROWS = SA * BS
POS_ROWS = 16
MSG_ROWS = RB_DEV * XQ + RB_DEV
BITS = 13.0
LN2 = 0.6931471805599453


def piece_of(me, place):
    return lax.rem(me + place, N_ROW)


def products_kernel(me_ref, rows_ref, ks_ref, a_ref, *refs):
    b_refs = refs[:N_ROW]
    own_ref = refs[N_ROW]
    msg_refs = refs[N_ROW + 1 : N_ROW + N_LAYER]
    acc, top = refs[N_ROW + N_LAYER :]
    row = me_ref[0]
    layer = me_ref[1]

    def clear(i, carry):
        acc[i] = jnp.zeros((BS, BS), jnp.float32)
        return carry

    lax.fori_loop(0, RB_DEV, clear, 0)

    for place in range(N_ROW):

        def half(h, carry):
            col = 2 * piece_of(row, place) + h
            base = col * SA
            for s in range(SA):
                target = rows_ref[base + s]
                k = ks_ref[base + s]
                acc[target] += jnp.dot(
                    a_ref[col, pl.ds(s * BS, BS), :],
                    b_refs[place][h * BLK_DEV + k],
                    preferred_element_type=jnp.float32,
                )
            return carry

        lax.fori_loop(0, 2, half, 0)

    def keep(i, carry):
        own_ref[i] = acc[i, pl.ds(layer * XQ, XQ), :]
        for q in range(1, N_LAYER):
            start = lax.rem(layer + q, N_LAYER) * XQ
            part = acc[i, pl.ds(start, XQ), :]
            top[q - 1, pl.ds(i, 1), :] = jnp.max(jnp.abs(part), axis=0, keepdims=True)
        return carry

    lax.fori_loop(0, RB_DEV, keep, 0)
    for q in range(1, N_LAYER):
        power = jnp.floor(jnp.log(jnp.maximum(top[q - 1], 1e-30)) * (1.0 / LN2))
        msg_refs[q - 1][pl.ds(RB_DEV * XQ, RB_DEV), :] = power.astype(jnp.int32).astype(jnp.int16)
        top[q - 1] = jnp.exp((BITS - power) * LN2)

    def pack(i, carry):
        for q in range(1, N_LAYER):
            start = lax.rem(layer + q, N_LAYER) * XQ
            part = acc[i, pl.ds(start, XQ), :] * top[q - 1, pl.ds(i, 1), :]
            msg_refs[q - 1][pl.ds(pl.multiple_of(i * XQ, XQ), XQ), :] = (
                jnp.round(part).astype(jnp.int32).astype(jnp.int16)
            )
        return carry

    lax.fori_loop(0, RB_DEV, pack, 0)


def products(me, rows, ks, a_all, pieces):
    smem = pl.BlockSpec(memory_space=pltpu.SMEM)
    vmem = pl.BlockSpec(memory_space=pltpu.VMEM)
    return pl.pallas_call(
        products_kernel,
        out_shape=[jax.ShapeDtypeStruct((RB_DEV, XQ, BS), jnp.float32)]
        + [jax.ShapeDtypeStruct((MSG_ROWS, BS), jnp.int16)] * (N_LAYER - 1),
        in_specs=[smem] * 3 + [vmem] * (1 + N_ROW),
        out_specs=[vmem] * N_LAYER,
        scratch_shapes=[
            pltpu.VMEM((RB_DEV + 1, BS, BS), jnp.float32),
            pltpu.VMEM((N_LAYER - 1, RB_DEV, BS), jnp.float32),
        ],
        compiler_params=pltpu.CompilerParams(vmem_limit_bytes=8 * 2**20),
        cost_estimate=pl.CostEstimate(
            flops=2 * N_COL * SA * BS**3, bytes_accessed=16 * 2**20, transcendentals=0
        ),
        name="products",
    )(me, rows, ks, a_all, *pieces)


def combine_kernel(*refs):
    out_ref = refs[-2]
    scale = refs[-1]
    for j in range(CB_DEV):
        own = refs[j * N_LAYER]
        msgs = refs[j * N_LAYER + 1 : (j + 1) * N_LAYER]
        for q in range(N_LAYER - 1):
            power = msgs[q][pl.ds(RB_DEV * XQ, RB_DEV), :].astype(jnp.int32).astype(jnp.float32)
            scale[q] = jnp.exp((power - BITS) * LN2)

        def step(i, carry):
            total = own[i]
            for q in range(N_LAYER - 1):
                part = msgs[q][pl.ds(pl.multiple_of(i * XQ, XQ), XQ), :]
                total = total + part.astype(jnp.int32).astype(jnp.float32) * scale[q, pl.ds(i, 1), :]
            out_ref[pl.ds(CB_DEV * i + j, XQ, stride=RB_DEV * CB_DEV), :] = total
            return carry

        lax.fori_loop(0, RB_DEV, step, 0)


def combine(parts):
    vmem = pl.BlockSpec(memory_space=pltpu.VMEM)
    return pl.pallas_call(
        combine_kernel,
        out_shape=jax.ShapeDtypeStruct((XQ * RB_DEV * CB_DEV, BS), jnp.float32),
        in_specs=[vmem] * len(parts),
        out_specs=vmem,
        scratch_shapes=[pltpu.VMEM((N_LAYER - 1, RB_DEV, BS), jnp.float32)],
        compiler_params=pltpu.CompilerParams(vmem_limit_bytes=8 * 2**20),
        name="combine",
    )(*parts)


def prepare_kernel(a_ref, rows_ref, ks_ref, live_ref, b_ref, cols_ref, a_out, zero_ref, one_ref, place, sems):
    copies = [pltpu.make_async_copy(a_ref, a_out.at[pl.ds(0, A_ROWS)], sems.at[2 * K_DEV])]
    for n in range(K_DEV):
        first = cols_ref[n, 0]
        copies.append(pltpu.make_async_copy(b_ref.at[n, first], zero_ref.at[n], sems.at[n]))
        copies.append(pltpu.make_async_copy(b_ref.at[n, 1 - first], one_ref.at[n], sems.at[K_DEV + n]))
    for copy in copies:
        copy.start()
    kind = lax.broadcasted_iota(jnp.int32, (POS_ROWS, BS), 0)
    lane = lax.broadcasted_iota(jnp.int32, (POS_ROWS, BS), 1)
    found = jnp.zeros((POS_ROWS, BS), jnp.int32)
    for s in range(SA):
        target = jnp.where(s < live_ref[0], rows_ref[s], RB_DEV)
        found = jnp.where((lane == s) & (kind == 0), target, found)
        found = jnp.where((lane == s) & (kind == 1), ks_ref[s], found)
    place[...] = found.astype(jnp.float32).astype(jnp.bfloat16)
    last = pltpu.make_async_copy(place, a_out.at[pl.ds(A_ROWS, POS_ROWS)], sems.at[2 * K_DEV + 1])
    last.start()
    for copy in copies:
        copy.wait()
    last.wait()


def prepare(a_vals, a_rows, a_ks, a_live, b_vals, b_cols):
    smem = pl.BlockSpec(memory_space=pltpu.SMEM)
    any_spec = pl.BlockSpec(memory_space=pl.ANY)
    return pl.pallas_call(
        prepare_kernel,
        out_shape=[
            jax.ShapeDtypeStruct((A_ROWS + POS_ROWS, BS), jnp.bfloat16),
            jax.ShapeDtypeStruct((K_DEV, BS, BS), jnp.bfloat16),
            jax.ShapeDtypeStruct((K_DEV, BS, BS), jnp.bfloat16),
        ],
        in_specs=[any_spec, smem, smem, smem, any_spec, smem],
        out_specs=[any_spec, any_spec, any_spec],
        scratch_shapes=[
            pltpu.VMEM((POS_ROWS, BS), jnp.bfloat16),
            pltpu.SemaphoreType.DMA((2 * K_DEV + 2,)),
        ],
        compiler_params=pltpu.CompilerParams(vmem_limit_bytes=60 * 2**20),
        name="prepare",
    )(
        a_vals.reshape(A_ROWS, BS),
        a_rows.reshape(SA),
        a_ks.reshape(SA),
        a_live.reshape(1),
        b_vals.reshape(K_DEV, PB, BS, BS),
        b_cols.reshape(K_DEV, PB),
    )


def shifted(value, axis, size, by):
    return lax.ppermute(value, axis, [(i, (i + by) % size) for i in range(size)])


def around(chunks, forward, backward):
    pieces = [[first] + [None] * (N_ROW - 1) for first in chunks]
    up = list(chunks)
    down = list(chunks)
    for step in range(1, max(*forward, *backward) + 1):
        for c in range(len(chunks)):
            up[c], down[c] = lax.optimization_barrier((up[c], down[c]))
            if step <= forward[c]:
                up[c] = shifted(up[c], "row", N_ROW, 1)
                pieces[c][N_ROW - step] = up[c]
            if step <= backward[c]:
                down[c] = shifted(down[c], "row", N_ROW, -1)
                pieces[c][step] = down[c]
    return pieces


def send_sums(parts):
    own, msgs = parts[0], parts[1:]
    return [own] + [shifted(msgs[q - 1], "layer", N_LAYER, q) for q in range(1, N_LAYER)]


def body(a_vals, a_rows, a_ks, a_live, b_vals, b_cols):
    a_send, b_zero, b_one = prepare(a_vals, a_rows, a_ks, a_live, b_vals, b_cols)
    pieces_zero, pieces_one = around([b_zero, b_one], (4, 3), (3, 4))
    me = jnp.stack([lax.axis_index("row"), lax.axis_index("layer")]).astype(jnp.int32)
    a_all = lax.all_gather(a_send, "col", axis=0)
    positions = a_all[:, A_ROWS : A_ROWS + 2, :SA].astype(jnp.int32)
    rows = positions[:, 0].reshape(N_COL * SA)
    ks = positions[:, 1].reshape(N_COL * SA)

    parts = send_sums(products(me, rows, ks, a_all, pieces_zero))
    parts += send_sums(products(me, rows, ks, a_all, pieces_one))
    return combine(parts).reshape(XQ, RB_DEV, CB_DEV, BS)


def solution(mesh):
    return jax.shard_map(
        body,
        mesh=mesh,
        in_specs=(
            P("layer", "row", "col", None, None, None),
            P("layer", "row", "col", None),
            P("layer", "row", "col", None),
            P("layer", "row", "col"),
            P(("layer", "row"), "col", None, None, None),
            P(("layer", "row"), "col", None),
        ),
        out_specs=P("layer", "row", "col", None),
        check_vma=False,
    )
```

```python
import functools

import jax
import jax.numpy as jnp
from jax import lax
from jax.experimental import pallas as pl
from jax.experimental.pallas import tpu as pltpu
from jax.sharding import PartitionSpec as P

BS = 128
BLK_DEV = 8
SA = 12
PB = 2
RB_DEV = 32
CB_DEV = 2
N_LAYER = 4
N_ROW = 8
N_COL = 16
K_DEV = 16
XQ = BS // N_LAYER
A_ROWS = SA * BS
POS_ROWS = 16
MSG_ROWS = RB_DEV * XQ + RB_DEV
BITS = 13.0
LN2 = 0.6931471805599453


def piece_of(me, place):
    return lax.rem(me + place, N_ROW)


def add_products(row, rows_ref, ks_ref, a_ref, pieces, acc):
    for place, b_ref in pieces:

        def half(h, carry):
            col = 2 * piece_of(row, place) + h
            base = col * SA
            for s in range(SA):
                target = rows_ref[base + s]
                k = ks_ref[base + s]
                acc[target] += jnp.dot(
                    a_ref[col, pl.ds(s * BS, BS), :],
                    b_ref[h * BLK_DEV + k],
                    preferred_element_type=jnp.float32,
                )
            return carry

        lax.fori_loop(0, 2, half, 0)


def open_kernel(places, me_ref, rows_ref, ks_ref, a_ref, *refs):
    b_refs, (out_ref, acc) = refs[: len(places)], refs[len(places) :]

    def clear(i, carry):
        acc[i] = jnp.zeros((BS, BS), jnp.float32)
        return carry

    lax.fori_loop(0, RB_DEV, clear, 0)
    add_products(me_ref[0], rows_ref, ks_ref, a_ref, list(zip(places, b_refs)), acc)

    def keep(i, carry):
        out_ref[i] = acc[i]
        return carry

    lax.fori_loop(0, RB_DEV, keep, 0)


def close_kernel(places, resumed, me_ref, rows_ref, ks_ref, a_ref, *refs):
    b_refs, refs = refs[: len(places)], refs[len(places) :]
    own_ref = refs[-2 - N_LAYER]
    msg_refs = refs[-1 - N_LAYER : -2]
    acc, top = refs[-2:]
    layer = me_ref[1]

    def load(i, carry):
        acc[i] = refs[0][i] if resumed else jnp.zeros((BS, BS), jnp.float32)
        return carry

    lax.fori_loop(0, RB_DEV, load, 0)
    add_products(me_ref[0], rows_ref, ks_ref, a_ref, list(zip(places, b_refs)), acc)

    def keep(i, carry):
        own_ref[i] = acc[i, pl.ds(layer * XQ, XQ), :]
        for q in range(1, N_LAYER):
            start = lax.rem(layer + q, N_LAYER) * XQ
            part = acc[i, pl.ds(start, XQ), :]
            top[q - 1, pl.ds(i, 1), :] = jnp.max(jnp.abs(part), axis=0, keepdims=True)
        return carry

    lax.fori_loop(0, RB_DEV, keep, 0)
    for q in range(1, N_LAYER):
        power = jnp.floor(jnp.log(jnp.maximum(top[q - 1], 1e-30)) * (1.0 / LN2))
        msg_refs[q - 1][pl.ds(RB_DEV * XQ, RB_DEV), :] = power.astype(jnp.int32).astype(jnp.int16)
        top[q - 1] = jnp.exp((BITS - power) * LN2)

    def pack(i, carry):
        for q in range(1, N_LAYER):
            start = lax.rem(layer + q, N_LAYER) * XQ
            part = acc[i, pl.ds(start, XQ), :] * top[q - 1, pl.ds(i, 1), :]
            msg_refs[q - 1][pl.ds(pl.multiple_of(i * XQ, XQ), XQ), :] = (
                jnp.round(part).astype(jnp.int32).astype(jnp.int16)
            )
        return carry

    lax.fori_loop(0, RB_DEV, pack, 0)


def products(me, rows, ks, a_all, pieces, close, before=()):
    smem = pl.BlockSpec(memory_space=pltpu.SMEM)
    vmem = pl.BlockSpec(memory_space=pltpu.VMEM)
    places, blocks = zip(*pieces)
    operands = [me, rows, ks, a_all, *blocks, *before]
    scratch = [pltpu.VMEM((RB_DEV + 1, BS, BS), jnp.float32)]
    if close:
        kernel, name = functools.partial(close_kernel, places, bool(before)), "close_sums"
        out_shape = [jax.ShapeDtypeStruct((RB_DEV, XQ, BS), jnp.float32)]
        out_shape += [jax.ShapeDtypeStruct((MSG_ROWS, BS), jnp.int16)] * (N_LAYER - 1)
        scratch.append(pltpu.VMEM((N_LAYER - 1, RB_DEV, BS), jnp.float32))
    else:
        kernel, name = functools.partial(open_kernel, places), "open_sums"
        out_shape = [jax.ShapeDtypeStruct((RB_DEV, BS, BS), jnp.float32)]
    return pl.pallas_call(
        kernel,
        out_shape=out_shape,
        in_specs=[smem] * 3 + [vmem] * (len(operands) - 3),
        out_specs=[vmem] * len(out_shape),
        scratch_shapes=scratch,
        compiler_params=pltpu.CompilerParams(vmem_limit_bytes=8 * 2**20),
        cost_estimate=pl.CostEstimate(flops=1024, bytes_accessed=1024, transcendentals=0),
        name=name,
    )(*operands)


def combine_kernel(*refs):
    out_ref, scale = refs[-2:]
    for j in range(CB_DEV):
        own_ref = refs[j * N_LAYER]
        msgs = refs[j * N_LAYER + 1 : (j + 1) * N_LAYER]
        for q in range(N_LAYER - 1):
            power = msgs[q][pl.ds(RB_DEV * XQ, RB_DEV), :].astype(jnp.int32).astype(jnp.float32)
            scale[q] = jnp.exp((power - BITS) * LN2)

        def step(i, carry):
            total = own_ref[i]
            for q in range(N_LAYER - 1):
                part = msgs[q][pl.ds(pl.multiple_of(i * XQ, XQ), XQ), :]
                total = total + part.astype(jnp.int32).astype(jnp.float32) * scale[q, pl.ds(i, 1), :]
            out_ref[pl.ds(CB_DEV * i + j, XQ, stride=RB_DEV * CB_DEV), :] = total
            return carry

        lax.fori_loop(0, RB_DEV, step, 0)


def combine(parts):
    vmem = pl.BlockSpec(memory_space=pltpu.VMEM)
    return pl.pallas_call(
        combine_kernel,
        out_shape=jax.ShapeDtypeStruct((XQ * RB_DEV * CB_DEV, BS), jnp.float32),
        in_specs=[vmem] * len(parts),
        out_specs=vmem,
        scratch_shapes=[pltpu.VMEM((N_LAYER - 1, RB_DEV, BS), jnp.float32)],
        compiler_params=pltpu.CompilerParams(vmem_limit_bytes=8 * 2**20),
        name="combine",
    )(*parts)


def prepare_kernel(
    a_ref, rows_ref, ks_ref, live_ref, b_ref, cols_ref, a_out, zero_out, one_out, a_in, zero_in, one_in, sems, out_sems
):
    copies = []
    for n in range(K_DEV):
        first = cols_ref[0, n]
        copies.append(pltpu.make_async_copy(b_ref.at[n, first], zero_in.at[n], sems.at[n]))
        copies.append(pltpu.make_async_copy(b_ref.at[n, 1 - first], one_in.at[n], sems.at[K_DEV + n]))
    copies.append(pltpu.make_async_copy(a_ref, a_in.at[pl.ds(0, A_ROWS)], sems.at[2 * K_DEV]))
    for copy in copies:
        copy.start()
    kind = lax.broadcasted_iota(jnp.int32, (POS_ROWS, BS), 0)
    lane = lax.broadcasted_iota(jnp.int32, (POS_ROWS, BS), 1)
    found = jnp.zeros((POS_ROWS, BS), jnp.int32)
    for s in range(SA):
        target = jnp.where(s < live_ref[0], rows_ref[s], RB_DEV)
        found = jnp.where((lane == s) & (kind == 0), target, found)
        found = jnp.where((lane == s) & (kind == 1), ks_ref[s], found)
    a_in[pl.ds(A_ROWS, POS_ROWS), :] = found.astype(jnp.float32).astype(jnp.bfloat16)
    for copy in copies:
        copy.wait()
    outs = [
        pltpu.make_async_copy(held, out, out_sems.at[at])
        for at, (held, out) in enumerate(((zero_in, zero_out), (one_in, one_out), (a_in, a_out)))
    ]
    for out in outs:
        out.start()
    for out in outs:
        out.wait()


def prepare(a_vals, a_rows, a_ks, a_live, b_vals, b_cols):
    smem = pl.BlockSpec(memory_space=pltpu.SMEM)
    any_spec = pl.BlockSpec(memory_space=pl.ANY)
    out_shape = [
        jax.ShapeDtypeStruct((A_ROWS + POS_ROWS, BS), jnp.bfloat16),
        jax.ShapeDtypeStruct((K_DEV, BS, BS), jnp.bfloat16),
        jax.ShapeDtypeStruct((K_DEV, BS, BS), jnp.bfloat16),
    ]
    return pl.pallas_call(
        prepare_kernel,
        out_shape=out_shape,
        in_specs=[any_spec, smem, smem, smem, any_spec, smem],
        out_specs=[any_spec] * 3,
        scratch_shapes=[pltpu.VMEM(one.shape, one.dtype) for one in out_shape]
        + [pltpu.SemaphoreType.DMA((2 * K_DEV + 1,)), pltpu.SemaphoreType.DMA((3,))],
        compiler_params=pltpu.CompilerParams(vmem_limit_bytes=60 * 2**20),
        name="prepare",
    )(
        a_vals.reshape(A_ROWS, BS),
        a_rows.reshape(SA),
        a_ks.reshape(SA),
        a_live.reshape(1),
        b_vals.reshape(K_DEV, PB, BS, BS),
        jnp.transpose(b_cols, (1, 2, 0)).reshape(PB, K_DEV),
    )


def shifted(value, axis, size, by):
    return lax.ppermute(value, axis, [(i, (i + by) % size) for i in range(size)])


def up(value):
    return shifted(value, "row", N_ROW, 1)


def down(value):
    return shifted(value, "row", N_ROW, -1)


def around(b_zero, b_one):
    zero = {0: b_zero, 7: up(b_zero), 1: down(b_zero)}
    one = {0: b_one, 7: up(b_one), 1: down(b_one)}
    zero[7], zero[1] = lax.optimization_barrier((zero[7], zero[1]))
    zero[6], zero[2] = up(zero[7]), down(zero[1])
    zero[6], zero[2], one[7], one[1] = lax.optimization_barrier((zero[6], zero[2], one[7], one[1]))
    zero[5], zero[3] = up(zero[6]), down(zero[2])
    one[6], one[2] = up(one[7]), down(one[1])
    zero[5], zero[3] = lax.optimization_barrier((zero[5], zero[3]))
    zero[4] = up(zero[5])
    one[6], one[2], zero[3] = lax.optimization_barrier((one[6], one[2], zero[3]))
    one[5], one[3] = up(one[6]), down(one[2])
    one[4] = down(one[3])
    return zero, one


def send_sums(parts):
    own, msgs = parts[0], parts[1:]
    return [own] + [shifted(msgs[q - 1], "layer", N_LAYER, q) for q in range(1, N_LAYER)]


def body(a_vals, a_rows, a_ks, a_live, b_vals, b_cols):
    a_send, b_zero, b_one = prepare(a_vals, a_rows, a_ks, a_live, b_vals, b_cols)
    zero, one = around(b_zero, b_one)
    me = jnp.stack([lax.axis_index("row"), lax.axis_index("layer")]).astype(jnp.int32)
    a_all = lax.all_gather(a_send, "col", axis=0)
    positions = a_all[:, A_ROWS : A_ROWS + 2, :SA].astype(jnp.int32)
    rows = positions[:, 0].reshape(N_COL * SA)
    ks = positions[:, 1].reshape(N_COL * SA)

    parts = send_sums(products(me, rows, ks, a_all, sorted(zero.items()), True))
    last = one.pop(4)
    before = products(me, rows, ks, a_all, sorted(one.items()), False)
    parts += send_sums(products(me, rows, ks, a_all, [(4, last)], True, before))
    return combine(parts).reshape(XQ, RB_DEV, CB_DEV, BS)


def solution(mesh):
    return jax.shard_map(
        body,
        mesh=mesh,
        in_specs=(
            P("layer", "row", "col", None, None, None),
            P("layer", "row", "col", None),
            P("layer", "row", "col", None),
            P("layer", "row", "col"),
            P(("layer", "row"), "col", None, None, None),
            P(("layer", "row"), "col", None),
        ),
        out_specs=P("layer", "row", "col", None),
        check_vma=False,
    )
```

```python
import functools

import jax
import jax.numpy as jnp
from jax import lax
from jax.experimental import pallas as pl
from jax.experimental.pallas import tpu as pltpu
from jax.sharding import PartitionSpec as P

BS = 128
BLK_DEV = 8
SA = 12
PB = 2
RB_DEV = 32
CB_DEV = 2
N_LAYER = 4
N_ROW = 8
N_COL = 16
K_DEV = 16
XQ = BS // N_LAYER
A_ROWS = SA * BS
POS_ROWS = 16
MSG_ROWS = RB_DEV * XQ + RB_DEV
BITS = 13.0
LN2 = 0.6931471805599453


def piece_of(me, place):
    return lax.rem(me + place, N_ROW)


def add_products(row, rows_ref, ks_ref, a_ref, places, chunks):
    for at, place in enumerate(places):

        def half(h, carry):
            col = 2 * piece_of(row, place) + h
            base = col * SA
            for s in range(SA):
                target = rows_ref[base + s]
                k = ks_ref[base + s]
                block = a_ref[col, pl.ds(s * BS, BS), :]
                for acc, b_refs in chunks:
                    acc[target] += jnp.dot(
                        block, b_refs[at][h * BLK_DEV + k], preferred_element_type=jnp.float32
                    )
            return carry

        lax.fori_loop(0, 2, half, 0)


def open_kernel(places, resumed, me_ref, rows_ref, ks_ref, a_ref, *refs):
    outs = refs[-CB_DEV:]
    count = len(places)
    chunks = [(outs[c], refs[c * count : (c + 1) * count]) for c in range(CB_DEV)]

    def load(i, carry):
        for c in range(CB_DEV):
            outs[c][i] = refs[CB_DEV * count + c][i] if resumed else jnp.zeros((BS, BS), jnp.float32)
        return carry

    lax.fori_loop(0, RB_DEV, load, 0)
    add_products(me_ref[0], rows_ref, ks_ref, a_ref, places, chunks)


def close_kernel(places, me_ref, rows_ref, ks_ref, a_ref, *refs):
    count = len(places)
    before_ref, own_ref = refs[count : count + 2]
    msg_refs = refs[count + 2 : -2]
    acc, top = refs[-2:]
    layer = me_ref[1]

    def load(i, carry):
        acc[i] = before_ref[i]
        return carry

    lax.fori_loop(0, RB_DEV, load, 0)
    add_products(me_ref[0], rows_ref, ks_ref, a_ref, places, [(acc, refs[:count])])

    def keep(i, carry):
        own_ref[i] = acc[i, pl.ds(layer * XQ, XQ), :]
        for q in range(1, N_LAYER):
            start = lax.rem(layer + q, N_LAYER) * XQ
            part = acc[i, pl.ds(start, XQ), :]
            top[q - 1, pl.ds(i, 1), :] = jnp.max(jnp.abs(part), axis=0, keepdims=True)
        return carry

    lax.fori_loop(0, RB_DEV, keep, 0)
    for q in range(1, N_LAYER):
        power = jnp.floor(jnp.log(jnp.maximum(top[q - 1], 1e-30)) * (1.0 / LN2))
        msg_refs[q - 1][pl.ds(RB_DEV * XQ, RB_DEV), :] = power.astype(jnp.int32).astype(jnp.int16)
        top[q - 1] = jnp.exp((BITS - power) * LN2)

    def pack(i, carry):
        for q in range(1, N_LAYER):
            start = lax.rem(layer + q, N_LAYER) * XQ
            part = acc[i, pl.ds(start, XQ), :] * top[q - 1, pl.ds(i, 1), :]
            msg_refs[q - 1][pl.ds(pl.multiple_of(i * XQ, XQ), XQ), :] = (
                jnp.round(part).astype(jnp.int32).astype(jnp.int16)
            )
        return carry

    lax.fori_loop(0, RB_DEV, pack, 0)


def call_products(kernel, name, out_shape, scratch, operands, flops):
    smem = pl.BlockSpec(memory_space=pltpu.SMEM)
    vmem = pl.BlockSpec(memory_space=pltpu.VMEM)
    return pl.pallas_call(
        kernel,
        out_shape=out_shape,
        in_specs=[smem] * 3 + [vmem] * (len(operands) - 3),
        out_specs=[vmem] * len(out_shape),
        scratch_shapes=scratch,
        compiler_params=pltpu.CompilerParams(vmem_limit_bytes=8 * 2**20),
        cost_estimate=pl.CostEstimate(flops=flops, bytes_accessed=2**20, transcendentals=0),
        name=name,
    )(*operands)


def open_sums(where, chunks, places, before=()):
    sums = jax.ShapeDtypeStruct((RB_DEV + 1, BS, BS), jnp.float32)
    blocks = [chunk[place] for chunk in chunks for place in places]
    return call_products(
        functools.partial(open_kernel, places, bool(before)),
        "open_sums",
        [sums] * CB_DEV,
        [],
        [*where, *blocks, *before],
        len(places) * 10**9,
    )


def close_sums(where, chunk, places, before):
    return call_products(
        functools.partial(close_kernel, places),
        "close_sums",
        [jax.ShapeDtypeStruct((RB_DEV, XQ, BS), jnp.float32)]
        + [jax.ShapeDtypeStruct((MSG_ROWS, BS), jnp.int16)] * (N_LAYER - 1),
        [
            pltpu.VMEM((RB_DEV + 1, BS, BS), jnp.float32),
            pltpu.VMEM((N_LAYER - 1, RB_DEV, BS), jnp.float32),
        ],
        [*where, *(chunk[place] for place in places), before],
        3 * 10**9,
    )


def combine_kernel(*refs):
    out_ref, scale = refs[-2:]
    for j in range(CB_DEV):
        own_ref = refs[j * N_LAYER]
        msgs = refs[j * N_LAYER + 1 : (j + 1) * N_LAYER]
        for q in range(N_LAYER - 1):
            power = msgs[q][pl.ds(RB_DEV * XQ, RB_DEV), :].astype(jnp.int32).astype(jnp.float32)
            scale[q] = jnp.exp((power - BITS) * LN2)

        def step(i, carry):
            total = own_ref[i]
            for q in range(N_LAYER - 1):
                part = msgs[q][pl.ds(pl.multiple_of(i * XQ, XQ), XQ), :]
                total = total + part.astype(jnp.int32).astype(jnp.float32) * scale[q, pl.ds(i, 1), :]
            out_ref[pl.ds(CB_DEV * i + j, XQ, stride=RB_DEV * CB_DEV), :] = total
            return carry

        lax.fori_loop(0, RB_DEV, step, 0)


def combine(parts):
    vmem = pl.BlockSpec(memory_space=pltpu.VMEM)
    return pl.pallas_call(
        combine_kernel,
        out_shape=jax.ShapeDtypeStruct((XQ * RB_DEV * CB_DEV, BS), jnp.float32),
        in_specs=[vmem] * len(parts),
        out_specs=vmem,
        scratch_shapes=[pltpu.VMEM((N_LAYER - 1, RB_DEV, BS), jnp.float32)],
        compiler_params=pltpu.CompilerParams(vmem_limit_bytes=8 * 2**20),
        name="combine",
    )(*parts)


def prepare_kernel(
    a_ref, rows_ref, ks_ref, live_ref, b_ref, cols_ref, a_out, zero_out, one_out, a_in, zero_in, one_in, sems, out_sems
):
    copies = []
    for n in range(K_DEV):
        first = cols_ref[0, n]
        copies.append(pltpu.make_async_copy(b_ref.at[n, first], zero_in.at[n], sems.at[n]))
        copies.append(pltpu.make_async_copy(b_ref.at[n, 1 - first], one_in.at[n], sems.at[K_DEV + n]))
    copies.append(pltpu.make_async_copy(a_ref, a_in.at[pl.ds(0, A_ROWS)], sems.at[2 * K_DEV]))
    for copy in copies:
        copy.start()
    kind = lax.broadcasted_iota(jnp.int32, (POS_ROWS, BS), 0)
    lane = lax.broadcasted_iota(jnp.int32, (POS_ROWS, BS), 1)
    found = jnp.zeros((POS_ROWS, BS), jnp.int32)
    for s in range(SA):
        target = jnp.where(s < live_ref[0, 0], rows_ref[s], RB_DEV)
        found = jnp.where((lane == s) & (kind == 0), target, found)
        found = jnp.where((lane == s) & (kind == 1), ks_ref[s], found)
    a_in[pl.ds(A_ROWS, POS_ROWS), :] = found.astype(jnp.float32).astype(jnp.bfloat16)
    for copy in copies:
        copy.wait()
    outs = [
        pltpu.make_async_copy(held, out, out_sems.at[at])
        for at, (held, out) in enumerate(((zero_in, zero_out), (one_in, one_out), (a_in, a_out)))
    ]
    for out in outs:
        out.start()
    for out in outs:
        out.wait()


def prepare(a_vals, a_rows, a_ks, a_live, b_vals, b_cols):
    smem = pl.BlockSpec(memory_space=pltpu.SMEM)
    any_spec = pl.BlockSpec(memory_space=pl.ANY)
    out_shape = [
        jax.ShapeDtypeStruct((A_ROWS + POS_ROWS, BS), jnp.bfloat16),
        jax.ShapeDtypeStruct((K_DEV, BS, BS), jnp.bfloat16),
        jax.ShapeDtypeStruct((K_DEV, BS, BS), jnp.bfloat16),
    ]
    return pl.pallas_call(
        prepare_kernel,
        out_shape=out_shape,
        in_specs=[any_spec, smem, smem, smem, any_spec, smem],
        out_specs=[any_spec] * 3,
        scratch_shapes=[pltpu.VMEM(one.shape, one.dtype) for one in out_shape]
        + [pltpu.SemaphoreType.DMA((2 * K_DEV + 1,)), pltpu.SemaphoreType.DMA((3,))],
        compiler_params=pltpu.CompilerParams(vmem_limit_bytes=60 * 2**20),
        name="prepare",
    )(
        a_vals.reshape(A_ROWS, BS),
        a_rows.reshape(SA),
        a_ks.reshape(SA),
        a_live.reshape(1, 1),
        b_vals.reshape(K_DEV, PB, BS, BS),
        jnp.transpose(b_cols, (1, 2, 0)).reshape(PB, K_DEV),
    )


def shifted(value, axis, size, by):
    return lax.ppermute(value, axis, [(i, (i + by) % size) for i in range(size)])


def up(value):
    return shifted(value, "row", N_ROW, 1)


def down(value):
    return shifted(value, "row", N_ROW, -1)


def around(b_zero, b_one, hold):
    zero, one = {0: b_zero}, {0: b_one}
    for step in range(1, N_ROW // 2 + 1):
        ahead = zero[(1 - step) % N_ROW], one[step - 1]
        if step == N_ROW // 2:
            ahead = hold(zero, one, *ahead)
        elif step > 1:
            ahead = lax.optimization_barrier(ahead)
        zero[N_ROW - step], one[step] = up(ahead[0]), down(ahead[1])
        if step == N_ROW // 2:
            break
        behind = one[(1 - step) % N_ROW], zero[step - 1]
        if step > 1:
            behind = lax.optimization_barrier(behind)
        one[N_ROW - step], zero[step] = up(behind[0]), down(behind[1])
    return zero, one


def send_sums(parts):
    own, msgs = parts[0], parts[1:]
    sent = {q: shifted(msgs[q - 1], "layer", N_LAYER, q) for q in (2, 1, 3)}
    return [own] + [sent[q] for q in range(1, N_LAYER)]


def body(a_vals, a_rows, a_ks, a_live, b_vals, b_cols):
    a_send, b_zero, b_one = prepare(a_vals, a_rows, a_ks, a_live, b_vals, b_cols)
    me = jnp.stack([lax.axis_index("row"), lax.axis_index("layer")]).astype(jnp.int32)
    a_all = lax.all_gather(a_send, "col", axis=0)
    positions = a_all[:, A_ROWS : A_ROWS + 2, :SA].astype(jnp.int32)
    rows = positions[:, 0].reshape(N_COL * SA)
    ks = positions[:, 1].reshape(N_COL * SA)
    where = (me, rows, ks, a_all)
    sums = []

    def hold(zero, one, *ahead):
        early = open_sums(where, (zero, one), (0, 7, 1))
        *ahead, first, second = lax.optimization_barrier((*ahead, *early))
        sums.extend((first, second))
        return ahead

    zero, one = around(b_zero, b_one, hold)
    sums = open_sums(where, (zero, one), (6, 2, 5, 3), sums)
    parts = send_sums(close_sums(where, zero, (4,), sums[0]))
    parts += send_sums(close_sums(where, one, (4,), sums[1]))
    return combine(parts).reshape(XQ, RB_DEV, CB_DEV, BS)


def solution(mesh):
    return jax.shard_map(
        body,
        mesh=mesh,
        in_specs=(
            P("layer", "row", "col", None, None, None),
            P("layer", "row", "col", None),
            P("layer", "row", "col", None),
            P("layer", "row", "col"),
            P(("layer", "row"), "col", None, None, None),
            P(("layer", "row"), "col", None),
        ),
        out_specs=P("layer", "row", "col", None),
        check_vma=False,
    )
```

```python
import functools

import jax
import jax.numpy as jnp
from jax import lax
from jax.experimental import pallas as pl
from jax.experimental.pallas import tpu as pltpu
from jax.sharding import PartitionSpec as P

BS = 128
BLK_DEV = 8
SA = 12
PB = 2
RB_DEV = 32
CB_DEV = 2
N_LAYER = 4
N_ROW = 8
N_COL = 16
K_DEV = 16
XQ = BS // N_LAYER
A_ROWS = SA * BS
POS_ROWS = 16
MSG_ROWS = RB_DEV * XQ + RB_DEV
BITS = 13.0
LN2 = 0.6931471805599453


def piece_of(me, place):
    return lax.rem(me + place, N_ROW)


def add_products(place_ref, a_ref, places, chunks):
    row = lax.axis_index("row")
    for at, place in enumerate(places):

        def half(h, carry):
            col = 2 * piece_of(row, place) + h
            for s in range(SA):
                target = place_ref[col, 0, s]
                k = place_ref[col, 1, s]
                block = a_ref[col, pl.ds(s * BS, BS), :]
                for acc, b_refs in chunks:
                    acc[target] += jnp.dot(
                        block, b_refs[at][h * BLK_DEV + k], preferred_element_type=jnp.float32
                    )
            return carry

        lax.fori_loop(0, 2, half, 0)


def open_kernel(places, resumed, place_ref, a_ref, *refs):
    outs = refs[-CB_DEV:]
    count = len(places)
    chunks = [(outs[c], refs[c * count : (c + 1) * count]) for c in range(CB_DEV)]

    def load(i, carry):
        for c in range(CB_DEV):
            outs[c][i] = refs[CB_DEV * count + c][i] if resumed else jnp.zeros((BS, BS), jnp.float32)
        return carry

    lax.fori_loop(0, RB_DEV, load, 0)
    add_products(place_ref, a_ref, places, chunks)


def close_kernel(places, place_ref, a_ref, *refs):
    count = len(places)
    before_ref, own_ref = refs[count : count + 2]
    msg_refs = refs[count + 2 : -2]
    acc, top = refs[-2:]
    layer = lax.axis_index("layer")

    def load(i, carry):
        acc[i] = before_ref[i]
        return carry

    lax.fori_loop(0, RB_DEV, load, 0)
    add_products(place_ref, a_ref, places, [(acc, refs[:count])])

    def keep(i, carry):
        own_ref[i] = acc[i, pl.ds(layer * XQ, XQ), :]
        for q in range(1, N_LAYER):
            start = lax.rem(layer + q, N_LAYER) * XQ
            part = acc[i, pl.ds(start, XQ), :]
            top[q - 1, pl.ds(i, 1), :] = jnp.max(jnp.abs(part), axis=0, keepdims=True)
        return carry

    lax.fori_loop(0, RB_DEV, keep, 0)
    for q in range(1, N_LAYER):
        power = jnp.floor(jnp.log(jnp.maximum(top[q - 1], 1e-30)) * (1.0 / LN2))
        msg_refs[q - 1][pl.ds(RB_DEV * XQ, RB_DEV), :] = power.astype(jnp.int32).astype(jnp.int16)
        top[q - 1] = jnp.exp((BITS - power) * LN2)

    def pack(i, carry):
        for q in range(1, N_LAYER):
            start = lax.rem(layer + q, N_LAYER) * XQ
            part = acc[i, pl.ds(start, XQ), :] * top[q - 1, pl.ds(i, 1), :]
            msg_refs[q - 1][pl.ds(pl.multiple_of(i * XQ, XQ), XQ), :] = (
                jnp.round(part).astype(jnp.int32).astype(jnp.int16)
            )
        return carry

    lax.fori_loop(0, RB_DEV, pack, 0)


def positions_kernel(a_ref, place_ref, held, place, sem):
    copy = pltpu.make_async_copy(a_ref.at[:, pl.ds(A_ROWS, POS_ROWS)], held, sem)
    copy.start()
    copy.wait()
    for col in range(N_COL):
        place[col] = held[col].astype(jnp.float32)[: POS_ROWS // 2].astype(jnp.int32)
    copy = pltpu.make_async_copy(place, place_ref, sem)
    copy.start()
    copy.wait()


def positions(a_all):
    shape = (N_COL, POS_ROWS // 2, BS)
    return pl.pallas_call(
        positions_kernel,
        out_shape=jax.ShapeDtypeStruct(shape, jnp.int32),
        in_specs=[pl.BlockSpec(memory_space=pltpu.HBM)],
        out_specs=pl.BlockSpec(memory_space=pltpu.SMEM),
        scratch_shapes=[
            pltpu.VMEM((N_COL, POS_ROWS, BS), jnp.bfloat16),
            pltpu.VMEM(shape, jnp.int32),
            pltpu.SemaphoreType.DMA(()),
        ],
        compiler_params=pltpu.CompilerParams(vmem_limit_bytes=50 * 2**20),
        name="positions",
    )(a_all)


def call_products(kernel, name, out_shape, scratch, operands, flops):
    smem = pl.BlockSpec(memory_space=pltpu.SMEM)
    vmem = pl.BlockSpec(memory_space=pltpu.VMEM)
    return pl.pallas_call(
        kernel,
        out_shape=out_shape,
        in_specs=[smem] + [vmem] * (len(operands) - 1),
        out_specs=[vmem] * len(out_shape),
        scratch_shapes=scratch,
        compiler_params=pltpu.CompilerParams(vmem_limit_bytes=6 * 2**20),
        cost_estimate=pl.CostEstimate(flops=flops, bytes_accessed=2**20, transcendentals=0),
        name=name,
    )(*operands)


def open_sums(where, chunks, places, before=()):
    sums = jax.ShapeDtypeStruct((RB_DEV + 1, BS, BS), jnp.float32)
    blocks = [chunk[place] for chunk in chunks for place in places]
    return call_products(
        functools.partial(open_kernel, places, bool(before)),
        "open_sums",
        [sums] * CB_DEV,
        [],
        [*where, *blocks, *before],
        len(places) * 10**9,
    )


def close_sums(where, chunk, places, before):
    return call_products(
        functools.partial(close_kernel, places),
        "close_sums",
        [jax.ShapeDtypeStruct((RB_DEV, XQ, BS), jnp.float32)]
        + [jax.ShapeDtypeStruct((MSG_ROWS, BS), jnp.int16)] * (N_LAYER - 1),
        [
            pltpu.VMEM((RB_DEV + 1, BS, BS), jnp.float32),
            pltpu.VMEM((N_LAYER - 1, RB_DEV, BS), jnp.float32),
        ],
        [*where, *(chunk[place] for place in places), before],
        3 * 10**9,
    )


def combine_kernel(*refs):
    out_ref, scale = refs[-2:]
    for j in range(CB_DEV):
        own_ref = refs[j * N_LAYER]
        msgs = refs[j * N_LAYER + 1 : (j + 1) * N_LAYER]
        for q in range(N_LAYER - 1):
            power = msgs[q][pl.ds(RB_DEV * XQ, RB_DEV), :].astype(jnp.int32).astype(jnp.float32)
            scale[q] = jnp.exp((power - BITS) * LN2)

        def step(i, carry):
            total = own_ref[i]
            for q in range(N_LAYER - 1):
                part = msgs[q][pl.ds(pl.multiple_of(i * XQ, XQ), XQ), :]
                total = total + part.astype(jnp.int32).astype(jnp.float32) * scale[q, pl.ds(i, 1), :]
            out_ref[pl.ds(CB_DEV * i + j, XQ, stride=RB_DEV * CB_DEV), :] = total
            return carry

        lax.fori_loop(0, RB_DEV, step, 0)


def combine(parts):
    vmem = pl.BlockSpec(memory_space=pltpu.VMEM)
    return pl.pallas_call(
        combine_kernel,
        out_shape=jax.ShapeDtypeStruct((XQ * RB_DEV * CB_DEV, BS), jnp.float32),
        in_specs=[vmem] * len(parts),
        out_specs=vmem,
        scratch_shapes=[pltpu.VMEM((N_LAYER - 1, RB_DEV, BS), jnp.float32)],
        compiler_params=pltpu.CompilerParams(vmem_limit_bytes=8 * 2**20),
        name="combine",
    )(*parts)


def prepare_kernel(
    a_ref, rows_ref, ks_ref, live_ref, b_ref, cols_ref, a_out, zero_out, one_out, a_in, zero_in, one_in, sems, out_sems
):
    copies = []
    for n in range(K_DEV):
        first = cols_ref[0, n]
        copies.append(pltpu.make_async_copy(b_ref.at[n, first], zero_in.at[n], sems.at[n]))
        copies.append(pltpu.make_async_copy(b_ref.at[n, 1 - first], one_in.at[n], sems.at[K_DEV + n]))
    copies.append(pltpu.make_async_copy(a_ref, a_in.at[pl.ds(0, A_ROWS)], sems.at[2 * K_DEV]))
    for copy in copies:
        copy.start()
    kind = lax.broadcasted_iota(jnp.int32, (POS_ROWS, BS), 0)
    lane = lax.broadcasted_iota(jnp.int32, (POS_ROWS, BS), 1)
    found = jnp.zeros((POS_ROWS, BS), jnp.int32)
    for s in range(SA):
        target = jnp.where(s < live_ref[0, 0], rows_ref[s], RB_DEV)
        found = jnp.where((lane == s) & (kind == 0), target, found)
        found = jnp.where((lane == s) & (kind == 1), ks_ref[s], found)
    a_in[pl.ds(A_ROWS, POS_ROWS), :] = found.astype(jnp.float32).astype(jnp.bfloat16)
    for copy in copies:
        copy.wait()
    outs = [
        pltpu.make_async_copy(held, out, out_sems.at[at])
        for at, (held, out) in enumerate(((zero_in, zero_out), (one_in, one_out), (a_in, a_out)))
    ]
    for out in outs:
        out.start()
    for out in outs:
        out.wait()


def prepare(a_vals, a_rows, a_ks, a_live, b_vals, b_cols):
    smem = pl.BlockSpec(memory_space=pltpu.SMEM)
    any_spec = pl.BlockSpec(memory_space=pl.ANY)
    out_shape = [
        jax.ShapeDtypeStruct((A_ROWS + POS_ROWS, BS), jnp.bfloat16),
        jax.ShapeDtypeStruct((K_DEV, BS, BS), jnp.bfloat16),
        jax.ShapeDtypeStruct((K_DEV, BS, BS), jnp.bfloat16),
    ]
    return pl.pallas_call(
        prepare_kernel,
        out_shape=out_shape,
        in_specs=[any_spec, smem, smem, smem, any_spec, smem],
        out_specs=[any_spec] * 3,
        scratch_shapes=[pltpu.VMEM(one.shape, one.dtype) for one in out_shape]
        + [pltpu.SemaphoreType.DMA((2 * K_DEV + 1,)), pltpu.SemaphoreType.DMA((3,))],
        compiler_params=pltpu.CompilerParams(vmem_limit_bytes=60 * 2**20),
        name="prepare",
    )(
        a_vals.reshape(A_ROWS, BS),
        a_rows.reshape(SA),
        a_ks.reshape(SA),
        a_live.reshape(1, 1),
        b_vals.reshape(K_DEV, PB, BS, BS),
        jnp.transpose(b_cols, (1, 2, 0)).reshape(PB, K_DEV),
    )


def shifted(value, axis, size, by):
    return lax.ppermute(value, axis, [(i, (i + by) % size) for i in range(size)])


def up(value):
    return shifted(value, "row", N_ROW, 1)


def down(value):
    return shifted(value, "row", N_ROW, -1)


def around(b_zero, b_one, hold):
    zero, one = {0: b_zero}, {0: b_one}
    for step in range(1, N_ROW // 2 + 1):
        ahead = zero[(1 - step) % N_ROW], one[step - 1]
        if step > 1:
            ahead = lax.optimization_barrier(ahead)
        zero[N_ROW - step], one[step] = up(ahead[0]), down(ahead[1])
        if step == N_ROW // 2:
            break
        behind = one[(1 - step) % N_ROW], zero[step - 1]
        if step == N_ROW // 2 - 1:
            behind = hold(*behind)
        elif step > 1:
            behind = lax.optimization_barrier(behind)
        one[N_ROW - step], zero[step] = up(behind[0]), down(behind[1])
    return zero, one


def send_sums(parts):
    own, msgs = parts[0], parts[1:]
    sent = {q: shifted(msgs[q - 1], "layer", N_LAYER, q) for q in (2, 1, 3)}
    return [own] + [sent[q] for q in range(1, N_LAYER)]


def body(a_vals, a_rows, a_ks, a_live, b_vals, b_cols):
    a_send, b_zero, b_one = prepare(a_vals, a_rows, a_ks, a_live, b_vals, b_cols)
    a_all = lax.all_gather(a_send, "col", axis=0)
    where = [positions(a_all), a_all]

    def hold(*behind):
        *behind, where[0] = lax.optimization_barrier((*behind, where[0]))
        return behind

    zero, one = around(b_zero, b_one, hold)
    sums = open_sums(where, (zero, one), (0, 7, 1, 6, 2))
    sums = open_sums(where, (zero, one), (5, 3), sums)
    parts = send_sums(close_sums(where, zero, (4,), sums[0]))
    parts += send_sums(close_sums(where, one, (4,), sums[1]))
    return combine(parts).reshape(XQ, RB_DEV, CB_DEV, BS)


def solution(mesh):
    return jax.shard_map(
        body,
        mesh=mesh,
        in_specs=(
            P("layer", "row", "col", None, None, None),
            P("layer", "row", "col", None),
            P("layer", "row", "col", None),
            P("layer", "row", "col"),
            P(("layer", "row"), "col", None, None, None),
            P(("layer", "row"), "col", None),
        ),
        out_specs=P("layer", "row", "col", None),
        check_vma=False,
    )
```

```python
import functools

import jax
import jax.numpy as jnp
from jax import lax
from jax.experimental import pallas as pl
from jax.experimental.pallas import tpu as pltpu
from jax.sharding import PartitionSpec as P

BS = 128
BLK_DEV = 8
SA = 12
PB = 2
RB_DEV = 32
CB_DEV = 2
N_LAYER = 4
N_ROW = 8
N_COL = 16
K_DEV = 16
XQ = BS // N_LAYER
A_ROWS = SA * BS
POS_ROWS = 16
MSG_ROWS = RB_DEV * XQ + RB_DEV
BITS = 13.0
LN2 = 0.6931471805599453


def piece_of(me, place):
    return lax.rem(me + place, N_ROW)


def add_products(place_ref, a_ref, places, chunks):
    row = lax.axis_index("row")
    for at, place in enumerate(places):

        def half(h, carry):
            col = 2 * piece_of(row, place) + h
            for s in range(SA):
                target = place_ref[col, s]
                k = place_ref[col, SA + s]
                block = a_ref[col, pl.ds(s * BS, BS), :]
                for acc, b_refs in chunks:
                    acc[target] += jnp.dot(
                        block, b_refs[at][h * BLK_DEV + k], preferred_element_type=jnp.float32
                    )
            return carry

        lax.fori_loop(0, 2, half, 0)


def open_kernel(places, resumed, place_ref, a_ref, *refs):
    outs = refs[-CB_DEV:]
    count = len(places)
    chunks = [(outs[c], refs[c * count : (c + 1) * count]) for c in range(CB_DEV)]

    def load(i, carry):
        for c in range(CB_DEV):
            outs[c][i] = refs[CB_DEV * count + c][i] if resumed else jnp.zeros((BS, BS), jnp.float32)
        return carry

    lax.fori_loop(0, RB_DEV, load, 0)
    add_products(place_ref, a_ref, places, chunks)


def close_kernel(places, place_ref, a_ref, *refs):
    count = len(places)
    before_ref, own_ref = refs[count : count + 2]
    msg_refs = refs[count + 2 : -2]
    acc, top = refs[-2:]
    layer = lax.axis_index("layer")

    def load(i, carry):
        acc[i] = before_ref[i]
        return carry

    lax.fori_loop(0, RB_DEV, load, 0)
    add_products(place_ref, a_ref, places, [(acc, refs[:count])])

    def keep(i, carry):
        own_ref[i] = acc[i, pl.ds(layer * XQ, XQ), :]
        for q in range(1, N_LAYER):
            start = lax.rem(layer + q, N_LAYER) * XQ
            part = acc[i, pl.ds(start, XQ), :]
            top[q - 1, pl.ds(i, 1), :] = jnp.max(jnp.abs(part), axis=0, keepdims=True)
        return carry

    lax.fori_loop(0, RB_DEV, keep, 0)
    for q in range(1, N_LAYER):
        power = jnp.floor(jnp.log(jnp.maximum(top[q - 1], 1e-30)) * (1.0 / LN2))
        msg_refs[q - 1][pl.ds(RB_DEV * XQ, RB_DEV), :] = power.astype(jnp.int32).astype(jnp.int16)
        top[q - 1] = jnp.exp((BITS - power) * LN2)

    def pack(i, carry):
        for q in range(1, N_LAYER):
            start = lax.rem(layer + q, N_LAYER) * XQ
            part = acc[i, pl.ds(start, XQ), :] * top[q - 1, pl.ds(i, 1), :]
            msg_refs[q - 1][pl.ds(pl.multiple_of(i * XQ, XQ), XQ), :] = (
                jnp.round(part).astype(jnp.int32).astype(jnp.int16)
            )
        return carry

    lax.fori_loop(0, RB_DEV, pack, 0)


def positions_kernel(a_ref, place_ref, held, place, sem):
    copy = pltpu.make_async_copy(a_ref.at[:, pl.ds(A_ROWS, POS_ROWS)], held, sem)
    copy.start()
    copy.wait()
    for col in range(N_COL):
        place[pl.ds(col, 1), :] = held[col].astype(jnp.float32)[:1].astype(jnp.int32)
    copy = pltpu.make_async_copy(place, place_ref, sem)
    copy.start()
    copy.wait()


def positions(a_all):
    shape = (N_COL, BS)
    return pl.pallas_call(
        positions_kernel,
        out_shape=jax.ShapeDtypeStruct(shape, jnp.int32),
        in_specs=[pl.BlockSpec(memory_space=pl.ANY)],
        out_specs=pl.BlockSpec(memory_space=pltpu.SMEM),
        scratch_shapes=[
            pltpu.VMEM((N_COL, POS_ROWS, BS), jnp.bfloat16),
            pltpu.VMEM(shape, jnp.int32),
            pltpu.SemaphoreType.DMA(()),
        ],
        compiler_params=pltpu.CompilerParams(vmem_limit_bytes=50 * 2**20),
        name="positions",
    )(a_all)


def call_products(kernel, name, out_shape, scratch, operands, flops):
    smem = pl.BlockSpec(memory_space=pltpu.SMEM)
    vmem = pl.BlockSpec(memory_space=pltpu.VMEM)
    return pl.pallas_call(
        kernel,
        out_shape=out_shape,
        in_specs=[smem] + [vmem] * (len(operands) - 1),
        out_specs=[vmem] * len(out_shape),
        scratch_shapes=scratch,
        compiler_params=pltpu.CompilerParams(vmem_limit_bytes=6 * 2**20),
        cost_estimate=pl.CostEstimate(flops=flops, bytes_accessed=2**20, transcendentals=0),
        name=name,
    )(*operands)


def open_sums(where, chunks, places, before=()):
    sums = jax.ShapeDtypeStruct((RB_DEV + 1, BS, BS), jnp.float32)
    blocks = [chunk[place] for chunk in chunks for place in places]
    return call_products(
        functools.partial(open_kernel, places, bool(before)),
        "open_sums",
        [sums] * CB_DEV,
        [],
        [*where, *blocks, *before],
        len(places) * 10**9,
    )


def close_sums(where, chunk, places, before):
    return call_products(
        functools.partial(close_kernel, places),
        "close_sums",
        [jax.ShapeDtypeStruct((RB_DEV, XQ, BS), jnp.float32)]
        + [jax.ShapeDtypeStruct((MSG_ROWS, BS), jnp.int16)] * (N_LAYER - 1),
        [
            pltpu.VMEM((RB_DEV + 1, BS, BS), jnp.float32),
            pltpu.VMEM((N_LAYER - 1, RB_DEV, BS), jnp.float32),
        ],
        [*where, *(chunk[place] for place in places), before],
        3 * 10**9,
    )


def add_messages(own_ref, msgs, scale, i):
    total = own_ref[i]
    for q in range(N_LAYER - 1):
        part = msgs[q][pl.ds(pl.multiple_of(i * XQ, XQ), XQ), :]
        total = total + part.astype(jnp.int32).astype(jnp.float32) * scale[q, pl.ds(i, 1), :]
    return total


def load_scales(msgs, scale):
    for q in range(N_LAYER - 1):
        power = msgs[q][pl.ds(RB_DEV * XQ, RB_DEV), :].astype(jnp.int32).astype(jnp.float32)
        scale[q] = jnp.exp((power - BITS) * LN2)


def first_combine_kernel(own_ref, *refs):
    msgs, (out_ref, scale) = refs[: N_LAYER - 1], refs[N_LAYER - 1 :]
    load_scales(msgs, scale)

    def step(i, carry):
        out_ref[i] = add_messages(own_ref, msgs, scale, i)
        return carry

    lax.fori_loop(0, RB_DEV, step, 0)


def last_combine_kernel(first_ref, own_ref, *refs):
    msgs, (out_ref, scale) = refs[: N_LAYER - 1], refs[N_LAYER - 1 :]
    load_scales(msgs, scale)

    def step(i, carry):
        out_ref[pl.ds(CB_DEV * i, XQ, stride=RB_DEV * CB_DEV), :] = first_ref[i]
        out_ref[pl.ds(CB_DEV * i + 1, XQ, stride=RB_DEV * CB_DEV), :] = add_messages(own_ref, msgs, scale, i)
        return carry

    lax.fori_loop(0, RB_DEV, step, 0)


def combine(kernel, shape, parts, name):
    vmem = pl.BlockSpec(memory_space=pltpu.VMEM)
    return pl.pallas_call(
        kernel,
        out_shape=jax.ShapeDtypeStruct(shape, jnp.float32),
        in_specs=[vmem] * len(parts),
        out_specs=vmem,
        scratch_shapes=[pltpu.VMEM((N_LAYER - 1, RB_DEV, BS), jnp.float32)],
        compiler_params=pltpu.CompilerParams(vmem_limit_bytes=6 * 2**20),
        cost_estimate=pl.CostEstimate(flops=10**9, bytes_accessed=2**20, transcendentals=0),
        name=name,
    )(*parts)


def prepare_kernel(
    a_ref, rows_ref, ks_ref, live_ref, b_ref, cols_ref, a_out, zero_out, one_out, a_in, zero_in, one_in, sems, out_sems
):
    copies = []
    for n in range(K_DEV):
        first = cols_ref[0, n]
        copies.append(pltpu.make_async_copy(b_ref.at[n, first], zero_in.at[n], sems.at[n]))
        copies.append(pltpu.make_async_copy(b_ref.at[n, 1 - first], one_in.at[n], sems.at[K_DEV + n]))
    copies.append(pltpu.make_async_copy(a_ref, a_in.at[pl.ds(0, A_ROWS)], sems.at[2 * K_DEV]))
    for copy in copies:
        copy.start()
    lane = lax.broadcasted_iota(jnp.int32, (POS_ROWS, BS), 1)
    found = jnp.zeros((POS_ROWS, BS), jnp.int32)
    for s in range(SA):
        target = jnp.where(s < live_ref[0, 0], rows_ref[s], RB_DEV)
        found = jnp.where(lane == s, target, found)
        found = jnp.where(lane == SA + s, ks_ref[s], found)
    a_in[pl.ds(A_ROWS, POS_ROWS), :] = found.astype(jnp.float32).astype(jnp.bfloat16)
    for copy in copies:
        copy.wait()
    outs = [
        pltpu.make_async_copy(held, out, out_sems.at[at])
        for at, (held, out) in enumerate(((zero_in, zero_out), (one_in, one_out), (a_in, a_out)))
    ]
    for out in outs:
        out.start()
    for out in outs:
        out.wait()


def prepare(a_vals, a_rows, a_ks, a_live, b_vals, b_cols):
    smem = pl.BlockSpec(memory_space=pltpu.SMEM)
    any_spec = pl.BlockSpec(memory_space=pl.ANY)
    out_shape = [
        jax.ShapeDtypeStruct((A_ROWS + POS_ROWS, BS), jnp.bfloat16),
        jax.ShapeDtypeStruct((K_DEV, BS, BS), jnp.bfloat16),
        jax.ShapeDtypeStruct((K_DEV, BS, BS), jnp.bfloat16),
    ]
    return pl.pallas_call(
        prepare_kernel,
        out_shape=out_shape,
        in_specs=[any_spec, smem, smem, smem, any_spec, smem],
        out_specs=[any_spec] * 3,
        scratch_shapes=[pltpu.VMEM(one.shape, one.dtype) for one in out_shape]
        + [pltpu.SemaphoreType.DMA((2 * K_DEV + 1,)), pltpu.SemaphoreType.DMA((3,))],
        compiler_params=pltpu.CompilerParams(vmem_limit_bytes=60 * 2**20),
        name="prepare",
    )(
        a_vals.reshape(A_ROWS, BS),
        a_rows.reshape(SA),
        a_ks.reshape(SA),
        a_live.reshape(1, 1),
        b_vals.reshape(K_DEV, PB, BS, BS),
        jnp.transpose(b_cols, (1, 2, 0)).reshape(PB, K_DEV),
    )


def shifted(value, axis, size, by):
    return lax.ppermute(value, axis, [(i, (i + by) % size) for i in range(size)])


def up(value):
    return shifted(value, "row", N_ROW, 1)


def down(value):
    return shifted(value, "row", N_ROW, -1)


def around(b_zero, b_one, hold, early):
    zero, one = {0: b_zero}, {0: b_one}
    zero[7], one[1] = up(zero[0]), down(one[0])
    one[7], zero[1] = up(one[0]), down(zero[0])
    zero[7], one[1] = lax.optimization_barrier((zero[7], one[1]))
    zero[6], one[2] = up(zero[7]), down(one[1])
    one[7], zero[1] = lax.optimization_barrier((one[7], zero[1]))
    one[6], zero[2] = up(one[7]), down(zero[1])
    zero[6], one[2] = lax.optimization_barrier((zero[6], one[2]))
    zero[5], one[3] = up(zero[6]), down(one[2])
    one[6], zero[2] = hold(one[6], zero[2])
    zero[3] = down(zero[2])
    zero[4] = up(zero[5])
    sums = early(zero, one)
    one[6], one[3], zero[3], *sums = lax.optimization_barrier((one[6], one[3], zero[3], *sums))
    one[5], one[4] = up(one[6]), down(one[3])
    return zero, one, sums


def send_sums(parts):
    own, msgs = parts[0], parts[1:]
    sent = {q: shifted(msgs[q - 1], "layer", N_LAYER, q) for q in (2, 1, 3)}
    return [own] + [sent[q] for q in range(1, N_LAYER)]


def body(a_vals, a_rows, a_ks, a_live, b_vals, b_cols):
    a_send, b_zero, b_one = prepare(a_vals, a_rows, a_ks, a_live, b_vals, b_cols)
    a_all = lax.all_gather(a_send, "col", axis=0)
    where = [positions(a_all), a_all]

    def hold(*behind):
        *behind, where[0] = lax.optimization_barrier((*behind, where[0]))
        return behind

    def early(zero, one):
        return open_sums(where, (zero, one), (0, 7, 1, 6, 2))

    zero, one, sums = around(b_zero, b_one, hold, early)
    parts = send_sums(close_sums(where, zero, (5, 3, 4), sums[0]))
    first = combine(first_combine_kernel, (RB_DEV, XQ, BS), parts, "first_combine")
    parts = send_sums(close_sums(where, one, (5, 3, 4), sums[1]))
    rows = XQ * RB_DEV * CB_DEV
    product = combine(last_combine_kernel, (rows, BS), [first] + parts, "last_combine")
    return product.reshape(XQ, RB_DEV, CB_DEV, BS)


def solution(mesh):
    return jax.shard_map(
        body,
        mesh=mesh,
        in_specs=(
            P("layer", "row", "col", None, None, None),
            P("layer", "row", "col", None),
            P("layer", "row", "col", None),
            P("layer", "row", "col"),
            P(("layer", "row"), "col", None, None, None),
            P(("layer", "row"), "col", None),
        ),
        out_specs=P("layer", "row", "col", None),
        check_vma=False,
    )
```

```python
import functools

import jax
import jax.numpy as jnp
from jax import lax
from jax.experimental import pallas as pl
from jax.experimental.pallas import tpu as pltpu
from jax.sharding import PartitionSpec as P

BS = 128
BLK_DEV = 8
SA = 12
PB = 2
RB_DEV = 32
CB_DEV = 2
N_LAYER = 4
N_ROW = 8
N_COL = 16
K_DEV = 16
XQ = BS // N_LAYER
A_ROWS = SA * BS
POS_ROWS = 16
MSG_ROWS = RB_DEV * XQ + RB_DEV
BITS = 13.0
LN2 = 0.6931471805599453


def piece_of(me, place):
    return lax.rem(me + place, N_ROW)


def add_products(place_ref, a_ref, places, chunks):
    row = lax.axis_index("row")
    for at, place in enumerate(places):

        def half(h, carry):
            col = 2 * piece_of(row, place) + h
            for s in range(SA):
                target = place_ref[col, s]
                k = place_ref[col, SA + s]
                block = a_ref[col, pl.ds(s * BS, BS), :]
                for acc, b_refs in chunks:
                    acc[target] += jnp.dot(
                        block, b_refs[at][h * BLK_DEV + k], preferred_element_type=jnp.float32
                    )
            return carry

        lax.fori_loop(0, 2, half, 0)


def open_kernel(places, resumed, place_ref, a_ref, *refs):
    outs = refs[-CB_DEV:]
    count = len(places)
    chunks = [(outs[c], refs[c * count : (c + 1) * count]) for c in range(CB_DEV)]

    def load(i, carry):
        for c in range(CB_DEV):
            outs[c][i] = refs[CB_DEV * count + c][i] if resumed else jnp.zeros((BS, BS), jnp.float32)
        return carry

    lax.fori_loop(0, RB_DEV, load, 0)
    add_products(place_ref, a_ref, places, chunks)


def close_kernel(places, place_ref, a_ref, *refs):
    count = len(places)
    before_ref, own_ref = refs[count : count + 2]
    msg_ref, acc, top = refs[count + 2 :]
    layer = lax.axis_index("layer")

    def load(i, carry):
        acc[i] = before_ref[i]
        return carry

    lax.fori_loop(0, RB_DEV, load, 0)
    add_products(place_ref, a_ref, places, [(acc, refs[:count])])

    def keep(i, carry):
        own_ref[i] = acc[i, pl.ds(layer * XQ, XQ), :]
        for to in range(N_LAYER):
            part = acc[i, pl.ds(to * XQ, XQ), :]
            top[to, pl.ds(i, 1), :] = jnp.max(jnp.abs(part), axis=0, keepdims=True)
        return carry

    lax.fori_loop(0, RB_DEV, keep, 0)
    for to in range(N_LAYER):
        power = jnp.floor(jnp.log(jnp.maximum(top[to], 1e-30)) * (1.0 / LN2))
        msg_ref[to, pl.ds(RB_DEV * XQ, RB_DEV), :] = power.astype(jnp.int32).astype(jnp.int16)
        top[to] = jnp.exp((BITS - power) * LN2)

    def pack(i, carry):
        for to in range(N_LAYER):
            part = acc[i, pl.ds(to * XQ, XQ), :] * top[to, pl.ds(i, 1), :]
            msg_ref[to, pl.ds(pl.multiple_of(i * XQ, XQ), XQ), :] = (
                jnp.round(part).astype(jnp.int32).astype(jnp.int16)
            )
        return carry

    lax.fori_loop(0, RB_DEV, pack, 0)


def positions_kernel(a_ref, place_ref, held, place, sem):
    copy = pltpu.make_async_copy(a_ref.at[:, pl.ds(A_ROWS, POS_ROWS)], held, sem)
    copy.start()
    copy.wait()
    for col in range(N_COL):
        place[pl.ds(col, 1), :] = held[col].astype(jnp.float32)[:1].astype(jnp.int32)
    copy = pltpu.make_async_copy(place, place_ref, sem)
    copy.start()
    copy.wait()


def positions(a_all):
    shape = (N_COL, BS)
    return pl.pallas_call(
        positions_kernel,
        out_shape=jax.ShapeDtypeStruct(shape, jnp.int32),
        in_specs=[pl.BlockSpec(memory_space=pl.ANY)],
        out_specs=pl.BlockSpec(memory_space=pltpu.SMEM),
        scratch_shapes=[
            pltpu.VMEM((N_COL, POS_ROWS, BS), jnp.bfloat16),
            pltpu.VMEM(shape, jnp.int32),
            pltpu.SemaphoreType.DMA(()),
        ],
        compiler_params=pltpu.CompilerParams(vmem_limit_bytes=50 * 2**20),
        name="positions",
    )(a_all)


def call_products(kernel, name, out_shape, scratch, operands, flops):
    smem = pl.BlockSpec(memory_space=pltpu.SMEM)
    vmem = pl.BlockSpec(memory_space=pltpu.VMEM)
    return pl.pallas_call(
        kernel,
        out_shape=out_shape,
        in_specs=[smem] + [vmem] * (len(operands) - 1),
        out_specs=[vmem] * len(out_shape),
        scratch_shapes=scratch,
        compiler_params=pltpu.CompilerParams(vmem_limit_bytes=6 * 2**20),
        cost_estimate=pl.CostEstimate(flops=flops, bytes_accessed=2**20, transcendentals=0),
        name=name,
    )(*operands)


def open_sums(where, chunks, places, before=()):
    sums = jax.ShapeDtypeStruct((RB_DEV + 1, BS, BS), jnp.float32)
    blocks = [chunk[place] for chunk in chunks for place in places]
    return call_products(
        functools.partial(open_kernel, places, bool(before)),
        "open_sums",
        [sums] * CB_DEV,
        [],
        [*where, *blocks, *before],
        len(places) * 10**9,
    )


def close_sums(where, chunk, places, before):
    return call_products(
        functools.partial(close_kernel, places),
        "close_sums",
        [jax.ShapeDtypeStruct((RB_DEV, XQ, BS), jnp.float32)]
        + [jax.ShapeDtypeStruct((N_LAYER, MSG_ROWS, BS), jnp.int16)],
        [
            pltpu.VMEM((RB_DEV + 1, BS, BS), jnp.float32),
            pltpu.VMEM((N_LAYER, RB_DEV, BS), jnp.float32),
        ],
        [*where, *(chunk[place] for place in places), before],
        3 * 10**9,
    )


def add_messages(own_ref, msg_ref, scale, i):
    total = own_ref[i]
    for q in range(1, N_LAYER):
        source = lax.rem(lax.axis_index("layer") + q, N_LAYER)
        part = msg_ref[source, pl.ds(pl.multiple_of(i * XQ, XQ), XQ), :]
        total = total + part.astype(jnp.int32).astype(jnp.float32) * scale[source, pl.ds(i, 1), :]
    return total


def load_scales(msg_ref, scale):
    for source in range(N_LAYER):
        power = msg_ref[source, pl.ds(RB_DEV * XQ, RB_DEV), :].astype(jnp.int32).astype(jnp.float32)
        scale[source] = jnp.exp((power - BITS) * LN2)


def first_combine_kernel(own_ref, msg_ref, out_ref, scale):
    load_scales(msg_ref, scale)

    def step(i, carry):
        out_ref[i] = add_messages(own_ref, msg_ref, scale, i)
        return carry

    lax.fori_loop(0, RB_DEV, step, 0)


def last_combine_kernel(first_ref, own_ref, msg_ref, out_ref, scale):
    load_scales(msg_ref, scale)

    def step(i, carry):
        out_ref[pl.ds(CB_DEV * i, XQ, stride=RB_DEV * CB_DEV), :] = first_ref[i]
        out_ref[pl.ds(CB_DEV * i + 1, XQ, stride=RB_DEV * CB_DEV), :] = add_messages(own_ref, msg_ref, scale, i)
        return carry

    lax.fori_loop(0, RB_DEV, step, 0)


def combine(kernel, shape, parts, name):
    vmem = pl.BlockSpec(memory_space=pltpu.VMEM)
    return pl.pallas_call(
        kernel,
        out_shape=jax.ShapeDtypeStruct(shape, jnp.float32),
        in_specs=[vmem] * len(parts),
        out_specs=vmem,
        scratch_shapes=[pltpu.VMEM((N_LAYER, RB_DEV, BS), jnp.float32)],
        compiler_params=pltpu.CompilerParams(vmem_limit_bytes=6 * 2**20),
        cost_estimate=pl.CostEstimate(flops=10**9, bytes_accessed=2**20, transcendentals=0),
        name=name,
    )(*parts)


def prepare_kernel(
    a_ref, rows_ref, ks_ref, live_ref, b_ref, cols_ref, a_out, zero_out, one_out, a_in, zero_in, one_in, sems, out_sems
):
    copies = []
    for n in range(K_DEV):
        first = cols_ref[0, n]
        copies.append(pltpu.make_async_copy(b_ref.at[n, first], zero_in.at[n], sems.at[n]))
        copies.append(pltpu.make_async_copy(b_ref.at[n, 1 - first], one_in.at[n], sems.at[K_DEV + n]))
    copies.append(pltpu.make_async_copy(a_ref, a_in.at[pl.ds(0, A_ROWS)], sems.at[2 * K_DEV]))
    for copy in copies:
        copy.start()
    lane = lax.broadcasted_iota(jnp.int32, (POS_ROWS, BS), 1)
    found = jnp.zeros((POS_ROWS, BS), jnp.int32)
    for s in range(SA):
        target = jnp.where(s < live_ref[0, 0, 0], rows_ref[s], RB_DEV)
        found = jnp.where(lane == s, target, found)
        found = jnp.where(lane == SA + s, ks_ref[s], found)
    a_in[pl.ds(A_ROWS, POS_ROWS), :] = found.astype(jnp.float32).astype(jnp.bfloat16)
    for copy in copies:
        copy.wait()
    outs = [
        pltpu.make_async_copy(held, out, out_sems.at[at])
        for at, (held, out) in enumerate(((zero_in, zero_out), (one_in, one_out), (a_in, a_out)))
    ]
    for out in outs:
        out.start()
    for out in outs:
        out.wait()


def prepare(a_vals, a_rows, a_ks, a_live, b_vals, b_cols):
    smem = pl.BlockSpec(memory_space=pltpu.SMEM)
    any_spec = pl.BlockSpec(memory_space=pl.ANY)
    out_shape = [
        jax.ShapeDtypeStruct((A_ROWS + POS_ROWS, BS), jnp.bfloat16),
        jax.ShapeDtypeStruct((K_DEV, BS, BS), jnp.bfloat16),
        jax.ShapeDtypeStruct((K_DEV, BS, BS), jnp.bfloat16),
    ]
    return pl.pallas_call(
        prepare_kernel,
        out_shape=out_shape,
        in_specs=[any_spec, smem, smem, smem, any_spec, smem],
        out_specs=[any_spec] * 3,
        scratch_shapes=[pltpu.VMEM(one.shape, one.dtype) for one in out_shape]
        + [pltpu.SemaphoreType.DMA((2 * K_DEV + 1,)), pltpu.SemaphoreType.DMA((3,))],
        compiler_params=pltpu.CompilerParams(vmem_limit_bytes=60 * 2**20),
        name="prepare",
    )(
        a_vals.reshape(A_ROWS, BS),
        a_rows.reshape(SA),
        a_ks.reshape(SA),
        a_live,
        b_vals.reshape(K_DEV, PB, BS, BS),
        jnp.transpose(b_cols, (1, 2, 0)).reshape(PB, K_DEV),
    )


def shifted(value, axis, size, by):
    return lax.ppermute(value, axis, [(i, (i + by) % size) for i in range(size)])


def up(value):
    return shifted(value, "row", N_ROW, 1)


def down(value):
    return shifted(value, "row", N_ROW, -1)


def around(b_zero, b_one, early):
    zero, one = {0: b_zero}, {0: b_one}
    zero[7], one[1] = up(zero[0]), down(one[0])
    one[7], zero[1] = up(one[0]), down(zero[0])
    zero[7], one[1] = lax.optimization_barrier((zero[7], one[1]))
    zero[6], one[2] = up(zero[7]), down(one[1])
    one[7], zero[1] = lax.optimization_barrier((one[7], zero[1]))
    one[6], zero[2] = up(one[7]), down(zero[1])
    zero[6], one[2] = lax.optimization_barrier((zero[6], one[2]))
    zero[5], one[3] = up(zero[6]), down(one[2])
    one[6], zero[2] = lax.optimization_barrier((one[6], zero[2]))
    zero[3] = down(zero[2])
    zero[4] = up(zero[5])
    sums = early(zero, one)
    one[6], one[3], zero[3], *sums = lax.optimization_barrier((one[6], one[3], zero[3], *sums))
    one[5], one[4] = up(one[6]), down(one[3])
    return zero, one, sums


def send_sums(parts):
    own, messages = parts
    return [own, lax.all_to_all(messages, "layer", 0, 0)]


def body(a_vals, a_rows, a_ks, a_live, b_vals, b_cols):
    a_send, b_zero, b_one = prepare(a_vals, a_rows, a_ks, a_live, b_vals, b_cols)
    a_all = lax.all_gather(a_send, "col", axis=0)
    where = [positions(a_all), a_all]
    def early(zero, one):
        return open_sums(where, (zero, one), (0, 7, 1, 6, 2))

    zero, one, sums = around(b_zero, b_one, early)
    parts = send_sums(close_sums(where, zero, (5, 3, 4), sums[0]))
    first = combine(first_combine_kernel, (RB_DEV, XQ, BS), parts, "first_combine")
    parts = send_sums(close_sums(where, one, (5, 3, 4), sums[1]))
    rows = XQ * RB_DEV * CB_DEV
    product = combine(last_combine_kernel, (rows, BS), [first] + parts, "last_combine")
    return product.reshape(XQ, RB_DEV, CB_DEV, BS)


def solution(mesh):
    return jax.shard_map(
        body,
        mesh=mesh,
        in_specs=(
            P("layer", "row", "col", None, None, None),
            P("layer", "row", "col", None),
            P("layer", "row", "col", None),
            P("layer", "row", "col"),
            P(("layer", "row"), "col", None, None, None),
            P(("layer", "row"), "col", None),
        ),
        out_specs=P("layer", "row", "col", None),
        check_vma=False,
    )
```

```python
import functools

import jax
import jax.numpy as jnp
from jax import lax
from jax.experimental import pallas as pl
from jax.experimental.pallas import tpu as pltpu
from jax.sharding import PartitionSpec as P

BS = 128
BLK_DEV = 8
SA = 12
PB = 2
RB_DEV = 32
CB_DEV = 2
N_LAYER = 4
N_ROW = 8
N_COL = 16
K_DEV = 16
XQ = BS // N_LAYER
A_ROWS = SA * BS
POS_ROWS = 16
MSG_ROWS = RB_DEV * XQ + RB_DEV
BITS = 13.0
LN2 = 0.6931471805599453


def piece_of(me, place):
    return lax.rem(me + place, N_ROW)


def add_products(place_ref, places, a_block, chunks):
    row = lax.axis_index("row")
    for at, place in enumerate(places):

        def half(h, carry):
            col = 2 * piece_of(row, place) + h
            for s in range(SA):
                target = place_ref[col, s]
                k = place_ref[col, SA + s]
                block = a_block(at, col, h, s)
                for acc, b_refs in chunks:
                    acc[target] += jnp.dot(
                        block, b_refs[at][h * BLK_DEV + k], preferred_element_type=jnp.float32
                    )
            return carry

        lax.fori_loop(0, 2, half, 0)


def open_kernel(places, width, resumed, place_ref, a_ref, *refs):
    outs = refs[-width:]
    count = len(places)
    chunks = [(outs[c], refs[c * count : (c + 1) * count]) for c in range(width)]

    def load(i, carry):
        for c in range(width):
            outs[c][i] = refs[width * count + c][i] if resumed else jnp.zeros((BS, BS), jnp.float32)
        return carry

    lax.fori_loop(0, RB_DEV, load, 0)
    add_products(place_ref, places, lambda at, col, h, s: a_ref[col, pl.ds(s * BS, BS), :], chunks)


def close_kernel(places, place_ref, a_ref, *refs):
    count = len(places)
    before_ref, msg_ref, acc, a_in, top, sems = refs[count:]
    row = lax.axis_index("row")
    copies = [
        pltpu.make_async_copy(
            a_ref.at[pl.ds(2 * piece_of(row, place), 2), pl.ds(0, A_ROWS)], a_in.at[at], sems.at[at]
        )
        for at, place in enumerate(places)
    ]
    for copy in copies:
        copy.start()

    def load(i, carry):
        acc[i] = before_ref[i]
        return carry

    lax.fori_loop(0, RB_DEV, load, 0)
    for copy in copies:
        copy.wait()
    add_products(
        place_ref, places, lambda at, col, h, s: a_in[at, h, pl.ds(s * BS, BS), :], [(acc, refs[:count])]
    )

    def keep(i, carry):
        for to in range(N_LAYER):
            part = acc[i, pl.ds(to * XQ, XQ), :]
            top[to, pl.ds(i, 1), :] = jnp.max(jnp.abs(part), axis=0, keepdims=True)
        return carry

    lax.fori_loop(0, RB_DEV, keep, 0)
    for to in range(N_LAYER):
        power = jnp.floor(jnp.log(jnp.maximum(top[to], 1e-30)) * (1.0 / LN2))
        msg_ref[to, pl.ds(RB_DEV * XQ, RB_DEV), :] = power.astype(jnp.int32).astype(jnp.int16)
        top[to] = jnp.exp((BITS - power) * LN2)

    def pack(i, carry):
        for to in range(N_LAYER):
            part = acc[i, pl.ds(to * XQ, XQ), :] * top[to, pl.ds(i, 1), :]
            msg_ref[to, pl.ds(pl.multiple_of(i * XQ, XQ), XQ), :] = (
                jnp.round(part).astype(jnp.int32).astype(jnp.int16)
            )
        return carry

    lax.fori_loop(0, RB_DEV, pack, 0)


def positions_kernel(a_ref, place_ref, held, place, sem):
    copy = pltpu.make_async_copy(a_ref.at[:, pl.ds(A_ROWS, POS_ROWS)], held, sem)
    copy.start()
    copy.wait()
    for col in range(N_COL):
        place[pl.ds(col, 1), :] = held[col].astype(jnp.float32)[:1].astype(jnp.int32)
    copy = pltpu.make_async_copy(place, place_ref, sem)
    copy.start()
    copy.wait()


def positions(a_all):
    shape = (N_COL, BS)
    return pl.pallas_call(
        positions_kernel,
        out_shape=jax.ShapeDtypeStruct(shape, jnp.int32),
        in_specs=[pl.BlockSpec(memory_space=pl.ANY)],
        out_specs=pl.BlockSpec(memory_space=pltpu.SMEM),
        scratch_shapes=[
            pltpu.VMEM((N_COL, POS_ROWS, BS), jnp.bfloat16),
            pltpu.VMEM(shape, jnp.int32),
            pltpu.SemaphoreType.DMA(()),
        ],
        compiler_params=pltpu.CompilerParams(vmem_limit_bytes=50 * 2**20),
        name="positions",
    )(a_all)


def call_products(kernel, name, out_shape, a_space, scratch, operands, flops, limit):
    smem = pl.BlockSpec(memory_space=pltpu.SMEM)
    vmem = pl.BlockSpec(memory_space=pltpu.VMEM)
    return pl.pallas_call(
        kernel,
        out_shape=out_shape,
        in_specs=[smem, pl.BlockSpec(memory_space=a_space)] + [vmem] * (len(operands) - 2),
        out_specs=[vmem] * len(out_shape),
        scratch_shapes=scratch,
        compiler_params=pltpu.CompilerParams(vmem_limit_bytes=limit * 2**20),
        cost_estimate=pl.CostEstimate(flops=flops, bytes_accessed=2**20, transcendentals=0),
        name=name,
    )(*operands)


def open_sums(where, chunks, places, before=()):
    sums = jax.ShapeDtypeStruct((RB_DEV + 1, BS, BS), jnp.float32)
    blocks = [chunk[place] for chunk in chunks for place in places]
    return call_products(
        functools.partial(open_kernel, places, len(chunks), bool(before)),
        "open_sums",
        [sums] * len(chunks),
        pltpu.VMEM,
        [],
        [*where, *blocks, *before],
        5 * 10**9,
        2,
    )


def close_sums(where, chunk, places, before, flops, limit):
    return call_products(
        functools.partial(close_kernel, places),
        "close_sums",
        [jax.ShapeDtypeStruct((N_LAYER, MSG_ROWS, BS), jnp.int16)],
        pl.ANY,
        [
            pltpu.VMEM((RB_DEV + 1, BS, BS), jnp.float32),
            pltpu.VMEM((len(places), 2, A_ROWS, BS), jnp.bfloat16),
            pltpu.VMEM((N_LAYER, RB_DEV, BS), jnp.float32),
            pltpu.SemaphoreType.DMA((len(places),)),
        ],
        [*where, *(chunk[place] for place in places), before],
        flops,
        limit,
    )[0]


def add_messages(msg_ref, scale, i):
    total = jnp.zeros((XQ, BS), jnp.float32)
    for source in range(N_LAYER):
        part = msg_ref[source, pl.ds(pl.multiple_of(i * XQ, XQ), XQ), :]
        total = total + part.astype(jnp.int32).astype(jnp.float32) * scale[source, pl.ds(i, 1), :]
    return total


def load_scales(msg_ref, scale):
    for source in range(N_LAYER):
        power = msg_ref[source, pl.ds(RB_DEV * XQ, RB_DEV), :].astype(jnp.int32).astype(jnp.float32)
        scale[source] = jnp.exp((power - BITS) * LN2)


def combine_kernel(*refs):
    msg_refs, out_ref, scales = refs[:CB_DEV], refs[CB_DEV], refs[CB_DEV + 1 :]
    for c in range(CB_DEV):
        load_scales(msg_refs[c], scales[c])

    def step(i, carry):
        for c in range(CB_DEV):
            out_ref[pl.ds(CB_DEV * i + c, XQ, stride=RB_DEV * CB_DEV), :] = add_messages(msg_refs[c], scales[c], i)
        return carry

    lax.fori_loop(0, RB_DEV, step, 0)


def combine(messages):
    vmem = pl.BlockSpec(memory_space=pltpu.VMEM)
    return pl.pallas_call(
        combine_kernel,
        out_shape=jax.ShapeDtypeStruct((XQ * RB_DEV * CB_DEV, BS), jnp.float32),
        in_specs=[vmem] * CB_DEV,
        out_specs=vmem,
        scratch_shapes=[pltpu.VMEM((N_LAYER, RB_DEV, BS), jnp.float32)] * CB_DEV,
        compiler_params=pltpu.CompilerParams(vmem_limit_bytes=8 * 2**20),
        name="combine",
    )(*messages)


def prepare_kernel(
    a_ref, rows_ref, ks_ref, live_ref, b_ref, cols_ref, a_out, zero_out, one_out, a_in, zero_in, one_in, sems, out_sems
):
    copies = []
    for n in range(K_DEV):
        first = cols_ref[0, n]
        copies.append(pltpu.make_async_copy(b_ref.at[n, first], zero_in.at[n], sems.at[n]))
        copies.append(pltpu.make_async_copy(b_ref.at[n, 1 - first], one_in.at[n], sems.at[K_DEV + n]))
    copies.append(pltpu.make_async_copy(a_ref, a_in.at[pl.ds(0, A_ROWS)], sems.at[2 * K_DEV]))
    for copy in copies:
        copy.start()
    lane = lax.broadcasted_iota(jnp.int32, (POS_ROWS, BS), 1)
    found = jnp.zeros((POS_ROWS, BS), jnp.int32)
    for s in range(SA):
        target = jnp.where(s < live_ref[0, 0, 0], rows_ref[s], RB_DEV)
        found = jnp.where(lane == s, target, found)
        found = jnp.where(lane == SA + s, ks_ref[s], found)
    a_in[pl.ds(A_ROWS, POS_ROWS), :] = found.astype(jnp.float32).astype(jnp.bfloat16)
    for copy in copies:
        copy.wait()
    outs = [
        pltpu.make_async_copy(held, out, out_sems.at[at])
        for at, (held, out) in enumerate(((zero_in, zero_out), (one_in, one_out), (a_in, a_out)))
    ]
    for out in outs:
        out.start()
    for out in outs:
        out.wait()


def prepare(a_vals, a_rows, a_ks, a_live, b_vals, b_cols):
    smem = pl.BlockSpec(memory_space=pltpu.SMEM)
    any_spec = pl.BlockSpec(memory_space=pl.ANY)
    out_shape = [
        jax.ShapeDtypeStruct((A_ROWS + POS_ROWS, BS), jnp.bfloat16),
        jax.ShapeDtypeStruct((K_DEV, BS, BS), jnp.bfloat16),
        jax.ShapeDtypeStruct((K_DEV, BS, BS), jnp.bfloat16),
    ]
    return pl.pallas_call(
        prepare_kernel,
        out_shape=out_shape,
        in_specs=[any_spec, smem, smem, smem, any_spec, smem],
        out_specs=[any_spec] * 3,
        scratch_shapes=[pltpu.VMEM(one.shape, one.dtype) for one in out_shape]
        + [pltpu.SemaphoreType.DMA((2 * K_DEV + 1,)), pltpu.SemaphoreType.DMA((3,))],
        compiler_params=pltpu.CompilerParams(vmem_limit_bytes=60 * 2**20),
        name="prepare",
    )(
        a_vals.reshape(A_ROWS, BS),
        a_rows.reshape(SA),
        a_ks.reshape(SA),
        a_live,
        b_vals.reshape(K_DEV, PB, BS, BS),
        jnp.transpose(b_cols, (1, 2, 0)).reshape(PB, K_DEV),
    )


def shifted(value, axis, size, by):
    return lax.ppermute(value, axis, [(i, (i + by) % size) for i in range(size)])


def up(value):
    return shifted(value, "row", N_ROW, 1)


def down(value):
    return shifted(value, "row", N_ROW, -1)


def around(b_zero, b_one, hold):
    zero, one = {0: b_zero}, {0: b_one}
    zero[7], one[1] = up(zero[0]), down(one[0])
    one[7], zero[1] = up(one[0]), down(zero[0])
    zero[7], one[1] = lax.optimization_barrier((zero[7], one[1]))
    zero[6], one[2] = up(zero[7]), down(one[1])
    one[7], zero[1] = lax.optimization_barrier((one[7], zero[1]))
    one[6], zero[2] = up(one[7]), down(zero[1])
    zero[6], one[2] = lax.optimization_barrier((zero[6], one[2]))
    zero[5], one[3] = up(zero[6]), down(one[2])
    one[6], zero[2] = hold(one[6], zero[2])
    zero[3] = down(zero[2])
    zero[5], one[6], one[3] = lax.optimization_barrier((zero[5], one[6], one[3]))
    zero[4] = up(zero[5])
    one[5], one[4] = up(one[6]), down(one[3])
    return zero, one


def exchange(messages):
    return lax.all_to_all(messages, "layer", 0, 0)


def body(a_vals, a_rows, a_ks, a_live, b_vals, b_cols):
    a_send, b_zero, b_one = prepare(a_vals, a_rows, a_ks, a_live, b_vals, b_cols)
    a_all = lax.all_gather(a_send, "col", axis=0)
    where = [positions(a_all), a_all]

    def hold(*moving):
        *moving, where[0] = lax.optimization_barrier((*moving, where[0]))
        return moving

    zero, one = around(b_zero, b_one, hold)
    sums = open_sums(where, (zero, one), (0, 7, 1, 6, 2))
    early = open_sums(where, (zero,), (5, 3), sums[:1])
    first = close_sums(where, zero, (4,), early[0], 2 * 10**10, 16)
    first, before = lax.optimization_barrier((first, sums[1]))
    first = exchange(first)
    last = close_sums(where, one, (5, 3, 4), before, 10**11, 52)
    first, last = lax.optimization_barrier((first, last))
    last = exchange(last)
    return combine((first, last)).reshape(XQ, RB_DEV, CB_DEV, BS)


def solution(mesh):
    return jax.shard_map(
        body,
        mesh=mesh,
        in_specs=(
            P("layer", "row", "col", None, None, None),
            P("layer", "row", "col", None),
            P("layer", "row", "col", None),
            P("layer", "row", "col"),
            P(("layer", "row"), "col", None, None, None),
            P(("layer", "row"), "col", None),
        ),
        out_specs=P("layer", "row", "col", None),
        check_vma=False,
    )
```

```python
import functools

import jax
import jax.numpy as jnp
from jax import lax
from jax.experimental import pallas as pl
from jax.experimental.pallas import tpu as pltpu
from jax.sharding import PartitionSpec as P

BS = 128
BLK_DEV = 8
SA = 12
PB = 2
RB_DEV = 32
CB_DEV = 2
N_LAYER = 4
N_ROW = 8
N_COL = 16
K_DEV = 16
XQ = BS // N_LAYER
A_ROWS = SA * BS
POS_ROWS = 16
MSG_ROWS = RB_DEV * XQ + RB_DEV
BITS = 13.0
LN2 = 0.6931471805599453


def piece_of(me, place):
    return lax.rem(me + place, N_ROW)


def add_products(place_ref, places, a_block, chunks):
    row = lax.axis_index("row")
    for at, place in enumerate(places):

        def half(h, carry):
            col = 2 * piece_of(row, place) + h
            for s in range(SA):
                target = place_ref[col, s]
                k = place_ref[col, SA + s]
                block = a_block(at, col, h, s)
                for acc, b_refs in chunks:
                    acc[target] += jnp.dot(
                        block, b_refs[at][h * BLK_DEV + k], preferred_element_type=jnp.float32
                    )
            return carry

        lax.fori_loop(0, 2, half, 0)


def open_kernel(places, width, resumed, place_ref, a_ref, *refs):
    outs = refs[-width:]
    count = len(places)
    chunks = [(outs[c], refs[c * count : (c + 1) * count]) for c in range(width)]

    def load(i, carry):
        for c in range(width):
            outs[c][i] = refs[width * count + c][i] if resumed else jnp.zeros((BS, BS), jnp.float32)
        return carry

    lax.fori_loop(0, RB_DEV, load, 0)
    add_products(place_ref, places, lambda at, col, h, s: a_ref[col, pl.ds(s * BS, BS), :], chunks)


def whole_kernel(places, place_ref, a_ref, *refs):
    count = len(places)
    before_ref, out_ref, acc = refs[count:]

    def load(i, carry):
        acc[i] = before_ref[i]
        return carry

    lax.fori_loop(0, RB_DEV, load, 0)
    add_products(
        place_ref, places, lambda at, col, h, s: a_ref[col, pl.ds(s * BS, BS), :], [(acc, refs[:count])]
    )

    def store(i, carry):
        out_ref[i] = acc[i]
        return carry

    lax.fori_loop(0, RB_DEV, store, 0)


def close_kernel(places, place_ref, a_ref, *refs):
    count = len(places)
    before_ref, msg_ref, acc, a_in, top, sems = refs[count:]
    row = lax.axis_index("row")
    copies = [
        pltpu.make_async_copy(
            a_ref.at[pl.ds(2 * piece_of(row, place), 2), pl.ds(0, A_ROWS)], a_in.at[at], sems.at[at]
        )
        for at, place in enumerate(places)
    ]
    for copy in copies:
        copy.start()

    def load(i, carry):
        acc[i] = before_ref[i]
        return carry

    lax.fori_loop(0, RB_DEV, load, 0)
    for copy in copies:
        copy.wait()
    add_products(
        place_ref, places, lambda at, col, h, s: a_in[at, h, pl.ds(s * BS, BS), :], [(acc, refs[:count])]
    )

    def keep(i, carry):
        for to in range(N_LAYER):
            part = acc[i, pl.ds(to * XQ, XQ), :]
            top[to, pl.ds(i, 1), :] = jnp.max(jnp.abs(part), axis=0, keepdims=True)
        return carry

    lax.fori_loop(0, RB_DEV, keep, 0)
    for to in range(N_LAYER):
        power = jnp.floor(jnp.log(jnp.maximum(top[to], 1e-30)) * (1.0 / LN2))
        msg_ref[to, pl.ds(RB_DEV * XQ, RB_DEV), :] = power.astype(jnp.int32).astype(jnp.int16)
        top[to] = jnp.exp((BITS - power) * LN2)

    def pack(i, carry):
        for to in range(N_LAYER):
            part = acc[i, pl.ds(to * XQ, XQ), :] * top[to, pl.ds(i, 1), :]
            msg_ref[to, pl.ds(pl.multiple_of(i * XQ, XQ), XQ), :] = (
                jnp.round(part).astype(jnp.int32).astype(jnp.int16)
            )
        return carry

    lax.fori_loop(0, RB_DEV, pack, 0)


def positions_kernel(a_ref, place_ref, held, place, sem):
    copy = pltpu.make_async_copy(a_ref.at[:, pl.ds(A_ROWS, POS_ROWS)], held, sem)
    copy.start()
    copy.wait()
    for col in range(N_COL):
        place[pl.ds(col, 1), :] = held[col].astype(jnp.float32)[:1].astype(jnp.int32)
    copy = pltpu.make_async_copy(place, place_ref, sem)
    copy.start()
    copy.wait()


def positions(a_all):
    shape = (N_COL, BS)
    return pl.pallas_call(
        positions_kernel,
        out_shape=jax.ShapeDtypeStruct(shape, jnp.int32),
        in_specs=[pl.BlockSpec(memory_space=pl.ANY)],
        out_specs=pl.BlockSpec(memory_space=pltpu.SMEM),
        scratch_shapes=[
            pltpu.VMEM((N_COL, POS_ROWS, BS), jnp.bfloat16),
            pltpu.VMEM(shape, jnp.int32),
            pltpu.SemaphoreType.DMA(()),
        ],
        compiler_params=pltpu.CompilerParams(vmem_limit_bytes=50 * 2**20),
        name="positions",
    )(a_all)


def call_products(kernel, name, out_shape, a_space, scratch, operands, flops, limit):
    smem = pl.BlockSpec(memory_space=pltpu.SMEM)
    vmem = pl.BlockSpec(memory_space=pltpu.VMEM)
    return pl.pallas_call(
        kernel,
        out_shape=out_shape,
        in_specs=[smem, pl.BlockSpec(memory_space=a_space)] + [vmem] * (len(operands) - 2),
        out_specs=[vmem] * len(out_shape),
        scratch_shapes=scratch,
        compiler_params=pltpu.CompilerParams(vmem_limit_bytes=limit * 2**20),
        cost_estimate=pl.CostEstimate(flops=flops, bytes_accessed=2**20, transcendentals=0),
        name=name,
    )(*operands)


def open_sums(where, chunks, places, before=()):
    sums = jax.ShapeDtypeStruct((RB_DEV + 1, BS, BS), jnp.float32)
    blocks = [chunk[place] for chunk in chunks for place in places]
    return call_products(
        functools.partial(open_kernel, places, len(chunks), bool(before)),
        "open_sums",
        [sums] * len(chunks),
        pltpu.VMEM,
        [],
        [*where, *blocks, *before],
        5 * 10**9,
        2,
    )


def whole_sums(where, chunk, places, before):
    return call_products(
        functools.partial(whole_kernel, places),
        "whole_sums",
        [jax.ShapeDtypeStruct((RB_DEV, BS, BS), jnp.float32)],
        pltpu.VMEM,
        [pltpu.VMEM((RB_DEV + 1, BS, BS), jnp.float32)],
        [*where, *(chunk[place] for place in places), before],
        13 * 10**10,
        6,
    )[0]


def close_sums(where, chunk, places, before):
    return call_products(
        functools.partial(close_kernel, places),
        "close_sums",
        [jax.ShapeDtypeStruct((N_LAYER, MSG_ROWS, BS), jnp.int16)],
        pl.ANY,
        [
            pltpu.VMEM((RB_DEV + 1, BS, BS), jnp.float32),
            pltpu.VMEM((len(places), 2, A_ROWS, BS), jnp.bfloat16),
            pltpu.VMEM((N_LAYER, RB_DEV, BS), jnp.float32),
            pltpu.SemaphoreType.DMA((len(places),)),
        ],
        [*where, *(chunk[place] for place in places), before],
        10**11,
        16,
    )[0]


def add_messages(msg_ref, scale, i):
    total = jnp.zeros((XQ, BS), jnp.float32)
    for source in range(N_LAYER):
        part = msg_ref[source, pl.ds(pl.multiple_of(i * XQ, XQ), XQ), :]
        total = total + part.astype(jnp.int32).astype(jnp.float32) * scale[source, pl.ds(i, 1), :]
    return total


def load_scales(msg_ref, scale):
    for source in range(N_LAYER):
        power = msg_ref[source, pl.ds(RB_DEV * XQ, RB_DEV), :].astype(jnp.int32).astype(jnp.float32)
        scale[source] = jnp.exp((power - BITS) * LN2)


def combine_kernel(first_ref, msg_ref, out_ref, scale):
    load_scales(msg_ref, scale)

    def step(i, carry):
        out_ref[pl.ds(CB_DEV * i, XQ, stride=RB_DEV * CB_DEV), :] = first_ref[i]
        out_ref[pl.ds(CB_DEV * i + 1, XQ, stride=RB_DEV * CB_DEV), :] = add_messages(msg_ref, scale, i)
        return carry

    lax.fori_loop(0, RB_DEV, step, 0)


def combine(first, messages):
    vmem = pl.BlockSpec(memory_space=pltpu.VMEM)
    return pl.pallas_call(
        combine_kernel,
        out_shape=jax.ShapeDtypeStruct((XQ * RB_DEV * CB_DEV, BS), jnp.float32),
        in_specs=[vmem] * 2,
        out_specs=vmem,
        scratch_shapes=[pltpu.VMEM((N_LAYER, RB_DEV, BS), jnp.float32)],
        compiler_params=pltpu.CompilerParams(vmem_limit_bytes=8 * 2**20),
        name="combine",
    )(first, messages)


def chunk_copies(chunk, b_ref, cols_ref, held, sems):
    copies = []
    for n in range(K_DEV):
        slot = cols_ref[0, n] if chunk == 0 else 1 - cols_ref[0, n]
        copies.append(pltpu.make_async_copy(b_ref.at[n, slot], held.at[n], sems.at[n]))
    return copies


def prepare_kernel(
    a_ref, rows_ref, ks_ref, live_ref, b_ref, cols_ref, a_out, zero_out, a_in, zero_in, sems, out_sems
):
    copies = chunk_copies(0, b_ref, cols_ref, zero_in, sems)
    copies.append(pltpu.make_async_copy(a_ref, a_in.at[pl.ds(0, A_ROWS)], sems.at[K_DEV]))
    for copy in copies:
        copy.start()
    lane = lax.broadcasted_iota(jnp.int32, (POS_ROWS, BS), 1)
    found = jnp.zeros((POS_ROWS, BS), jnp.int32)
    for s in range(SA):
        target = jnp.where(s < live_ref[0, 0, 0], rows_ref[s], RB_DEV)
        found = jnp.where(lane == s, target, found)
        found = jnp.where(lane == SA + s, ks_ref[s], found)
    a_in[pl.ds(A_ROWS, POS_ROWS), :] = found.astype(jnp.float32).astype(jnp.bfloat16)
    outs = [
        pltpu.make_async_copy(zero_in, zero_out, out_sems.at[0]),
        pltpu.make_async_copy(a_in, a_out, out_sems.at[1]),
    ]
    for copy in copies[:-1]:
        copy.wait()
    outs[0].start()
    copies[-1].wait()
    outs[1].start()
    for out in outs:
        out.wait()


def prepare_last_kernel(b_ref, cols_ref, one_out, one_in, sems, out_sem):
    copies = chunk_copies(1, b_ref, cols_ref, one_in, sems)
    for copy in copies:
        copy.start()
    for copy in copies:
        copy.wait()
    out = pltpu.make_async_copy(one_in, one_out, out_sem)
    out.start()
    out.wait()


def prepare(a_vals, a_rows, a_ks, a_live, b_vals, b_cols):
    smem = pl.BlockSpec(memory_space=pltpu.SMEM)
    any_spec = pl.BlockSpec(memory_space=pl.ANY)
    params = pltpu.CompilerParams(vmem_limit_bytes=60 * 2**20)
    a_send = jax.ShapeDtypeStruct((A_ROWS + POS_ROWS, BS), jnp.bfloat16)
    chunk = jax.ShapeDtypeStruct((K_DEV, BS, BS), jnp.bfloat16)
    b_vals = b_vals.reshape(K_DEV, PB, BS, BS)
    b_cols = jnp.transpose(b_cols, (1, 2, 0)).reshape(PB, K_DEV)
    a_all, b_zero = pl.pallas_call(
        prepare_kernel,
        out_shape=[a_send, chunk],
        in_specs=[any_spec, smem, smem, smem, any_spec, smem],
        out_specs=[any_spec] * 2,
        scratch_shapes=[pltpu.VMEM(one.shape, one.dtype) for one in (a_send, chunk)]
        + [pltpu.SemaphoreType.DMA((K_DEV + 1,)), pltpu.SemaphoreType.DMA((2,))],
        compiler_params=params,
        name="prepare",
    )(a_vals.reshape(A_ROWS, BS), a_rows.reshape(SA), a_ks.reshape(SA), a_live, b_vals, b_cols)
    b_vals, b_zero = lax.optimization_barrier((b_vals, b_zero))
    b_one = pl.pallas_call(
        prepare_last_kernel,
        out_shape=chunk,
        in_specs=[any_spec, smem],
        out_specs=any_spec,
        scratch_shapes=[
            pltpu.VMEM(chunk.shape, chunk.dtype),
            pltpu.SemaphoreType.DMA((K_DEV,)),
            pltpu.SemaphoreType.DMA(()),
        ],
        compiler_params=params,
        name="prepare_last",
    )(b_vals, b_cols)
    return a_all, b_zero, b_one


def shifted(value, axis, size, by):
    return lax.ppermute(value, axis, [(i, (i + by) % size) for i in range(size)])


def up(value):
    return shifted(value, "row", N_ROW, 1)


def down(value):
    return shifted(value, "row", N_ROW, -1)


def around(b_zero, b_one, hold):
    zero, one = {0: b_zero}, {0: b_one}
    zero[7], one[1] = up(zero[0]), down(one[0])
    one[7], zero[1] = up(one[0]), down(zero[0])
    zero[6], one[2] = up(zero[7]), down(one[1])
    one[7], zero[1] = lax.optimization_barrier((one[7], zero[1]))
    one[6], zero[2] = up(one[7]), down(zero[1])
    zero[6], one[2] = lax.optimization_barrier((zero[6], one[2]))
    zero[5], one[3] = up(zero[6]), down(one[2])
    one[6], zero[2] = hold(one[6], zero[2])
    zero[3] = down(zero[2])
    zero[5], one[6], one[3] = lax.optimization_barrier((zero[5], one[6], one[3]))
    zero[4] = up(zero[5])
    one[5], one[4] = up(one[6]), down(one[3])
    return zero, one


def exchange(messages):
    return lax.all_to_all(messages, "layer", 0, 0)


def body(a_vals, a_rows, a_ks, a_live, b_vals, b_cols):
    a_send, b_zero, b_one = prepare(a_vals, a_rows, a_ks, a_live, b_vals, b_cols)
    a_all = lax.all_gather(a_send, "col", axis=0)
    where = [positions(a_all), a_all]

    def hold(*moving):
        *moving, where[0] = lax.optimization_barrier((*moving, where[0]))
        return moving

    zero, one = around(b_zero, b_one, hold)
    sums = open_sums(where, (zero, one), (0, 7, 1, 6, 2))
    early = open_sums(where, (zero,), (5, 3), sums[:1])
    first = whole_sums(where, zero, (4,), early[0])
    first, before = lax.optimization_barrier((first, sums[1]))
    first = lax.psum_scatter(first, "layer", scatter_dimension=1, tiled=True)
    last = exchange(close_sums(where, one, (5, 3, 4), before))
    return combine(first, last).reshape(XQ, RB_DEV, CB_DEV, BS)


def solution(mesh):
    return jax.shard_map(
        body,
        mesh=mesh,
        in_specs=(
            P("layer", "row", "col", None, None, None),
            P("layer", "row", "col", None),
            P("layer", "row", "col", None),
            P("layer", "row", "col"),
            P(("layer", "row"), "col", None, None, None),
            P(("layer", "row"), "col", None),
        ),
        out_specs=P("layer", "row", "col", None),
        check_vma=False,
    )
```

```python
import functools

import jax
import jax.numpy as jnp
from jax import lax
from jax.experimental import pallas as pl
from jax.experimental.pallas import tpu as pltpu
from jax.sharding import PartitionSpec as P

BS = 128
BLK_DEV = 8
SA = 12
PB = 2
RB_DEV = 32
CB_DEV = 2
N_LAYER = 4
N_ROW = 8
N_COL = 16
K_DEV = 16
XQ = BS // N_LAYER
A_ROWS = SA * BS
POS_ROWS = 16
MSG_ROWS = RB_DEV * XQ + RB_DEV
BITS = 13.0
LN2 = 0.6931471805599453


def piece_of(me, place):
    return lax.rem(me + place, N_ROW)


def add_products(place_ref, a_ref, places, chunks):
    row = lax.axis_index("row")
    for at, place in enumerate(places):

        def half(h, carry):
            col = 2 * piece_of(row, place) + h
            for s in range(SA):
                target = place_ref[col, s]
                k = place_ref[col, SA + s]
                block = a_ref[col, pl.ds(s * BS, BS), :]
                for acc, b_refs in chunks:
                    acc[target] += jnp.dot(
                        block, b_refs[at][h * BLK_DEV + k], preferred_element_type=jnp.float32
                    )
            return carry

        lax.fori_loop(0, 2, half, 0)


def open_kernel(places, width, resumed, place_ref, a_ref, *refs):
    outs = refs[-width:]
    count = len(places)
    chunks = [(outs[c], refs[c * count : (c + 1) * count]) for c in range(width)]

    def load(i, carry):
        for c in range(width):
            outs[c][i] = refs[width * count + c][i] if resumed else jnp.zeros((BS, BS), jnp.float32)
        return carry

    lax.fori_loop(0, RB_DEV, load, 0)
    add_products(place_ref, a_ref, places, chunks)


def close_kernel(places, place_ref, a_ref, *refs):
    count = len(places)
    before_ref, own_ref = refs[count : count + 2]
    msg_refs = refs[count + 2 : -2]
    acc, top = refs[-2:]
    layer = lax.axis_index("layer")

    def load(i, carry):
        acc[i] = before_ref[i]
        return carry

    lax.fori_loop(0, RB_DEV, load, 0)
    add_products(place_ref, a_ref, places, [(acc, refs[:count])])

    def keep(i, carry):
        own_ref[i] = acc[i, pl.ds(layer * XQ, XQ), :]
        for q in range(1, N_LAYER):
            start = lax.rem(layer + q, N_LAYER) * XQ
            part = acc[i, pl.ds(start, XQ), :]
            top[q - 1, pl.ds(i, 1), :] = jnp.max(jnp.abs(part), axis=0, keepdims=True)
        return carry

    lax.fori_loop(0, RB_DEV, keep, 0)
    for q in range(1, N_LAYER):
        power = jnp.floor(jnp.log(jnp.maximum(top[q - 1], 1e-30)) * (1.0 / LN2))
        msg_refs[q - 1][pl.ds(RB_DEV * XQ, RB_DEV), :] = power.astype(jnp.int32).astype(jnp.int16)
        top[q - 1] = jnp.exp((BITS - power) * LN2)

    def pack(i, carry):
        for q in range(1, N_LAYER):
            start = lax.rem(layer + q, N_LAYER) * XQ
            part = acc[i, pl.ds(start, XQ), :] * top[q - 1, pl.ds(i, 1), :]
            msg_refs[q - 1][pl.ds(pl.multiple_of(i * XQ, XQ), XQ), :] = (
                jnp.round(part).astype(jnp.int32).astype(jnp.int16)
            )
        return carry

    lax.fori_loop(0, RB_DEV, pack, 0)


def positions_kernel(a_ref, place_ref, held, place, sem):
    copy = pltpu.make_async_copy(a_ref.at[:, pl.ds(A_ROWS, POS_ROWS)], held, sem)
    copy.start()
    copy.wait()
    for col in range(N_COL):
        place[pl.ds(col, 1), :] = held[col].astype(jnp.float32)[:1].astype(jnp.int32)
    copy = pltpu.make_async_copy(place, place_ref, sem)
    copy.start()
    copy.wait()


def positions(a_all):
    shape = (N_COL, BS)
    return pl.pallas_call(
        positions_kernel,
        out_shape=jax.ShapeDtypeStruct(shape, jnp.int32),
        in_specs=[pl.BlockSpec(memory_space=pl.ANY)],
        out_specs=pl.BlockSpec(memory_space=pltpu.SMEM),
        scratch_shapes=[
            pltpu.VMEM((N_COL, POS_ROWS, BS), jnp.bfloat16),
            pltpu.VMEM(shape, jnp.int32),
            pltpu.SemaphoreType.DMA(()),
        ],
        compiler_params=pltpu.CompilerParams(vmem_limit_bytes=50 * 2**20),
        name="positions",
    )(a_all)


def call_products(kernel, name, out_shape, scratch, operands, flops):
    smem = pl.BlockSpec(memory_space=pltpu.SMEM)
    vmem = pl.BlockSpec(memory_space=pltpu.VMEM)
    return pl.pallas_call(
        kernel,
        out_shape=out_shape,
        in_specs=[smem] + [vmem] * (len(operands) - 1),
        out_specs=[vmem] * len(out_shape),
        scratch_shapes=scratch,
        compiler_params=pltpu.CompilerParams(vmem_limit_bytes=6 * 2**20),
        cost_estimate=pl.CostEstimate(flops=flops, bytes_accessed=2**20, transcendentals=0),
        name=name,
    )(*operands)


def open_sums(where, chunks, places, before=()):
    sums = jax.ShapeDtypeStruct((RB_DEV + 1, BS, BS), jnp.float32)
    blocks = [chunk[place] for chunk in chunks for place in places]
    return call_products(
        functools.partial(open_kernel, places, len(chunks), bool(before)),
        "open_sums",
        [sums] * len(chunks),
        [],
        [*where, *blocks, *before],
        5 * 10**9,
    )


def close_sums(where, chunk, places, before, flops):
    return call_products(
        functools.partial(close_kernel, places),
        "close_sums",
        [jax.ShapeDtypeStruct((RB_DEV, XQ, BS), jnp.float32)]
        + [jax.ShapeDtypeStruct((MSG_ROWS, BS), jnp.int16)] * (N_LAYER - 1),
        [
            pltpu.VMEM((RB_DEV + 1, BS, BS), jnp.float32),
            pltpu.VMEM((N_LAYER - 1, RB_DEV, BS), jnp.float32),
        ],
        [*where, *(chunk[place] for place in places), before],
        flops,
    )


def add_messages(own_ref, msgs, scale, i):
    total = own_ref[i]
    for q in range(N_LAYER - 1):
        part = msgs[q][pl.ds(pl.multiple_of(i * XQ, XQ), XQ), :]
        total = total + part.astype(jnp.int32).astype(jnp.float32) * scale[q, pl.ds(i, 1), :]
    return total


def load_scales(msgs, scale):
    for q in range(N_LAYER - 1):
        power = msgs[q][pl.ds(RB_DEV * XQ, RB_DEV), :].astype(jnp.int32).astype(jnp.float32)
        scale[q] = jnp.exp((power - BITS) * LN2)


def first_combine_kernel(own_ref, *refs):
    msgs, (out_ref, scale) = refs[: N_LAYER - 1], refs[N_LAYER - 1 :]
    load_scales(msgs, scale)

    def step(i, carry):
        out_ref[i] = add_messages(own_ref, msgs, scale, i)
        return carry

    lax.fori_loop(0, RB_DEV, step, 0)


def last_combine_kernel(first_ref, own_ref, *refs):
    msgs, (out_ref, scale) = refs[: N_LAYER - 1], refs[N_LAYER - 1 :]
    load_scales(msgs, scale)

    def step(i, carry):
        out_ref[pl.ds(CB_DEV * i, XQ, stride=RB_DEV * CB_DEV), :] = first_ref[i]
        out_ref[pl.ds(CB_DEV * i + 1, XQ, stride=RB_DEV * CB_DEV), :] = add_messages(own_ref, msgs, scale, i)
        return carry

    lax.fori_loop(0, RB_DEV, step, 0)


def combine(kernel, shape, parts, name):
    vmem = pl.BlockSpec(memory_space=pltpu.VMEM)
    return pl.pallas_call(
        kernel,
        out_shape=jax.ShapeDtypeStruct(shape, jnp.float32),
        in_specs=[vmem] * len(parts),
        out_specs=vmem,
        scratch_shapes=[pltpu.VMEM((N_LAYER - 1, RB_DEV, BS), jnp.float32)],
        compiler_params=pltpu.CompilerParams(vmem_limit_bytes=6 * 2**20),
        cost_estimate=pl.CostEstimate(flops=10**9, bytes_accessed=2**20, transcendentals=0),
        name=name,
    )(*parts)


def prepare_kernel(
    a_ref, rows_ref, ks_ref, live_ref, b_ref, cols_ref, a_out, zero_out, one_out, a_in, zero_in, one_in, sems, out_sems
):
    copies = []
    for n in range(K_DEV):
        first = cols_ref[0, n]
        copies.append(pltpu.make_async_copy(b_ref.at[n, first], zero_in.at[n], sems.at[n]))
        copies.append(pltpu.make_async_copy(b_ref.at[n, 1 - first], one_in.at[n], sems.at[K_DEV + n]))
    copies.append(pltpu.make_async_copy(a_ref, a_in.at[pl.ds(0, A_ROWS)], sems.at[2 * K_DEV]))
    for copy in copies:
        copy.start()
    lane = lax.broadcasted_iota(jnp.int32, (POS_ROWS, BS), 1)
    found = jnp.zeros((POS_ROWS, BS), jnp.int32)
    for s in range(SA):
        target = jnp.where(s < live_ref[0, 0, 0], rows_ref[s], RB_DEV)
        found = jnp.where(lane == s, target, found)
        found = jnp.where(lane == SA + s, ks_ref[s], found)
    a_in[pl.ds(A_ROWS, POS_ROWS), :] = found.astype(jnp.float32).astype(jnp.bfloat16)
    for copy in copies:
        copy.wait()
    outs = [
        pltpu.make_async_copy(held, out, out_sems.at[at])
        for at, (held, out) in enumerate(((zero_in, zero_out), (one_in, one_out), (a_in, a_out)))
    ]
    for out in outs:
        out.start()
    for out in outs:
        out.wait()


def prepare(a_vals, a_rows, a_ks, a_live, b_vals, b_cols):
    smem = pl.BlockSpec(memory_space=pltpu.SMEM)
    any_spec = pl.BlockSpec(memory_space=pl.ANY)
    out_shape = [
        jax.ShapeDtypeStruct((A_ROWS + POS_ROWS, BS), jnp.bfloat16),
        jax.ShapeDtypeStruct((K_DEV, BS, BS), jnp.bfloat16),
        jax.ShapeDtypeStruct((K_DEV, BS, BS), jnp.bfloat16),
    ]
    return pl.pallas_call(
        prepare_kernel,
        out_shape=out_shape,
        in_specs=[any_spec, smem, smem, smem, any_spec, smem],
        out_specs=[any_spec] * 3,
        scratch_shapes=[pltpu.VMEM(one.shape, one.dtype) for one in out_shape]
        + [pltpu.SemaphoreType.DMA((2 * K_DEV + 1,)), pltpu.SemaphoreType.DMA((3,))],
        compiler_params=pltpu.CompilerParams(vmem_limit_bytes=60 * 2**20),
        name="prepare",
    )(
        a_vals.reshape(A_ROWS, BS),
        a_rows.reshape(SA),
        a_ks.reshape(SA),
        a_live,
        b_vals.reshape(K_DEV, PB, BS, BS),
        jnp.transpose(b_cols, (1, 2, 0)).reshape(PB, K_DEV),
    )


def shifted(value, axis, size, by):
    return lax.ppermute(value, axis, [(i, (i + by) % size) for i in range(size)])


def up(value):
    return shifted(value, "row", N_ROW, 1)


def down(value):
    return shifted(value, "row", N_ROW, -1)


def around(b_zero, b_one, hold):
    zero, one = {0: b_zero}, {0: b_one}
    zero[7], one[1] = up(zero[0]), down(one[0])
    one[7], zero[1] = up(one[0]), down(zero[0])
    zero[7], one[1] = lax.optimization_barrier((zero[7], one[1]))
    zero[6], one[2] = up(zero[7]), down(one[1])
    zero[1], one[7] = lax.optimization_barrier((zero[1], one[7]))
    one[6], zero[2] = up(one[7]), down(zero[1])
    zero[6], one[2] = lax.optimization_barrier((zero[6], one[2]))
    zero[5], one[3] = up(zero[6]), down(one[2])
    one[6], zero[2] = hold(one[6], zero[2])
    zero[3] = down(zero[2])
    zero[5], one[6], one[3] = lax.optimization_barrier((zero[5], one[6], one[3]))
    zero[4] = up(zero[5])
    one[5], one[4] = up(one[6]), down(one[3])
    return zero, one


def send_sums(parts):
    own, msgs = parts[0], parts[1:]
    sent = {q: shifted(msgs[q - 1], "layer", N_LAYER, q) for q in (2, 1, 3)}
    return [own] + [sent[q] for q in range(1, N_LAYER)]


def body(a_vals, a_rows, a_ks, a_live, b_vals, b_cols):
    a_send, b_zero, b_one = prepare(a_vals, a_rows, a_ks, a_live, b_vals, b_cols)
    a_all = lax.all_gather(a_send, "col", axis=0)
    where = [positions(a_all), a_all]

    def hold(*behind):
        *behind, where[0] = lax.optimization_barrier((*behind, where[0]))
        return behind

    zero, one = around(b_zero, b_one, hold)
    sums = open_sums(where, (zero, one), (0, 7, 1, 6, 2))
    early = open_sums(where, (zero,), (5, 3), sums[:1])
    parts = send_sums(close_sums(where, zero, (4,), early[0], 2 * 10**10))
    first = combine(first_combine_kernel, (RB_DEV, XQ, BS), parts, "first_combine")
    parts = send_sums(close_sums(where, one, (5, 3, 4), sums[1], 10**11))
    rows = XQ * RB_DEV * CB_DEV
    product = combine(last_combine_kernel, (rows, BS), [first] + parts, "last_combine")
    return product.reshape(XQ, RB_DEV, CB_DEV, BS)


def solution(mesh):
    return jax.shard_map(
        body,
        mesh=mesh,
        in_specs=(
            P("layer", "row", "col", None, None, None),
            P("layer", "row", "col", None),
            P("layer", "row", "col", None),
            P("layer", "row", "col"),
            P(("layer", "row"), "col", None, None, None),
            P(("layer", "row"), "col", None),
        ),
        out_specs=P("layer", "row", "col", None),
        check_vma=False,
    )
```

```python
import functools

import jax
import jax.numpy as jnp
from jax import lax
from jax.experimental import pallas as pl
from jax.experimental.pallas import tpu as pltpu
from jax.sharding import PartitionSpec as P

BS = 128
BLK_DEV = 8
SA = 12
PB = 2
RB_DEV = 32
CB_DEV = 2
N_LAYER = 4
N_ROW = 8
N_COL = 16
K_DEV = 16
XQ = BS // N_LAYER
A_ROWS = SA * BS
POS_ROWS = 16
MSG_ROWS = RB_DEV * XQ + RB_DEV
BITS = 13.0
LN2 = 0.6931471805599453


def piece_of(me, place):
    return lax.rem(me + place, N_ROW)


def add_products(place_ref, a_ref, places, chunks):
    row = lax.axis_index("row")
    for at, place in enumerate(places):

        def half(h, carry):
            col = 2 * piece_of(row, place) + h
            for s in range(SA):
                target = place_ref[col, s]
                k = place_ref[col, SA + s]
                block = a_ref[col, pl.ds(s * BS, BS), :]
                for acc, b_refs in chunks:
                    acc[target] += jnp.dot(
                        block, b_refs[at][h * BLK_DEV + k], preferred_element_type=jnp.float32
                    )
            return carry

        lax.fori_loop(0, 2, half, 0)


def open_kernel(places, width, resumed, place_ref, a_ref, *refs):
    outs = refs[-width:]
    count = len(places)
    chunks = [(outs[c], refs[c * count : (c + 1) * count]) for c in range(width)]

    def load(i, carry):
        for c in range(width):
            outs[c][i] = refs[width * count + c][i] if resumed else jnp.zeros((BS, BS), jnp.float32)
        return carry

    lax.fori_loop(0, RB_DEV, load, 0)
    add_products(place_ref, a_ref, places, chunks)


def close_kernel(places, place_ref, a_ref, *refs):
    count = len(places)
    before_ref, own_ref = refs[count : count + 2]
    msg_refs = refs[count + 2 : -2]
    acc, top = refs[-2:]
    layer = lax.axis_index("layer")

    def load(i, carry):
        acc[i] = before_ref[i]
        return carry

    lax.fori_loop(0, RB_DEV, load, 0)
    add_products(place_ref, a_ref, places, [(acc, refs[:count])])

    def keep(i, carry):
        own_ref[i] = acc[i, pl.ds(layer * XQ, XQ), :]
        for q in range(1, N_LAYER):
            start = lax.rem(layer + q, N_LAYER) * XQ
            part = acc[i, pl.ds(start, XQ), :]
            top[q - 1, pl.ds(i, 1), :] = jnp.max(jnp.abs(part), axis=0, keepdims=True)
        return carry

    lax.fori_loop(0, RB_DEV, keep, 0)
    for q in range(1, N_LAYER):
        power = jnp.floor(jnp.log(jnp.maximum(top[q - 1], 1e-30)) * (1.0 / LN2))
        msg_refs[q - 1][pl.ds(RB_DEV * XQ, RB_DEV), :] = power.astype(jnp.int32).astype(jnp.int16)
        top[q - 1] = jnp.exp((BITS - power) * LN2)

    def pack(i, carry):
        for q in range(1, N_LAYER):
            start = lax.rem(layer + q, N_LAYER) * XQ
            part = acc[i, pl.ds(start, XQ), :] * top[q - 1, pl.ds(i, 1), :]
            msg_refs[q - 1][pl.ds(pl.multiple_of(i * XQ, XQ), XQ), :] = (
                jnp.round(part).astype(jnp.int32).astype(jnp.int16)
            )
        return carry

    lax.fori_loop(0, RB_DEV, pack, 0)


def positions_kernel(a_ref, place_ref, held, place, sem):
    copy = pltpu.make_async_copy(a_ref.at[:, pl.ds(A_ROWS, POS_ROWS)], held, sem)
    copy.start()
    copy.wait()
    for col in range(N_COL):
        place[pl.ds(col, 1), :] = held[col].astype(jnp.float32)[:1].astype(jnp.int32)
    copy = pltpu.make_async_copy(place, place_ref, sem)
    copy.start()
    copy.wait()


def positions(a_all):
    shape = (N_COL, BS)
    return pl.pallas_call(
        positions_kernel,
        out_shape=jax.ShapeDtypeStruct(shape, jnp.int32),
        in_specs=[pl.BlockSpec(memory_space=pl.ANY)],
        out_specs=pl.BlockSpec(memory_space=pltpu.SMEM),
        scratch_shapes=[
            pltpu.VMEM((N_COL, POS_ROWS, BS), jnp.bfloat16),
            pltpu.VMEM(shape, jnp.int32),
            pltpu.SemaphoreType.DMA(()),
        ],
        compiler_params=pltpu.CompilerParams(vmem_limit_bytes=50 * 2**20),
        name="positions",
    )(a_all)


def call_products(kernel, name, out_shape, scratch, operands, flops):
    smem = pl.BlockSpec(memory_space=pltpu.SMEM)
    vmem = pl.BlockSpec(memory_space=pltpu.VMEM)
    return pl.pallas_call(
        kernel,
        out_shape=out_shape,
        in_specs=[smem] + [vmem] * (len(operands) - 1),
        out_specs=[vmem] * len(out_shape),
        scratch_shapes=scratch,
        compiler_params=pltpu.CompilerParams(vmem_limit_bytes=6 * 2**20),
        cost_estimate=pl.CostEstimate(flops=flops, bytes_accessed=2**20, transcendentals=0),
        name=name,
    )(*operands)


def open_sums(where, chunks, places, before=()):
    sums = jax.ShapeDtypeStruct((RB_DEV + 1, BS, BS), jnp.float32)
    blocks = [chunk[place] for chunk in chunks for place in places]
    return call_products(
        functools.partial(open_kernel, places, len(chunks), bool(before)),
        "open_sums",
        [sums] * len(chunks),
        [],
        [*where, *blocks, *before],
        5 * 10**9,
    )


def close_sums(where, chunk, places, before, flops):
    return call_products(
        functools.partial(close_kernel, places),
        "close_sums",
        [jax.ShapeDtypeStruct((RB_DEV, XQ, BS), jnp.float32)]
        + [jax.ShapeDtypeStruct((MSG_ROWS, BS), jnp.int16)] * (N_LAYER - 1),
        [
            pltpu.VMEM((RB_DEV + 1, BS, BS), jnp.float32),
            pltpu.VMEM((N_LAYER - 1, RB_DEV, BS), jnp.float32),
        ],
        [*where, *(chunk[place] for place in places), before],
        flops,
    )


def add_messages(own_ref, msgs, scale, i):
    total = own_ref[i]
    for q in range(N_LAYER - 1):
        part = msgs[q][pl.ds(pl.multiple_of(i * XQ, XQ), XQ), :]
        total = total + part.astype(jnp.int32).astype(jnp.float32) * scale[q, pl.ds(i, 1), :]
    return total


def load_scales(msgs, scale):
    for q in range(N_LAYER - 1):
        power = msgs[q][pl.ds(RB_DEV * XQ, RB_DEV), :].astype(jnp.int32).astype(jnp.float32)
        scale[q] = jnp.exp((power - BITS) * LN2)


def first_combine_kernel(own_ref, *refs):
    msgs, (out_ref, scale) = refs[: N_LAYER - 1], refs[N_LAYER - 1 :]
    load_scales(msgs, scale)

    def step(i, carry):
        out_ref[i] = add_messages(own_ref, msgs, scale, i)
        return carry

    lax.fori_loop(0, RB_DEV, step, 0)


def last_combine_kernel(first_ref, own_ref, *refs):
    msgs, (out_ref, scale) = refs[: N_LAYER - 1], refs[N_LAYER - 1 :]
    load_scales(msgs, scale)

    def step(i, carry):
        out_ref[pl.ds(CB_DEV * i, XQ, stride=RB_DEV * CB_DEV), :] = first_ref[i]
        out_ref[pl.ds(CB_DEV * i + 1, XQ, stride=RB_DEV * CB_DEV), :] = add_messages(own_ref, msgs, scale, i)
        return carry

    lax.fori_loop(0, RB_DEV, step, 0)


def combine(kernel, shape, parts, name):
    vmem = pl.BlockSpec(memory_space=pltpu.VMEM)
    return pl.pallas_call(
        kernel,
        out_shape=jax.ShapeDtypeStruct(shape, jnp.float32),
        in_specs=[vmem] * len(parts),
        out_specs=vmem,
        scratch_shapes=[pltpu.VMEM((N_LAYER - 1, RB_DEV, BS), jnp.float32)],
        compiler_params=pltpu.CompilerParams(vmem_limit_bytes=6 * 2**20),
        cost_estimate=pl.CostEstimate(flops=10**9, bytes_accessed=2**20, transcendentals=0),
        name=name,
    )(*parts)


def prepare_kernel(
    a_ref, rows_ref, ks_ref, live_ref, b_ref, cols_ref, a_out, zero_out, one_out, a_in, zero_in, one_in, sems, out_sems
):
    copies = []
    for n in range(K_DEV):
        first = cols_ref[0, n]
        copies.append(pltpu.make_async_copy(b_ref.at[n, first], zero_in.at[n], sems.at[n]))
        copies.append(pltpu.make_async_copy(b_ref.at[n, 1 - first], one_in.at[n], sems.at[K_DEV + n]))
    copies.append(pltpu.make_async_copy(a_ref, a_in.at[pl.ds(0, A_ROWS)], sems.at[2 * K_DEV]))
    for copy in copies:
        copy.start()
    lane = lax.broadcasted_iota(jnp.int32, (POS_ROWS, BS), 1)
    found = jnp.zeros((POS_ROWS, BS), jnp.int32)
    for s in range(SA):
        target = jnp.where(s < live_ref[0, 0, 0], rows_ref[s], RB_DEV)
        found = jnp.where(lane == s, target, found)
        found = jnp.where(lane == SA + s, ks_ref[s], found)
    a_in[pl.ds(A_ROWS, POS_ROWS), :] = found.astype(jnp.float32).astype(jnp.bfloat16)
    for copy in copies:
        copy.wait()
    outs = [
        pltpu.make_async_copy(held, out, out_sems.at[at])
        for at, (held, out) in enumerate(((zero_in, zero_out), (one_in, one_out), (a_in, a_out)))
    ]
    for out in outs:
        out.start()
    for out in outs:
        out.wait()


def prepare(a_vals, a_rows, a_ks, a_live, b_vals, b_cols):
    smem = pl.BlockSpec(memory_space=pltpu.SMEM)
    any_spec = pl.BlockSpec(memory_space=pl.ANY)
    out_shape = [
        jax.ShapeDtypeStruct((A_ROWS + POS_ROWS, BS), jnp.bfloat16),
        jax.ShapeDtypeStruct((K_DEV, BS, BS), jnp.bfloat16),
        jax.ShapeDtypeStruct((K_DEV, BS, BS), jnp.bfloat16),
    ]
    return pl.pallas_call(
        prepare_kernel,
        out_shape=out_shape,
        in_specs=[any_spec, smem, smem, smem, any_spec, smem],
        out_specs=[any_spec] * 3,
        scratch_shapes=[pltpu.VMEM(one.shape, one.dtype) for one in out_shape]
        + [pltpu.SemaphoreType.DMA((2 * K_DEV + 1,)), pltpu.SemaphoreType.DMA((3,))],
        compiler_params=pltpu.CompilerParams(vmem_limit_bytes=60 * 2**20),
        name="prepare",
    )(
        a_vals.reshape(A_ROWS, BS),
        a_rows.reshape(SA),
        a_ks.reshape(SA),
        a_live,
        b_vals.reshape(K_DEV, PB, BS, BS),
        jnp.transpose(b_cols, (1, 2, 0)).reshape(PB, K_DEV),
    )


def shifted(value, axis, size, by):
    return lax.ppermute(value, axis, [(i, (i + by) % size) for i in range(size)])


def up(value):
    return shifted(value, "row", N_ROW, 1)


def down(value):
    return shifted(value, "row", N_ROW, -1)


def around(b_zero, b_one, hold, early):
    zero, one = {0: b_zero}, {0: b_one}
    zero[7], one[1] = up(zero[0]), down(one[0])
    one[7], zero[1] = up(one[0]), down(zero[0])
    zero[7], one[1] = lax.optimization_barrier((zero[7], one[1]))
    zero[6], one[2] = up(zero[7]), down(one[1])
    zero[1], one[7] = lax.optimization_barrier((zero[1], one[7]))
    one[6], zero[2] = up(one[7]), down(zero[1])
    zero[6], one[2] = lax.optimization_barrier((zero[6], one[2]))
    zero[5], one[3] = up(zero[6]), down(one[2])
    one[6], zero[2] = hold(one[6], zero[2])
    zero[3] = down(zero[2])
    zero[4] = up(zero[5])
    sums = early(zero, one)
    one[6], one[3], *sums = lax.optimization_barrier((one[6], one[3], *sums))
    one[5], one[4] = up(one[6]), down(one[3])
    return zero, one, sums


def send_sums(parts):
    own, msgs = parts[0], parts[1:]
    sent = {q: shifted(msgs[q - 1], "layer", N_LAYER, q) for q in (2, 1, 3)}
    return [own] + [sent[q] for q in range(1, N_LAYER)]


def body(a_vals, a_rows, a_ks, a_live, b_vals, b_cols):
    a_send, b_zero, b_one = prepare(a_vals, a_rows, a_ks, a_live, b_vals, b_cols)
    a_all = lax.all_gather(a_send, "col", axis=0)
    where = [positions(a_all), a_all]

    def hold(*behind):
        *behind, where[0] = lax.optimization_barrier((*behind, where[0]))
        return behind

    def early(zero, one):
        return open_sums(where, (zero, one), (0, 7, 1, 6, 2))

    zero, one, sums = around(b_zero, b_one, hold, early)
    before = open_sums(where, (zero,), (5, 3), sums[:1])
    parts = send_sums(close_sums(where, zero, (4,), before[0], 2 * 10**10))
    first = combine(first_combine_kernel, (RB_DEV, XQ, BS), parts, "first_combine")
    parts = send_sums(close_sums(where, one, (5, 3, 4), sums[1], 10**11))
    rows = XQ * RB_DEV * CB_DEV
    product = combine(last_combine_kernel, (rows, BS), [first] + parts, "last_combine")
    return product.reshape(XQ, RB_DEV, CB_DEV, BS)


def solution(mesh):
    return jax.shard_map(
        body,
        mesh=mesh,
        in_specs=(
            P("layer", "row", "col", None, None, None),
            P("layer", "row", "col", None),
            P("layer", "row", "col", None),
            P("layer", "row", "col"),
            P(("layer", "row"), "col", None, None, None),
            P(("layer", "row"), "col", None),
        ),
        out_specs=P("layer", "row", "col", None),
        check_vma=False,
    )
```

```python
import functools

import jax
import jax.numpy as jnp
from jax import lax
from jax.experimental import pallas as pl
from jax.experimental.pallas import tpu as pltpu
from jax.sharding import PartitionSpec as P

BS = 128
BLK_DEV = 8
SA = 12
PB = 2
RB_DEV = 32
CB_DEV = 2
N_LAYER = 4
N_ROW = 8
N_COL = 16
K_DEV = 16
XQ = BS // N_LAYER
A_ROWS = SA * BS
POS_ROWS = 16
MSG_ROWS = RB_DEV * XQ + RB_DEV
BITS = 13.0
LN2 = 0.6931471805599453


def piece_of(me, place):
    return lax.rem(me + place, N_ROW)


def add_products(place_ref, a_ref, places, chunks):
    row = lax.axis_index("row")
    for at, place in enumerate(places):

        def half(h, carry):
            col = 2 * piece_of(row, place) + h
            for s in range(SA):
                target = place_ref[col, s]
                k = place_ref[col, SA + s]
                block = a_ref[col, pl.ds(s * BS, BS), :]
                for acc, b_refs in chunks:
                    acc[target] += jnp.dot(
                        block, b_refs[at][h * BLK_DEV + k], preferred_element_type=jnp.float32
                    )
            return carry

        lax.fori_loop(0, 2, half, 0)


def open_kernel(places, width, resumed, place_ref, a_ref, *refs):
    outs = refs[-width:]
    count = len(places)
    chunks = [(outs[c], refs[c * count : (c + 1) * count]) for c in range(width)]

    def load(i, carry):
        for c in range(width):
            outs[c][i] = refs[width * count + c][i] if resumed else jnp.zeros((BS, BS), jnp.float32)
        return carry

    lax.fori_loop(0, RB_DEV, load, 0)
    add_products(place_ref, a_ref, places, chunks)


def close_kernel(places, place_ref, a_ref, *refs):
    count = len(places)
    before_ref, own_ref = refs[count : count + 2]
    msg_refs = refs[count + 2 : -2]
    acc, top = refs[-2:]
    layer = lax.axis_index("layer")

    def load(i, carry):
        acc[i] = before_ref[i]
        return carry

    lax.fori_loop(0, RB_DEV, load, 0)
    add_products(place_ref, a_ref, places, [(acc, refs[:count])])

    def keep(i, carry):
        own_ref[i] = acc[i, pl.ds(layer * XQ, XQ), :]
        for q in range(1, N_LAYER):
            start = lax.rem(layer + q, N_LAYER) * XQ
            part = acc[i, pl.ds(start, XQ), :]
            top[q - 1, pl.ds(i, 1), :] = jnp.max(jnp.abs(part), axis=0, keepdims=True)
        return carry

    lax.fori_loop(0, RB_DEV, keep, 0)
    for q in range(1, N_LAYER):
        power = jnp.floor(jnp.log(jnp.maximum(top[q - 1], 1e-30)) * (1.0 / LN2))
        msg_refs[q - 1][pl.ds(RB_DEV * XQ, RB_DEV), :] = power.astype(jnp.int32).astype(jnp.int16)
        top[q - 1] = jnp.exp((BITS - power) * LN2)

    def pack(i, carry):
        for q in range(1, N_LAYER):
            start = lax.rem(layer + q, N_LAYER) * XQ
            part = acc[i, pl.ds(start, XQ), :] * top[q - 1, pl.ds(i, 1), :]
            msg_refs[q - 1][pl.ds(pl.multiple_of(i * XQ, XQ), XQ), :] = (
                jnp.round(part).astype(jnp.int32).astype(jnp.int16)
            )
        return carry

    lax.fori_loop(0, RB_DEV, pack, 0)


def positions_kernel(a_ref, place_ref, held, place, sem):
    copy = pltpu.make_async_copy(a_ref.at[:, pl.ds(A_ROWS, POS_ROWS)], held, sem)
    copy.start()
    copy.wait()
    for col in range(N_COL):
        place[pl.ds(col, 1), :] = held[col].astype(jnp.float32)[:1].astype(jnp.int32)
    copy = pltpu.make_async_copy(place, place_ref, sem)
    copy.start()
    copy.wait()


def positions(a_all):
    shape = (N_COL, BS)
    return pl.pallas_call(
        positions_kernel,
        out_shape=jax.ShapeDtypeStruct(shape, jnp.int32),
        in_specs=[pl.BlockSpec(memory_space=pl.ANY)],
        out_specs=pl.BlockSpec(memory_space=pltpu.SMEM),
        scratch_shapes=[
            pltpu.VMEM((N_COL, POS_ROWS, BS), jnp.bfloat16),
            pltpu.VMEM(shape, jnp.int32),
            pltpu.SemaphoreType.DMA(()),
        ],
        compiler_params=pltpu.CompilerParams(vmem_limit_bytes=50 * 2**20),
        cost_estimate=pl.CostEstimate(flops=5 * 10**9, bytes_accessed=2**20, transcendentals=0),
        name="positions",
    )(a_all)


def call_products(kernel, name, out_shape, scratch, operands, flops):
    smem = pl.BlockSpec(memory_space=pltpu.SMEM)
    vmem = pl.BlockSpec(memory_space=pltpu.VMEM)
    return pl.pallas_call(
        kernel,
        out_shape=out_shape,
        in_specs=[smem] + [vmem] * (len(operands) - 1),
        out_specs=[vmem] * len(out_shape),
        scratch_shapes=scratch,
        compiler_params=pltpu.CompilerParams(vmem_limit_bytes=6 * 2**20),
        cost_estimate=pl.CostEstimate(flops=flops, bytes_accessed=2**20, transcendentals=0),
        name=name,
    )(*operands)


def open_sums(where, chunks, places, before=()):
    sums = jax.ShapeDtypeStruct((RB_DEV + 1, BS, BS), jnp.float32)
    blocks = [chunk[place] for chunk in chunks for place in places]
    return call_products(
        functools.partial(open_kernel, places, len(chunks), bool(before)),
        "open_sums",
        [sums] * len(chunks),
        [],
        [*where, *blocks, *before],
        5 * 10**9,
    )


def close_sums(where, chunk, places, before, flops):
    return call_products(
        functools.partial(close_kernel, places),
        "close_sums",
        [jax.ShapeDtypeStruct((RB_DEV, XQ, BS), jnp.float32)]
        + [jax.ShapeDtypeStruct((MSG_ROWS, BS), jnp.int16)] * (N_LAYER - 1),
        [
            pltpu.VMEM((RB_DEV + 1, BS, BS), jnp.float32),
            pltpu.VMEM((N_LAYER - 1, RB_DEV, BS), jnp.float32),
        ],
        [*where, *(chunk[place] for place in places), before],
        flops,
    )


def add_messages(own_ref, msgs, scale, i):
    total = own_ref[i]
    for q in range(N_LAYER - 1):
        part = msgs[q][pl.ds(pl.multiple_of(i * XQ, XQ), XQ), :]
        total = total + part.astype(jnp.int32).astype(jnp.float32) * scale[q, pl.ds(i, 1), :]
    return total


def load_scales(msgs, scale):
    for q in range(N_LAYER - 1):
        power = msgs[q][pl.ds(RB_DEV * XQ, RB_DEV), :].astype(jnp.int32).astype(jnp.float32)
        scale[q] = jnp.exp((power - BITS) * LN2)


def first_combine_kernel(own_ref, *refs):
    msgs, (out_ref, scale) = refs[: N_LAYER - 1], refs[N_LAYER - 1 :]
    load_scales(msgs, scale)

    def step(i, carry):
        out_ref[i] = add_messages(own_ref, msgs, scale, i)
        return carry

    lax.fori_loop(0, RB_DEV, step, 0)


def last_combine_kernel(first_ref, own_ref, *refs):
    msgs, (out_ref, scale) = refs[: N_LAYER - 1], refs[N_LAYER - 1 :]
    load_scales(msgs, scale)

    def step(i, carry):
        out_ref[pl.ds(CB_DEV * i, XQ, stride=RB_DEV * CB_DEV), :] = first_ref[i]
        out_ref[pl.ds(CB_DEV * i + 1, XQ, stride=RB_DEV * CB_DEV), :] = add_messages(own_ref, msgs, scale, i)
        return carry

    lax.fori_loop(0, RB_DEV, step, 0)


def combine(kernel, shape, parts, name):
    vmem = pl.BlockSpec(memory_space=pltpu.VMEM)
    return pl.pallas_call(
        kernel,
        out_shape=jax.ShapeDtypeStruct(shape, jnp.float32),
        in_specs=[vmem] * len(parts),
        out_specs=vmem,
        scratch_shapes=[pltpu.VMEM((N_LAYER - 1, RB_DEV, BS), jnp.float32)],
        compiler_params=pltpu.CompilerParams(vmem_limit_bytes=6 * 2**20),
        cost_estimate=pl.CostEstimate(flops=10**9, bytes_accessed=2**20, transcendentals=0),
        name=name,
    )(*parts)


def prepare_kernel(
    a_ref, rows_ref, ks_ref, live_ref, b_ref, cols_ref, a_out, zero_out, one_out, a_in, zero_in, one_in, sems, out_sems
):
    copies = []
    for n in range(K_DEV):
        first = cols_ref[0, n]
        copies.append(pltpu.make_async_copy(b_ref.at[n, first], zero_in.at[n], sems.at[n]))
        copies.append(pltpu.make_async_copy(b_ref.at[n, 1 - first], one_in.at[n], sems.at[K_DEV + n]))
    copies.append(pltpu.make_async_copy(a_ref, a_in.at[pl.ds(0, A_ROWS)], sems.at[2 * K_DEV]))
    for copy in copies:
        copy.start()
    lane = lax.broadcasted_iota(jnp.int32, (POS_ROWS, BS), 1)
    found = jnp.zeros((POS_ROWS, BS), jnp.int32)
    for s in range(SA):
        target = jnp.where(s < live_ref[0, 0, 0], rows_ref[s], RB_DEV)
        found = jnp.where(lane == s, target, found)
        found = jnp.where(lane == SA + s, ks_ref[s], found)
    a_in[pl.ds(A_ROWS, POS_ROWS), :] = found.astype(jnp.float32).astype(jnp.bfloat16)
    for copy in copies:
        copy.wait()
    outs = [
        pltpu.make_async_copy(held, out, out_sems.at[at])
        for at, (held, out) in enumerate(((zero_in, zero_out), (one_in, one_out), (a_in, a_out)))
    ]
    for out in outs:
        out.start()
    for out in outs:
        out.wait()


def prepare(a_vals, a_rows, a_ks, a_live, b_vals, b_cols):
    smem = pl.BlockSpec(memory_space=pltpu.SMEM)
    any_spec = pl.BlockSpec(memory_space=pl.ANY)
    out_shape = [
        jax.ShapeDtypeStruct((A_ROWS + POS_ROWS, BS), jnp.bfloat16),
        jax.ShapeDtypeStruct((K_DEV, BS, BS), jnp.bfloat16),
        jax.ShapeDtypeStruct((K_DEV, BS, BS), jnp.bfloat16),
    ]
    return pl.pallas_call(
        prepare_kernel,
        out_shape=out_shape,
        in_specs=[any_spec, smem, smem, smem, any_spec, smem],
        out_specs=[any_spec] * 3,
        scratch_shapes=[pltpu.VMEM(one.shape, one.dtype) for one in out_shape]
        + [pltpu.SemaphoreType.DMA((2 * K_DEV + 1,)), pltpu.SemaphoreType.DMA((3,))],
        compiler_params=pltpu.CompilerParams(vmem_limit_bytes=60 * 2**20),
        name="prepare",
    )(
        a_vals.reshape(A_ROWS, BS),
        a_rows.reshape(SA),
        a_ks.reshape(SA),
        a_live,
        b_vals.reshape(K_DEV, PB, BS, BS),
        jnp.transpose(b_cols, (1, 2, 0)).reshape(PB, K_DEV),
    )


def shifted(value, axis, size, by):
    return lax.ppermute(value, axis, [(i, (i + by) % size) for i in range(size)])


def up(value):
    return shifted(value, "row", N_ROW, 1)


def down(value):
    return shifted(value, "row", N_ROW, -1)


def around(b_zero, b_one, hold, early):
    zero, one = {0: b_zero}, {0: b_one}
    zero[7], one[1] = up(zero[0]), down(one[0])
    one[7], zero[1] = up(one[0]), down(zero[0])
    zero[7], one[1] = lax.optimization_barrier((zero[7], one[1]))
    zero[6], one[2] = up(zero[7]), down(one[1])
    zero[1], one[7] = lax.optimization_barrier((zero[1], one[7]))
    one[6], zero[2] = up(one[7]), down(zero[1])
    zero[6], one[2] = lax.optimization_barrier((zero[6], one[2]))
    zero[5], one[3] = up(zero[6]), down(one[2])
    one[6], zero[2] = hold(one[6], zero[2])
    zero[3] = down(zero[2])
    sums = early(zero, one)
    zero[5], *sums = lax.optimization_barrier((zero[5], *sums))
    zero[4] = up(zero[5])
    one[6], one[3], *sums = lax.optimization_barrier((one[6], one[3], *sums))
    one[5], one[4] = up(one[6]), down(one[3])
    return zero, one, sums


def send_sums(parts):
    own, msgs = parts[0], parts[1:]
    sent = {q: shifted(msgs[q - 1], "layer", N_LAYER, q) for q in (2, 1, 3)}
    return [own, *sent.values()]


def body(a_vals, a_rows, a_ks, a_live, b_vals, b_cols):
    a_send, b_zero, b_one = prepare(a_vals, a_rows, a_ks, a_live, b_vals, b_cols)
    a_all = lax.all_gather(a_send, "col", axis=0)
    where = [positions(a_all), a_all]

    def hold(*behind):
        *behind, where[0] = lax.optimization_barrier((*behind, where[0]))
        return behind

    def early(zero, one):
        return open_sums(where, (zero, one), (7, 1, 6, 2))

    zero, one, sums = around(b_zero, b_one, hold, early)
    before = open_sums(where, (zero,), (5, 3, 0), sums[:1])
    parts = send_sums(close_sums(where, zero, (4,), before[0], 2 * 10**10))
    first = combine(first_combine_kernel, (RB_DEV, XQ, BS), parts, "first_combine")
    parts = send_sums(close_sums(where, one, (0, 5, 3, 4), sums[1], 10**11))
    rows = XQ * RB_DEV * CB_DEV
    product = combine(last_combine_kernel, (rows, BS), [first] + parts, "last_combine")
    return product.reshape(XQ, RB_DEV, CB_DEV, BS)


def solution(mesh):
    return jax.shard_map(
        body,
        mesh=mesh,
        in_specs=(
            P("layer", "row", "col", None, None, None),
            P("layer", "row", "col", None),
            P("layer", "row", "col", None),
            P("layer", "row", "col"),
            P(("layer", "row"), "col", None, None, None),
            P(("layer", "row"), "col", None),
        ),
        out_specs=P("layer", "row", "col", None),
        check_vma=False,
    )
```

```python
import functools

import jax
import jax.numpy as jnp
from jax import lax
from jax.experimental import pallas as pl
from jax.experimental.pallas import tpu as pltpu
from jax.sharding import PartitionSpec as P

BS = 128
BLK_DEV = 8
SA = 12
PB = 2
RB_DEV = 32
CB_DEV = 2
N_LAYER = 4
N_ROW = 8
N_COL = 16
K_DEV = 16
XQ = BS // N_LAYER
A_ROWS = SA * BS
POS_ROWS = 16
MSG_ROWS = RB_DEV * XQ + RB_DEV
BITS = 13.0
LN2 = 0.6931471805599453


def piece_of(me, place):
    return lax.rem(me + place, N_ROW)


def add_products(place_ref, a_ref, places, acc, b_refs):
    row = lax.axis_index("row")
    for place, b_ref in zip(places, b_refs):

        def half(h, carry):
            col = 2 * piece_of(row, place) + h
            for s in range(SA):
                target = place_ref[col, s]
                k = place_ref[col, SA + s]
                acc[target] += jnp.dot(
                    a_ref[col, pl.ds(s * BS, BS), :],
                    b_ref[h * BLK_DEV + k],
                    preferred_element_type=jnp.float32,
                )
            return carry

        lax.fori_loop(0, 2, half, 0)


def add_both(place_ref, a_ref, places, accs, b_refs):
    row = lax.axis_index("row")
    for place, pair in zip(places, b_refs):

        def half(h, carry):
            col = 2 * piece_of(row, place) + h
            for s in range(SA):
                target = place_ref[col, s]
                k = place_ref[col, SA + s]
                block = a_ref[col, pl.ds(s * BS, BS), :]
                for acc, b_ref in zip(accs, pair):
                    acc[target] += jnp.dot(
                        block, b_ref[h * BLK_DEV + k], preferred_element_type=jnp.float32
                    )
            return carry

        lax.fori_loop(0, 2, half, 0)


def open_kernel(both, alone, resumed, place_ref, a_ref, *refs):
    width = len(alone)
    outs = refs[-width:]
    refs = list(refs[:-width])

    pairs = [[refs.pop(0) for _ in range(width)] for _ in both]
    singles = [[refs.pop(0) for _ in places] for places in alone]

    def load(i, carry):
        for c in range(width):
            outs[c][i] = refs[c][i] if resumed else jnp.zeros((BS, BS), jnp.float32)
        return carry

    lax.fori_loop(0, RB_DEV, load, 0)
    add_both(place_ref, a_ref, both, outs, pairs)
    for c in range(width):
        add_products(place_ref, a_ref, alone[c], outs[c], singles[c])


def close_kernel(places, place_ref, a_ref, *refs):
    count = len(places)
    before_ref, own_ref = refs[count : count + 2]
    msg_refs = refs[count + 2 : -2]
    acc, top = refs[-2:]
    layer = lax.axis_index("layer")

    def load(i, carry):
        acc[i] = before_ref[i]
        return carry

    lax.fori_loop(0, RB_DEV, load, 0)
    add_products(place_ref, a_ref, places, acc, refs[:count])

    def keep(i, carry):
        own_ref[i] = acc[i, pl.ds(layer * XQ, XQ), :]
        for q in range(1, N_LAYER):
            start = lax.rem(layer + q, N_LAYER) * XQ
            part = acc[i, pl.ds(start, XQ), :]
            top[q - 1, pl.ds(i, 1), :] = jnp.max(jnp.abs(part), axis=0, keepdims=True)
        return carry

    lax.fori_loop(0, RB_DEV, keep, 0)
    for q in range(1, N_LAYER):
        power = jnp.floor(jnp.log(jnp.maximum(top[q - 1], 1e-30)) * (1.0 / LN2))
        msg_refs[q - 1][pl.ds(RB_DEV * XQ, RB_DEV), :] = power.astype(jnp.int32).astype(jnp.int16)
        top[q - 1] = jnp.exp((BITS - power) * LN2)

    def pack(i, carry):
        for q in range(1, N_LAYER):
            start = lax.rem(layer + q, N_LAYER) * XQ
            part = acc[i, pl.ds(start, XQ), :] * top[q - 1, pl.ds(i, 1), :]
            msg_refs[q - 1][pl.ds(pl.multiple_of(i * XQ, XQ), XQ), :] = (
                jnp.round(part).astype(jnp.int32).astype(jnp.int16)
            )
        return carry

    lax.fori_loop(0, RB_DEV, pack, 0)


def positions_kernel(a_ref, place_ref, held, place, sem):
    copy = pltpu.make_async_copy(a_ref.at[:, pl.ds(A_ROWS, POS_ROWS)], held, sem)
    copy.start()
    copy.wait()
    for col in range(N_COL):
        place[pl.ds(col, 1), :] = held[col].astype(jnp.float32)[:1].astype(jnp.int32)
    copy = pltpu.make_async_copy(place, place_ref, sem)
    copy.start()
    copy.wait()


def positions(a_all):
    shape = (N_COL, BS)
    return pl.pallas_call(
        positions_kernel,
        out_shape=jax.ShapeDtypeStruct(shape, jnp.int32),
        in_specs=[pl.BlockSpec(memory_space=pl.ANY)],
        out_specs=pl.BlockSpec(memory_space=pltpu.SMEM),
        scratch_shapes=[
            pltpu.VMEM((N_COL, POS_ROWS, BS), jnp.bfloat16),
            pltpu.VMEM(shape, jnp.int32),
            pltpu.SemaphoreType.DMA(()),
        ],
        compiler_params=pltpu.CompilerParams(vmem_limit_bytes=50 * 2**20),
        cost_estimate=pl.CostEstimate(flops=5 * 10**9, bytes_accessed=2**20, transcendentals=0),
        name="positions",
    )(a_all)


def call_products(kernel, name, out_shape, scratch, operands, flops):
    smem = pl.BlockSpec(memory_space=pltpu.SMEM)
    vmem = pl.BlockSpec(memory_space=pltpu.VMEM)
    return pl.pallas_call(
        kernel,
        out_shape=out_shape,
        in_specs=[smem] + [vmem] * (len(operands) - 1),
        out_specs=[vmem] * len(out_shape),
        scratch_shapes=scratch,
        compiler_params=pltpu.CompilerParams(vmem_limit_bytes=6 * 2**20),
        cost_estimate=pl.CostEstimate(flops=flops, bytes_accessed=2**20, transcendentals=0),
        name=name,
    )(*operands)


def open_sums(where, chunks, both, alone, before=()):
    sums = jax.ShapeDtypeStruct((RB_DEV + 1, BS, BS), jnp.float32)
    blocks = [chunk[place] for place in both for chunk in chunks]
    blocks += [chunk[place] for chunk, places in zip(chunks, alone) for place in places]
    return call_products(
        functools.partial(open_kernel, both, alone, bool(before)),
        "open_sums",
        [sums] * len(chunks),
        [],
        [*where, *blocks, *before],
        5 * 10**9,
    )


def close_sums(where, chunk, places, before, flops):
    return call_products(
        functools.partial(close_kernel, places),
        "close_sums",
        [jax.ShapeDtypeStruct((RB_DEV, XQ, BS), jnp.float32)]
        + [jax.ShapeDtypeStruct((MSG_ROWS, BS), jnp.int16)] * (N_LAYER - 1),
        [
            pltpu.VMEM((RB_DEV + 1, BS, BS), jnp.float32),
            pltpu.VMEM((N_LAYER - 1, RB_DEV, BS), jnp.float32),
        ],
        [*where, *(chunk[place] for place in places), before],
        flops,
    )


def add_messages(own_ref, msgs, scale, i):
    total = own_ref[i]
    for q in range(N_LAYER - 1):
        part = msgs[q][pl.ds(pl.multiple_of(i * XQ, XQ), XQ), :]
        total = total + part.astype(jnp.int32).astype(jnp.float32) * scale[q, pl.ds(i, 1), :]
    return total


def load_scales(msgs, scale):
    for q in range(N_LAYER - 1):
        power = msgs[q][pl.ds(RB_DEV * XQ, RB_DEV), :].astype(jnp.int32).astype(jnp.float32)
        scale[q] = jnp.exp((power - BITS) * LN2)


def first_combine_kernel(own_ref, *refs):
    msgs, (out_ref, scale) = refs[: N_LAYER - 1], refs[N_LAYER - 1 :]
    load_scales(msgs, scale)

    def step(i, carry):
        out_ref[i] = add_messages(own_ref, msgs, scale, i)
        return carry

    lax.fori_loop(0, RB_DEV, step, 0)


def last_combine_kernel(first_ref, own_ref, *refs):
    msgs, (out_ref, scale) = refs[: N_LAYER - 1], refs[N_LAYER - 1 :]
    load_scales(msgs, scale)

    def step(i, carry):
        out_ref[pl.ds(CB_DEV * i, XQ, stride=RB_DEV * CB_DEV), :] = first_ref[i]
        out_ref[pl.ds(CB_DEV * i + 1, XQ, stride=RB_DEV * CB_DEV), :] = add_messages(own_ref, msgs, scale, i)
        return carry

    lax.fori_loop(0, RB_DEV, step, 0)


def combine(kernel, shape, parts, name):
    vmem = pl.BlockSpec(memory_space=pltpu.VMEM)
    return pl.pallas_call(
        kernel,
        out_shape=jax.ShapeDtypeStruct(shape, jnp.float32),
        in_specs=[vmem] * len(parts),
        out_specs=vmem,
        scratch_shapes=[pltpu.VMEM((N_LAYER - 1, RB_DEV, BS), jnp.float32)],
        compiler_params=pltpu.CompilerParams(vmem_limit_bytes=6 * 2**20),
        cost_estimate=pl.CostEstimate(flops=10**9, bytes_accessed=2**20, transcendentals=0),
        name=name,
    )(*parts)


def prepare_kernel(
    a_ref, rows_ref, ks_ref, live_ref, b_ref, cols_ref, a_out, zero_out, one_out, a_in, zero_in, one_in, sems, out_sems
):
    copies = []
    for n in range(K_DEV):
        first = cols_ref[0, n]
        copies.append(pltpu.make_async_copy(b_ref.at[n, first], zero_in.at[n], sems.at[n]))
        copies.append(pltpu.make_async_copy(b_ref.at[n, 1 - first], one_in.at[n], sems.at[K_DEV + n]))
    copies.append(pltpu.make_async_copy(a_ref, a_in.at[pl.ds(0, A_ROWS)], sems.at[2 * K_DEV]))
    for copy in copies:
        copy.start()
    lane = lax.broadcasted_iota(jnp.int32, (POS_ROWS, BS), 1)
    found = jnp.zeros((POS_ROWS, BS), jnp.int32)
    for s in range(SA):
        target = jnp.where(s < live_ref[0, 0, 0], rows_ref[s], RB_DEV)
        found = jnp.where(lane == s, target, found)
        found = jnp.where(lane == SA + s, ks_ref[s], found)
    a_in[pl.ds(A_ROWS, POS_ROWS), :] = found.astype(jnp.float32).astype(jnp.bfloat16)
    for copy in copies:
        copy.wait()
    outs = [
        pltpu.make_async_copy(held, out, out_sems.at[at])
        for at, (held, out) in enumerate(((zero_in, zero_out), (one_in, one_out), (a_in, a_out)))
    ]
    for out in outs:
        out.start()
    for out in outs:
        out.wait()


def prepare(a_vals, a_rows, a_ks, a_live, b_vals, b_cols):
    smem = pl.BlockSpec(memory_space=pltpu.SMEM)
    any_spec = pl.BlockSpec(memory_space=pl.ANY)
    out_shape = [
        jax.ShapeDtypeStruct((A_ROWS + POS_ROWS, BS), jnp.bfloat16),
        jax.ShapeDtypeStruct((K_DEV, BS, BS), jnp.bfloat16),
        jax.ShapeDtypeStruct((K_DEV, BS, BS), jnp.bfloat16),
    ]
    return pl.pallas_call(
        prepare_kernel,
        out_shape=out_shape,
        in_specs=[any_spec, smem, smem, smem, any_spec, smem],
        out_specs=[any_spec] * 3,
        scratch_shapes=[pltpu.VMEM(one.shape, one.dtype) for one in out_shape]
        + [pltpu.SemaphoreType.DMA((2 * K_DEV + 1,)), pltpu.SemaphoreType.DMA((3,))],
        compiler_params=pltpu.CompilerParams(vmem_limit_bytes=60 * 2**20),
        name="prepare",
    )(
        a_vals.reshape(A_ROWS, BS),
        a_rows.reshape(SA),
        a_ks.reshape(SA),
        a_live,
        b_vals.reshape(K_DEV, PB, BS, BS),
        jnp.transpose(b_cols, (1, 2, 0)).reshape(PB, K_DEV),
    )


def shifted(value, axis, size, by):
    return lax.ppermute(value, axis, [(i, (i + by) % size) for i in range(size)])


def up(value):
    return shifted(value, "row", N_ROW, 1)


def down(value):
    return shifted(value, "row", N_ROW, -1)


def around(b_zero, b_one, hold, early, middle):
    zero, one = {0: b_zero}, {0: b_one}
    zero[7], one[1] = up(zero[0]), down(one[0])
    one[7], zero[1] = up(one[0]), down(zero[0])
    zero[7], one[1] = lax.optimization_barrier((zero[7], one[1]))
    zero[6], one[2] = up(zero[7]), down(one[1])
    zero[1], one[7] = lax.optimization_barrier((zero[1], one[7]))
    one[6], zero[2] = up(one[7]), down(zero[1])
    zero[6], one[2] = lax.optimization_barrier((zero[6], one[2]))
    zero[5], one[3] = up(zero[6]), down(one[2])
    one[6], zero[2] = hold(one[6], zero[2])
    zero[3] = down(zero[2])
    sums = early(zero, one)
    zero[5], *sums = lax.optimization_barrier((zero[5], *sums))
    zero[4] = up(zero[5])
    sums = middle(zero, one, sums)
    one[6], one[3], *sums = lax.optimization_barrier((one[6], one[3], *sums))
    one[5], one[4] = up(one[6]), down(one[3])
    return zero, one, sums


def send_sums(parts):
    own, msgs = parts[0], parts[1:]
    sent = {q: shifted(msgs[q - 1], "layer", N_LAYER, q) for q in (2, 1, 3)}
    return [own, *sent.values()]


def body(a_vals, a_rows, a_ks, a_live, b_vals, b_cols):
    a_send, b_zero, b_one = prepare(a_vals, a_rows, a_ks, a_live, b_vals, b_cols)
    a_all = lax.all_gather(a_send, "col", axis=0)
    where = [positions(a_all), a_all]

    def hold(*behind):
        *behind, where[0] = lax.optimization_barrier((*behind, where[0]))
        return behind

    def early(zero, one):
        return open_sums(where, (zero, one), (7, 1, 6, 2), ((), ()))

    def middle(zero, one, sums):
        return open_sums(where, (zero, one), (0,), ((5,), (3,)), sums)

    zero, one, sums = around(b_zero, b_one, hold, early, middle)
    before = open_sums(where, (zero,), (), ((3,),), sums[:1])
    parts = send_sums(close_sums(where, zero, (4,), before[0], 2 * 10**10))
    first = combine(first_combine_kernel, (RB_DEV, XQ, BS), parts, "first_combine")
    parts = send_sums(close_sums(where, one, (5, 4), sums[1], 10**11))
    rows = XQ * RB_DEV * CB_DEV
    product = combine(last_combine_kernel, (rows, BS), [first] + parts, "last_combine")
    return product.reshape(XQ, RB_DEV, CB_DEV, BS)


def solution(mesh):
    return jax.shard_map(
        body,
        mesh=mesh,
        in_specs=(
            P("layer", "row", "col", None, None, None),
            P("layer", "row", "col", None),
            P("layer", "row", "col", None),
            P("layer", "row", "col"),
            P(("layer", "row"), "col", None, None, None),
            P(("layer", "row"), "col", None),
        ),
        out_specs=P("layer", "row", "col", None),
        check_vma=False,
    )
```

```python
import functools

import jax
import jax.numpy as jnp
from jax import lax
from jax.experimental import pallas as pl
from jax.experimental.pallas import tpu as pltpu
from jax.sharding import PartitionSpec as P

BS = 128
BLK_DEV = 8
SA = 12
PB = 2
RB_DEV = 32
CB_DEV = 2
N_LAYER = 4
N_ROW = 8
N_COL = 16
K_DEV = 16
XQ = BS // N_LAYER
A_ROWS = SA * BS
POS_ROWS = 16
MSG_ROWS = RB_DEV * XQ + RB_DEV
BITS = 13.0
LN2 = 0.6931471805599453


def piece_of(me, place):
    return lax.rem(me + place, N_ROW)


def add_products(place_ref, a_ref, places, acc, b_refs):
    row = lax.axis_index("row")
    for place, b_ref in zip(places, b_refs):

        def half(h, carry):
            col = 2 * piece_of(row, place) + h
            for s in range(SA):
                target = place_ref[col, s]
                k = place_ref[col, SA + s]
                acc[target] += jnp.dot(
                    a_ref[col, pl.ds(s * BS, BS), :],
                    b_ref[h * BLK_DEV + k],
                    preferred_element_type=jnp.float32,
                )
            return carry

        lax.fori_loop(0, 2, half, 0)


def add_both(place_ref, a_ref, places, accs, b_refs):
    row = lax.axis_index("row")
    for place, pair in zip(places, b_refs):

        def half(h, carry):
            col = 2 * piece_of(row, place) + h
            for s in range(SA):
                target = place_ref[col, s]
                k = place_ref[col, SA + s]
                block = a_ref[col, pl.ds(s * BS, BS), :]
                for acc, b_ref in zip(accs, pair):
                    acc[target] += jnp.dot(
                        block, b_ref[h * BLK_DEV + k], preferred_element_type=jnp.float32
                    )
            return carry

        lax.fori_loop(0, 2, half, 0)


def open_kernel(both, alone, resumed, place_ref, a_ref, *refs):
    width = len(alone)
    outs = refs[-width:]
    refs = list(refs[:-width])

    pairs = [[refs.pop(0) for _ in range(width)] for _ in both]
    singles = [[refs.pop(0) for _ in places] for places in alone]

    def load(i, carry):
        for c in range(width):
            outs[c][i] = refs[c][i] if resumed else jnp.zeros((BS, BS), jnp.float32)
        return carry

    lax.fori_loop(0, RB_DEV, load, 0)
    add_both(place_ref, a_ref, both, outs, pairs)
    for c in range(width):
        add_products(place_ref, a_ref, alone[c], outs[c], singles[c])


def close_kernel(places, place_ref, a_ref, *refs):
    count = len(places)
    before_ref, own_ref = refs[count : count + 2]
    msg_refs = refs[count + 2 : -2]
    acc, top = refs[-2:]
    layer = lax.axis_index("layer")

    def load(i, carry):
        acc[i] = before_ref[i]
        return carry

    lax.fori_loop(0, RB_DEV, load, 0)
    add_products(place_ref, a_ref, places, acc, refs[:count])

    def keep(i, carry):
        own_ref[i] = acc[i, pl.ds(layer * XQ, XQ), :]
        for q in range(1, N_LAYER):
            start = lax.rem(layer + q, N_LAYER) * XQ
            part = acc[i, pl.ds(start, XQ), :]
            top[q - 1, pl.ds(i, 1), :] = jnp.max(jnp.abs(part), axis=0, keepdims=True)
        return carry

    lax.fori_loop(0, RB_DEV, keep, 0)
    for q in range(1, N_LAYER):
        power = jnp.floor(jnp.log(jnp.maximum(top[q - 1], 1e-30)) * (1.0 / LN2))
        msg_refs[q - 1][pl.ds(RB_DEV * XQ, RB_DEV), :] = power.astype(jnp.int32).astype(jnp.int16)
        top[q - 1] = jnp.exp((BITS - power) * LN2)

    def pack(i, carry):
        for q in range(1, N_LAYER):
            start = lax.rem(layer + q, N_LAYER) * XQ
            part = acc[i, pl.ds(start, XQ), :] * top[q - 1, pl.ds(i, 1), :]
            msg_refs[q - 1][pl.ds(pl.multiple_of(i * XQ, XQ), XQ), :] = (
                jnp.round(part).astype(jnp.int32).astype(jnp.int16)
            )
        return carry

    lax.fori_loop(0, RB_DEV, pack, 0)


def positions_kernel(a_ref, place_ref, held, place, sem):
    copy = pltpu.make_async_copy(a_ref.at[:, pl.ds(A_ROWS, POS_ROWS)], held, sem)
    copy.start()
    copy.wait()
    for col in range(N_COL):
        place[pl.ds(col, 1), :] = held[col].astype(jnp.float32)[:1].astype(jnp.int32)
    copy = pltpu.make_async_copy(place, place_ref, sem)
    copy.start()
    copy.wait()


def positions(a_all):
    shape = (N_COL, BS)
    return pl.pallas_call(
        positions_kernel,
        out_shape=jax.ShapeDtypeStruct(shape, jnp.int32),
        in_specs=[pl.BlockSpec(memory_space=pl.ANY)],
        out_specs=pl.BlockSpec(memory_space=pltpu.SMEM),
        scratch_shapes=[
            pltpu.VMEM((N_COL, POS_ROWS, BS), jnp.bfloat16),
            pltpu.VMEM(shape, jnp.int32),
            pltpu.SemaphoreType.DMA(()),
        ],
        compiler_params=pltpu.CompilerParams(vmem_limit_bytes=50 * 2**20),
        cost_estimate=pl.CostEstimate(flops=5 * 10**9, bytes_accessed=2**20, transcendentals=0),
        name="positions",
    )(a_all)


def call_products(kernel, name, out_shape, scratch, operands, flops):
    smem = pl.BlockSpec(memory_space=pltpu.SMEM)
    vmem = pl.BlockSpec(memory_space=pltpu.VMEM)
    return pl.pallas_call(
        kernel,
        out_shape=out_shape,
        in_specs=[smem] + [vmem] * (len(operands) - 1),
        out_specs=[vmem] * len(out_shape),
        scratch_shapes=scratch,
        compiler_params=pltpu.CompilerParams(vmem_limit_bytes=6 * 2**20),
        cost_estimate=pl.CostEstimate(flops=flops, bytes_accessed=2**20, transcendentals=0),
        name=name,
    )(*operands)


def open_sums(where, chunks, both, alone, before=()):
    sums = jax.ShapeDtypeStruct((RB_DEV + 1, BS, BS), jnp.float32)
    blocks = [chunk[place] for place in both for chunk in chunks]
    blocks += [chunk[place] for chunk, places in zip(chunks, alone) for place in places]
    return call_products(
        functools.partial(open_kernel, both, alone, bool(before)),
        "open_sums",
        [sums] * len(chunks),
        [],
        [*where, *blocks, *before],
        5 * 10**9,
    )


def close_sums(where, chunk, places, before, flops):
    return call_products(
        functools.partial(close_kernel, places),
        "close_sums",
        [jax.ShapeDtypeStruct((RB_DEV, XQ, BS), jnp.float32)]
        + [jax.ShapeDtypeStruct((MSG_ROWS, BS), jnp.int16)] * (N_LAYER - 1),
        [
            pltpu.VMEM((RB_DEV + 1, BS, BS), jnp.float32),
            pltpu.VMEM((N_LAYER - 1, RB_DEV, BS), jnp.float32),
        ],
        [*where, *(chunk[place] for place in places), before],
        flops,
    )


def add_messages(own_ref, msgs, scale, i):
    total = own_ref[i]
    for q in range(N_LAYER - 1):
        part = msgs[q][pl.ds(pl.multiple_of(i * XQ, XQ), XQ), :]
        total = total + part.astype(jnp.int32).astype(jnp.float32) * scale[q, pl.ds(i, 1), :]
    return total


def load_scales(msgs, scale):
    for q in range(N_LAYER - 1):
        power = msgs[q][pl.ds(RB_DEV * XQ, RB_DEV), :].astype(jnp.int32).astype(jnp.float32)
        scale[q] = jnp.exp((power - BITS) * LN2)


def first_combine_kernel(own_ref, *refs):
    msgs, (out_ref, scale) = refs[: N_LAYER - 1], refs[N_LAYER - 1 :]
    load_scales(msgs, scale)

    def step(i, carry):
        out_ref[i] = add_messages(own_ref, msgs, scale, i)
        return carry

    lax.fori_loop(0, RB_DEV, step, 0)


def last_combine_kernel(first_ref, own_ref, *refs):
    msgs, (out_ref, scale) = refs[: N_LAYER - 1], refs[N_LAYER - 1 :]
    load_scales(msgs, scale)

    def step(i, carry):
        out_ref[pl.ds(CB_DEV * i, XQ, stride=RB_DEV * CB_DEV), :] = first_ref[i]
        out_ref[pl.ds(CB_DEV * i + 1, XQ, stride=RB_DEV * CB_DEV), :] = add_messages(own_ref, msgs, scale, i)
        return carry

    lax.fori_loop(0, RB_DEV, step, 0)


def combine(kernel, shape, parts, name):
    vmem = pl.BlockSpec(memory_space=pltpu.VMEM)
    return pl.pallas_call(
        kernel,
        out_shape=jax.ShapeDtypeStruct(shape, jnp.float32),
        in_specs=[vmem] * len(parts),
        out_specs=vmem,
        scratch_shapes=[pltpu.VMEM((N_LAYER - 1, RB_DEV, BS), jnp.float32)],
        compiler_params=pltpu.CompilerParams(vmem_limit_bytes=6 * 2**20),
        cost_estimate=pl.CostEstimate(flops=10**9, bytes_accessed=2**20, transcendentals=0),
        name=name,
    )(*parts)


def prepare_kernel(
    a_ref, rows_ref, ks_ref, live_ref, b_ref, cols_ref, a_out, zero_out, one_out, a_in, zero_in, one_in, sems, out_sems
):
    copies = []
    for n in range(K_DEV):
        first = cols_ref[0, n]
        copies.append(pltpu.make_async_copy(b_ref.at[n, first], zero_in.at[n], sems.at[n]))
        copies.append(pltpu.make_async_copy(b_ref.at[n, 1 - first], one_in.at[n], sems.at[K_DEV + n]))
    copies.append(pltpu.make_async_copy(a_ref, a_in.at[pl.ds(0, A_ROWS)], sems.at[2 * K_DEV]))
    for copy in copies:
        copy.start()
    lane = lax.broadcasted_iota(jnp.int32, (POS_ROWS, BS), 1)
    found = jnp.zeros((POS_ROWS, BS), jnp.int32)
    for s in range(SA):
        target = jnp.where(s < live_ref[0, 0, 0], rows_ref[s], RB_DEV)
        found = jnp.where(lane == s, target, found)
        found = jnp.where(lane == SA + s, ks_ref[s], found)
    a_in[pl.ds(A_ROWS, POS_ROWS), :] = found.astype(jnp.float32).astype(jnp.bfloat16)
    for copy in copies:
        copy.wait()
    outs = [
        pltpu.make_async_copy(held, out, out_sems.at[at])
        for at, (held, out) in enumerate(((zero_in, zero_out), (one_in, one_out), (a_in, a_out)))
    ]
    for out in outs:
        out.start()
    for out in outs:
        out.wait()


def prepare(a_vals, a_rows, a_ks, a_live, b_vals, b_cols):
    smem = pl.BlockSpec(memory_space=pltpu.SMEM)
    any_spec = pl.BlockSpec(memory_space=pl.ANY)
    out_shape = [
        jax.ShapeDtypeStruct((A_ROWS + POS_ROWS, BS), jnp.bfloat16),
        jax.ShapeDtypeStruct((K_DEV, BS, BS), jnp.bfloat16),
        jax.ShapeDtypeStruct((K_DEV, BS, BS), jnp.bfloat16),
    ]
    return pl.pallas_call(
        prepare_kernel,
        out_shape=out_shape,
        in_specs=[any_spec, smem, smem, smem, any_spec, smem],
        out_specs=[any_spec] * 3,
        scratch_shapes=[pltpu.VMEM(one.shape, one.dtype) for one in out_shape]
        + [pltpu.SemaphoreType.DMA((2 * K_DEV + 1,)), pltpu.SemaphoreType.DMA((3,))],
        compiler_params=pltpu.CompilerParams(vmem_limit_bytes=60 * 2**20),
        name="prepare",
    )(
        a_vals.reshape(A_ROWS, BS),
        a_rows.reshape(SA),
        a_ks.reshape(SA),
        a_live,
        b_vals.reshape(K_DEV, PB, BS, BS),
        jnp.transpose(b_cols, (1, 2, 0)).reshape(PB, K_DEV),
    )


def shifted(value, axis, size, by):
    return lax.ppermute(value, axis, [(i, (i + by) % size) for i in range(size)])


def up(value):
    return shifted(value, "row", N_ROW, 1)


def down(value):
    return shifted(value, "row", N_ROW, -1)


def around(b_zero, b_one, hold, early, middle):
    zero, one = {0: b_zero}, {0: b_one}
    zero[7], one[1] = up(zero[0]), down(one[0])
    one[7], zero[1] = up(one[0]), down(zero[0])
    zero[7], one[1] = lax.optimization_barrier((zero[7], one[1]))
    zero[6], one[2] = up(zero[7]), down(one[1])
    zero[1], one[7] = lax.optimization_barrier((zero[1], one[7]))
    one[6], zero[2] = up(one[7]), down(zero[1])
    zero[6], one[2] = lax.optimization_barrier((zero[6], one[2]))
    zero[5], one[3] = up(zero[6]), down(one[2])
    one[6], zero[2] = hold(one[6], zero[2])
    zero[3] = down(zero[2])
    sums = early(zero, one)
    zero[5], *sums = lax.optimization_barrier((zero[5], *sums))
    zero[4] = up(zero[5])
    sums = middle(zero, one, sums)
    one[3], one[6], *sums = lax.optimization_barrier((one[3], one[6], *sums))
    one[4], one[5] = down(one[3]), up(one[6])
    return zero, one, sums


def send_sums(parts):
    own, msgs = parts[0], parts[1:]
    sent = {q: shifted(msgs[q - 1], "layer", N_LAYER, q) for q in (2, 1, 3)}
    return [own, *sent.values()]


def body(a_vals, a_rows, a_ks, a_live, b_vals, b_cols):
    a_send, b_zero, b_one = prepare(a_vals, a_rows, a_ks, a_live, b_vals, b_cols)
    a_all = lax.all_gather(a_send, "col", axis=0)
    where = [positions(a_all), a_all]

    def hold(*behind):
        *behind, where[0] = lax.optimization_barrier((*behind, where[0]))
        return behind

    def early(zero, one):
        return open_sums(where, (zero, one), (7, 1, 6, 2), ((), ()))

    def middle(zero, one, sums):
        return open_sums(where, (zero, one), (0,), ((5,), (3,)), sums)

    zero, one, sums = around(b_zero, b_one, hold, early, middle)
    before = open_sums(where, (zero,), (), ((3,),), sums[:1])
    parts = send_sums(close_sums(where, zero, (4,), before[0], 2 * 10**10))
    first = combine(first_combine_kernel, (RB_DEV, XQ, BS), parts, "first_combine")
    parts = send_sums(close_sums(where, one, (4, 5), sums[1], 10**11))
    rows = XQ * RB_DEV * CB_DEV
    product = combine(last_combine_kernel, (rows, BS), [first] + parts, "last_combine")
    return product.reshape(XQ, RB_DEV, CB_DEV, BS)


def solution(mesh):
    return jax.shard_map(
        body,
        mesh=mesh,
        in_specs=(
            P("layer", "row", "col", None, None, None),
            P("layer", "row", "col", None),
            P("layer", "row", "col", None),
            P("layer", "row", "col"),
            P(("layer", "row"), "col", None, None, None),
            P(("layer", "row"), "col", None),
        ),
        out_specs=P("layer", "row", "col", None),
        check_vma=False,
    )
```

```python
import functools

import jax
import jax.numpy as jnp
from jax import lax
from jax.experimental import pallas as pl
from jax.experimental.pallas import tpu as pltpu
from jax.sharding import PartitionSpec as P

BS = 128
BLK_DEV = 8
SA = 12
PB = 2
RB_DEV = 32
CB_DEV = 2
N_LAYER = 4
N_ROW = 8
N_COL = 16
K_DEV = 16
XQ = BS // N_LAYER
A_ROWS = SA * BS
POS_ROWS = 16
MSG_ROWS = RB_DEV * XQ + RB_DEV
BITS = 13.0
LN2 = 0.6931471805599453


def piece_of(me, place):
    return lax.rem(me + place, N_ROW)


def add_products(place_ref, a_ref, places, acc, b_refs):
    row = lax.axis_index("row")
    for place, b_ref in zip(places, b_refs):

        def half(h, carry):
            col = 2 * piece_of(row, place) + h
            for s in range(SA):
                target = place_ref[col, s]
                k = place_ref[col, SA + s]
                acc[target] += jnp.dot(
                    a_ref[col, pl.ds(s * BS, BS), :],
                    b_ref[h * BLK_DEV + k],
                    preferred_element_type=jnp.float32,
                )
            return carry

        lax.fori_loop(0, 2, half, 0)


def add_both(place_ref, a_ref, places, accs, b_refs):
    row = lax.axis_index("row")
    for place, pair in zip(places, b_refs):

        def half(h, carry):
            col = 2 * piece_of(row, place) + h
            for s in range(SA):
                target = place_ref[col, s]
                k = place_ref[col, SA + s]
                block = a_ref[col, pl.ds(s * BS, BS), :]
                for acc, b_ref in zip(accs, pair):
                    acc[target] += jnp.dot(
                        block, b_ref[h * BLK_DEV + k], preferred_element_type=jnp.float32
                    )
            return carry

        lax.fori_loop(0, 2, half, 0)


def open_kernel(both, alone, resumed, place_ref, a_ref, *refs):
    width = len(alone)
    outs = refs[-width:]
    refs = list(refs[:-width])

    pairs = [[refs.pop(0) for _ in range(width)] for _ in both]
    singles = [[refs.pop(0) for _ in places] for places in alone]

    def load(i, carry):
        for c in range(width):
            outs[c][i] = refs[c][i] if resumed else jnp.zeros((BS, BS), jnp.float32)
        return carry

    lax.fori_loop(0, RB_DEV, load, 0)
    add_both(place_ref, a_ref, both, outs, pairs)
    for c in range(width):
        add_products(place_ref, a_ref, alone[c], outs[c], singles[c])


def close_kernel(places, place_ref, a_ref, *refs):
    count = len(places)
    before_ref, own_ref = refs[count : count + 2]
    msg_refs = refs[count + 2 : -2]
    acc, top = refs[-2:]
    layer = lax.axis_index("layer")

    def load(i, carry):
        acc[i] = before_ref[i]
        return carry

    lax.fori_loop(0, RB_DEV, load, 0)
    add_products(place_ref, a_ref, places, acc, refs[:count])

    def keep(i, carry):
        own_ref[i] = acc[i, pl.ds(layer * XQ, XQ), :]
        for q in range(1, N_LAYER):
            start = lax.rem(layer + q, N_LAYER) * XQ
            part = acc[i, pl.ds(start, XQ), :]
            top[q - 1, pl.ds(i, 1), :] = jnp.max(jnp.abs(part), axis=0, keepdims=True)
        return carry

    lax.fori_loop(0, RB_DEV, keep, 0)
    for q in range(1, N_LAYER):
        power = jnp.floor(jnp.log(jnp.maximum(top[q - 1], 1e-30)) * (1.0 / LN2))
        msg_refs[q - 1][pl.ds(RB_DEV * XQ, RB_DEV), :] = power.astype(jnp.int32).astype(jnp.int16)
        top[q - 1] = jnp.exp((BITS - power) * LN2)

    def pack(i, carry):
        for q in range(1, N_LAYER):
            start = lax.rem(layer + q, N_LAYER) * XQ
            part = acc[i, pl.ds(start, XQ), :] * top[q - 1, pl.ds(i, 1), :]
            msg_refs[q - 1][pl.ds(pl.multiple_of(i * XQ, XQ), XQ), :] = (
                jnp.round(part).astype(jnp.int32).astype(jnp.int16)
            )
        return carry

    lax.fori_loop(0, RB_DEV, pack, 0)


def positions_kernel(a_ref, place_ref, held, place, sem):
    copy = pltpu.make_async_copy(a_ref.at[:, pl.ds(A_ROWS, POS_ROWS)], held, sem)
    copy.start()
    copy.wait()
    for col in range(N_COL):
        place[pl.ds(col, 1), :] = held[col].astype(jnp.float32)[:1].astype(jnp.int32)
    copy = pltpu.make_async_copy(place, place_ref, sem)
    copy.start()
    copy.wait()


def positions(a_all):
    shape = (N_COL, BS)
    return pl.pallas_call(
        positions_kernel,
        out_shape=jax.ShapeDtypeStruct(shape, jnp.int32),
        in_specs=[pl.BlockSpec(memory_space=pl.ANY)],
        out_specs=pl.BlockSpec(memory_space=pltpu.SMEM),
        scratch_shapes=[
            pltpu.VMEM((N_COL, POS_ROWS, BS), jnp.bfloat16),
            pltpu.VMEM(shape, jnp.int32),
            pltpu.SemaphoreType.DMA(()),
        ],
        compiler_params=pltpu.CompilerParams(vmem_limit_bytes=50 * 2**20),
        cost_estimate=pl.CostEstimate(flops=5 * 10**9, bytes_accessed=2**20, transcendentals=0),
        name="positions",
    )(a_all)


def call_products(kernel, name, out_shape, scratch, operands, flops):
    smem = pl.BlockSpec(memory_space=pltpu.SMEM)
    vmem = pl.BlockSpec(memory_space=pltpu.VMEM)
    return pl.pallas_call(
        kernel,
        out_shape=out_shape,
        in_specs=[smem] + [vmem] * (len(operands) - 1),
        out_specs=[vmem] * len(out_shape),
        scratch_shapes=scratch,
        compiler_params=pltpu.CompilerParams(vmem_limit_bytes=6 * 2**20),
        cost_estimate=pl.CostEstimate(flops=flops, bytes_accessed=2**20, transcendentals=0),
        name=name,
    )(*operands)


def open_sums(where, chunks, both, alone, before=()):
    sums = jax.ShapeDtypeStruct((RB_DEV + 1, BS, BS), jnp.float32)
    blocks = [chunk[place] for place in both for chunk in chunks]
    blocks += [chunk[place] for chunk, places in zip(chunks, alone) for place in places]
    return call_products(
        functools.partial(open_kernel, both, alone, bool(before)),
        "open_sums",
        [sums] * len(chunks),
        [],
        [*where, *blocks, *before],
        5 * 10**9,
    )


def close_sums(where, chunk, places, before, flops):
    return call_products(
        functools.partial(close_kernel, places),
        "close_sums",
        [jax.ShapeDtypeStruct((RB_DEV, XQ, BS), jnp.float32)]
        + [jax.ShapeDtypeStruct((MSG_ROWS, BS), jnp.int16)] * (N_LAYER - 1),
        [
            pltpu.VMEM((RB_DEV + 1, BS, BS), jnp.float32),
            pltpu.VMEM((N_LAYER - 1, RB_DEV, BS), jnp.float32),
        ],
        [*where, *(chunk[place] for place in places), before],
        flops,
    )


def add_messages(own_ref, msgs, scale, i):
    total = own_ref[i]
    for q in range(N_LAYER - 1):
        part = msgs[q][pl.ds(pl.multiple_of(i * XQ, XQ), XQ), :]
        total = total + part.astype(jnp.int32).astype(jnp.float32) * scale[q, pl.ds(i, 1), :]
    return total


def load_scales(msgs, scale):
    for q in range(N_LAYER - 1):
        power = msgs[q][pl.ds(RB_DEV * XQ, RB_DEV), :].astype(jnp.int32).astype(jnp.float32)
        scale[q] = jnp.exp((power - BITS) * LN2)


def first_combine_kernel(own_ref, *refs):
    msgs, (out_ref, scale) = refs[: N_LAYER - 1], refs[N_LAYER - 1 :]
    load_scales(msgs, scale)

    def step(i, carry):
        out_ref[i] = add_messages(own_ref, msgs, scale, i)
        return carry

    lax.fori_loop(0, RB_DEV, step, 0)


def last_combine_kernel(first_ref, own_ref, *refs):
    msgs, (out_ref, scale) = refs[: N_LAYER - 1], refs[N_LAYER - 1 :]
    load_scales(msgs, scale)

    def step(i, carry):
        out_ref[pl.ds(CB_DEV * i, XQ, stride=RB_DEV * CB_DEV), :] = first_ref[i]
        out_ref[pl.ds(CB_DEV * i + 1, XQ, stride=RB_DEV * CB_DEV), :] = add_messages(own_ref, msgs, scale, i)
        return carry

    lax.fori_loop(0, RB_DEV, step, 0)


def combine(kernel, shape, parts, name):
    vmem = pl.BlockSpec(memory_space=pltpu.VMEM)
    return pl.pallas_call(
        kernel,
        out_shape=jax.ShapeDtypeStruct(shape, jnp.float32),
        in_specs=[vmem] * len(parts),
        out_specs=vmem,
        scratch_shapes=[pltpu.VMEM((N_LAYER - 1, RB_DEV, BS), jnp.float32)],
        compiler_params=pltpu.CompilerParams(vmem_limit_bytes=6 * 2**20),
        cost_estimate=pl.CostEstimate(flops=10**9, bytes_accessed=2**20, transcendentals=0),
        name=name,
    )(*parts)


def prepare_kernel(
    a_ref, rows_ref, ks_ref, live_ref, b_ref, cols_ref, a_out, zero_out, one_out, a_in, b_in, zero_in, one_in, sems
):
    load_b = pltpu.make_async_copy(b_ref, b_in, sems.at[0])
    load_a = pltpu.make_async_copy(a_ref, a_in.at[pl.ds(0, A_ROWS)], sems.at[1])
    load_b.start()
    load_a.start()
    lane = lax.broadcasted_iota(jnp.int32, (POS_ROWS, BS), 1)
    found = jnp.zeros((POS_ROWS, BS), jnp.int32)
    for s in range(SA):
        target = jnp.where(s < live_ref[0, 0, 0], rows_ref[s], RB_DEV)
        found = jnp.where(lane == s, target, found)
        found = jnp.where(lane == SA + s, ks_ref[s], found)
    a_in[pl.ds(A_ROWS, POS_ROWS), :] = found.astype(jnp.float32).astype(jnp.bfloat16)
    stores = [
        pltpu.make_async_copy(held, out, sems.at[2 + at])
        for at, (held, out) in enumerate(((zero_in, zero_out), (one_in, one_out), (a_in, a_out)))
    ]
    load_b.wait()
    for n in range(K_DEV):
        zero_in[n] = b_in[n, cols_ref[0, n]]
    stores[0].start()
    load_a.wait()
    stores[2].start()
    for n in range(K_DEV):
        one_in[n] = b_in[n, 1 - cols_ref[0, n]]
    stores[1].start()
    for store in stores:
        store.wait()


def prepare(a_vals, a_rows, a_ks, a_live, b_vals, b_cols):
    smem = pl.BlockSpec(memory_space=pltpu.SMEM)
    any_spec = pl.BlockSpec(memory_space=pl.ANY)
    a_send = jax.ShapeDtypeStruct((A_ROWS + POS_ROWS, BS), jnp.bfloat16)
    chunk = jax.ShapeDtypeStruct((K_DEV, BS, BS), jnp.bfloat16)
    return pl.pallas_call(
        prepare_kernel,
        out_shape=[a_send, chunk, chunk],
        in_specs=[any_spec, smem, smem, smem, any_spec, smem],
        out_specs=[any_spec] * 3,
        scratch_shapes=[
            pltpu.VMEM(a_send.shape, a_send.dtype),
            pltpu.VMEM((K_DEV, PB, BS, BS), jnp.bfloat16),
            pltpu.VMEM(chunk.shape, chunk.dtype),
            pltpu.VMEM(chunk.shape, chunk.dtype),
            pltpu.SemaphoreType.DMA((5,)),
        ],
        compiler_params=pltpu.CompilerParams(vmem_limit_bytes=60 * 2**20),
        name="prepare",
    )(
        a_vals.reshape(A_ROWS, BS),
        a_rows.reshape(SA),
        a_ks.reshape(SA),
        a_live,
        b_vals.reshape(K_DEV, PB, BS, BS),
        jnp.transpose(b_cols, (1, 2, 0)).reshape(PB, K_DEV),
    )


def shifted(value, axis, size, by):
    return lax.ppermute(value, axis, [(i, (i + by) % size) for i in range(size)])


def up(value):
    return shifted(value, "row", N_ROW, 1)


def down(value):
    return shifted(value, "row", N_ROW, -1)


def around(b_zero, b_one, hold, early, middle):
    zero, one = {0: b_zero}, {0: b_one}
    zero[7], one[1] = up(zero[0]), down(one[0])
    one[7], zero[1] = up(one[0]), down(zero[0])
    zero[7], one[1] = lax.optimization_barrier((zero[7], one[1]))
    zero[6], one[2] = up(zero[7]), down(one[1])
    zero[1], one[7] = lax.optimization_barrier((zero[1], one[7]))
    one[6], zero[2] = up(one[7]), down(zero[1])
    zero[6], one[2] = lax.optimization_barrier((zero[6], one[2]))
    zero[5], one[3] = up(zero[6]), down(one[2])
    one[6], zero[2] = hold(one[6], zero[2])
    zero[3] = down(zero[2])
    sums = early(zero, one)
    zero[5], *sums = lax.optimization_barrier((zero[5], *sums))
    zero[4] = up(zero[5])
    sums = middle(zero, one, sums)
    one[3], one[6], *sums = lax.optimization_barrier((one[3], one[6], *sums))
    one[4], one[5] = down(one[3]), up(one[6])
    return zero, one, sums


def send_sums(parts):
    own, msgs = parts[0], parts[1:]
    sent = {q: shifted(msgs[q - 1], "layer", N_LAYER, q) for q in (2, 1, 3)}
    return [own, *sent.values()]


def body(a_vals, a_rows, a_ks, a_live, b_vals, b_cols):
    a_send, b_zero, b_one = prepare(a_vals, a_rows, a_ks, a_live, b_vals, b_cols)
    a_all = lax.all_gather(a_send, "col", axis=0)
    where = [positions(a_all), a_all]

    def hold(*behind):
        *behind, where[0] = lax.optimization_barrier((*behind, where[0]))
        return behind

    def early(zero, one):
        return open_sums(where, (zero, one), (7, 1), ((), ()))

    def middle(zero, one, sums):
        return open_sums(where, (zero, one), (6, 2, 0), ((5,), (3,)), sums)

    zero, one, sums = around(b_zero, b_one, hold, early, middle)
    before = open_sums(where, (zero,), (), ((3,),), sums[:1])
    parts = send_sums(close_sums(where, zero, (4,), before[0], 2 * 10**10))
    first = combine(first_combine_kernel, (RB_DEV, XQ, BS), parts, "first_combine")
    parts = send_sums(close_sums(where, one, (4, 5), sums[1], 10**11))
    rows = XQ * RB_DEV * CB_DEV
    product = combine(last_combine_kernel, (rows, BS), [first] + parts, "last_combine")
    return product.reshape(XQ, RB_DEV, CB_DEV, BS)


def solution(mesh):
    return jax.shard_map(
        body,
        mesh=mesh,
        in_specs=(
            P("layer", "row", "col", None, None, None),
            P("layer", "row", "col", None),
            P("layer", "row", "col", None),
            P("layer", "row", "col"),
            P(("layer", "row"), "col", None, None, None),
            P(("layer", "row"), "col", None),
        ),
        out_specs=P("layer", "row", "col", None),
        check_vma=False,
    )
```

```python
import functools

import jax
import jax.numpy as jnp
from jax import lax
from jax.experimental import pallas as pl
from jax.experimental.pallas import tpu as pltpu
from jax.sharding import PartitionSpec as P

BS = 128
BLK_DEV = 8
SA = 12
PB = 2
RB_DEV = 32
CB_DEV = 2
N_LAYER = 4
N_ROW = 8
N_COL = 16
K_DEV = 16
XQ = BS // N_LAYER
A_ROWS = SA * BS
POS_ROWS = 16
MSG_ROWS = RB_DEV * XQ + RB_DEV
BITS = 13.0
LN2 = 0.6931471805599453


def piece_of(me, place):
    return lax.rem(me + place, N_ROW)


def add_products(place_ref, a_ref, places, acc, b_refs):
    row = lax.axis_index("row")
    for place, b_ref in zip(places, b_refs):

        def half(h, carry):
            col = 2 * piece_of(row, place) + h
            for s in range(SA):
                target = place_ref[col, s]
                k = place_ref[col, SA + s]
                acc[target] += jnp.dot(
                    a_ref[col, pl.ds(s * BS, BS), :],
                    b_ref[h * BLK_DEV + k],
                    preferred_element_type=jnp.float32,
                )
            return carry

        lax.fori_loop(0, 2, half, 0)


def add_both(place_ref, a_ref, places, accs, b_refs):
    row = lax.axis_index("row")
    for place, pair in zip(places, b_refs):

        def half(h, carry):
            col = 2 * piece_of(row, place) + h
            for s in range(SA):
                target = place_ref[col, s]
                k = place_ref[col, SA + s]
                block = a_ref[col, pl.ds(s * BS, BS), :]
                for acc, b_ref in zip(accs, pair):
                    acc[target] += jnp.dot(
                        block, b_ref[h * BLK_DEV + k], preferred_element_type=jnp.float32
                    )
            return carry

        lax.fori_loop(0, 2, half, 0)


def open_kernel(both, alone, resumed, place_ref, a_ref, *refs):
    width = len(alone)
    outs = refs[-width:]
    refs = list(refs[:-width])

    pairs = [[refs.pop(0) for _ in range(width)] for _ in both]
    singles = [[refs.pop(0) for _ in places] for places in alone]

    def load(i, carry):
        for c in range(width):
            outs[c][i] = refs[c][i] if resumed else jnp.zeros((BS, BS), jnp.float32)
        return carry

    lax.fori_loop(0, RB_DEV, load, 0)
    add_both(place_ref, a_ref, both, outs, pairs)
    for c in range(width):
        add_products(place_ref, a_ref, alone[c], outs[c], singles[c])


def close_kernel(places, place_ref, a_ref, *refs):
    count = len(places)
    before_ref, own_ref = refs[count : count + 2]
    msg_refs = refs[count + 2 : -2]
    acc, top = refs[-2:]
    layer = lax.axis_index("layer")

    def load(i, carry):
        acc[i] = before_ref[i]
        return carry

    lax.fori_loop(0, RB_DEV, load, 0)
    add_products(place_ref, a_ref, places, acc, refs[:count])

    def keep(i, carry):
        own_ref[i] = acc[i, pl.ds(layer * XQ, XQ), :]
        for q in range(1, N_LAYER):
            start = lax.rem(layer + q, N_LAYER) * XQ
            part = acc[i, pl.ds(start, XQ), :]
            top[q - 1, pl.ds(i, 1), :] = jnp.max(jnp.abs(part), axis=0, keepdims=True)
        return carry

    lax.fori_loop(0, RB_DEV, keep, 0)
    for q in range(1, N_LAYER):
        power = jnp.floor(jnp.log(jnp.maximum(top[q - 1], 1e-30)) * (1.0 / LN2))
        msg_refs[q - 1][pl.ds(RB_DEV * XQ, RB_DEV), :] = power.astype(jnp.int32).astype(jnp.int16)
        top[q - 1] = jnp.exp((BITS - power) * LN2)

    def pack(i, carry):
        for q in range(1, N_LAYER):
            start = lax.rem(layer + q, N_LAYER) * XQ
            part = acc[i, pl.ds(start, XQ), :] * top[q - 1, pl.ds(i, 1), :]
            msg_refs[q - 1][pl.ds(pl.multiple_of(i * XQ, XQ), XQ), :] = (
                jnp.round(part).astype(jnp.int32).astype(jnp.int16)
            )
        return carry

    lax.fori_loop(0, RB_DEV, pack, 0)


def positions_kernel(a_ref, place_ref, held, place, sem):
    copy = pltpu.make_async_copy(a_ref.at[:, pl.ds(A_ROWS, POS_ROWS)], held, sem)
    copy.start()
    copy.wait()
    for col in range(N_COL):
        place[pl.ds(col, 1), :] = held[col].astype(jnp.float32)[:1].astype(jnp.int32)
    copy = pltpu.make_async_copy(place, place_ref, sem)
    copy.start()
    copy.wait()


def positions(a_all):
    shape = (N_COL, BS)
    return pl.pallas_call(
        positions_kernel,
        out_shape=jax.ShapeDtypeStruct(shape, jnp.int32),
        in_specs=[pl.BlockSpec(memory_space=pl.ANY)],
        out_specs=pl.BlockSpec(memory_space=pltpu.SMEM),
        scratch_shapes=[
            pltpu.VMEM((N_COL, POS_ROWS, BS), jnp.bfloat16),
            pltpu.VMEM(shape, jnp.int32),
            pltpu.SemaphoreType.DMA(()),
        ],
        compiler_params=pltpu.CompilerParams(vmem_limit_bytes=50 * 2**20),
        cost_estimate=pl.CostEstimate(flops=5 * 10**9, bytes_accessed=2**20, transcendentals=0),
        name="positions",
    )(a_all)


def call_products(kernel, name, out_shape, scratch, operands, flops):
    smem = pl.BlockSpec(memory_space=pltpu.SMEM)
    vmem = pl.BlockSpec(memory_space=pltpu.VMEM)
    return pl.pallas_call(
        kernel,
        out_shape=out_shape,
        in_specs=[smem] + [vmem] * (len(operands) - 1),
        out_specs=[vmem] * len(out_shape),
        scratch_shapes=scratch,
        compiler_params=pltpu.CompilerParams(vmem_limit_bytes=6 * 2**20),
        cost_estimate=pl.CostEstimate(flops=flops, bytes_accessed=2**20, transcendentals=0),
        name=name,
    )(*operands)


def open_sums(where, chunks, both, alone, before=()):
    sums = jax.ShapeDtypeStruct((RB_DEV + 1, BS, BS), jnp.float32)
    blocks = [chunk[place] for place in both for chunk in chunks]
    blocks += [chunk[place] for chunk, places in zip(chunks, alone) for place in places]
    return call_products(
        functools.partial(open_kernel, both, alone, bool(before)),
        "open_sums",
        [sums] * len(chunks),
        [],
        [*where, *blocks, *before],
        5 * 10**9,
    )


def close_sums(where, chunk, places, before, flops):
    return call_products(
        functools.partial(close_kernel, places),
        "close_sums",
        [jax.ShapeDtypeStruct((RB_DEV, XQ, BS), jnp.float32)]
        + [jax.ShapeDtypeStruct((MSG_ROWS, BS), jnp.int16)] * (N_LAYER - 1),
        [
            pltpu.VMEM((RB_DEV + 1, BS, BS), jnp.float32),
            pltpu.VMEM((N_LAYER - 1, RB_DEV, BS), jnp.float32),
        ],
        [*where, *(chunk[place] for place in places), before],
        flops,
    )


def add_messages(own_ref, msgs, scale, i):
    total = own_ref[i]
    for q in range(N_LAYER - 1):
        part = msgs[q][pl.ds(pl.multiple_of(i * XQ, XQ), XQ), :]
        total = total + part.astype(jnp.int32).astype(jnp.float32) * scale[q, pl.ds(i, 1), :]
    return total


def load_scales(msgs, scale):
    for q in range(N_LAYER - 1):
        power = msgs[q][pl.ds(RB_DEV * XQ, RB_DEV), :].astype(jnp.int32).astype(jnp.float32)
        scale[q] = jnp.exp((power - BITS) * LN2)


def first_combine_kernel(own_ref, *refs):
    msgs, (out_ref, scale) = refs[: N_LAYER - 1], refs[N_LAYER - 1 :]
    load_scales(msgs, scale)

    def step(i, carry):
        out_ref[i] = add_messages(own_ref, msgs, scale, i)
        return carry

    lax.fori_loop(0, RB_DEV, step, 0)


def last_combine_kernel(first_ref, own_ref, *refs):
    msgs, (out_ref, scale) = refs[: N_LAYER - 1], refs[N_LAYER - 1 :]
    load_scales(msgs, scale)

    def step(i, carry):
        out_ref[pl.ds(CB_DEV * i, XQ, stride=RB_DEV * CB_DEV), :] = first_ref[i]
        out_ref[pl.ds(CB_DEV * i + 1, XQ, stride=RB_DEV * CB_DEV), :] = add_messages(own_ref, msgs, scale, i)
        return carry

    lax.fori_loop(0, RB_DEV, step, 0)


def combine(kernel, shape, parts, name):
    vmem = pl.BlockSpec(memory_space=pltpu.VMEM)
    return pl.pallas_call(
        kernel,
        out_shape=jax.ShapeDtypeStruct(shape, jnp.float32),
        in_specs=[vmem] * len(parts),
        out_specs=vmem,
        scratch_shapes=[pltpu.VMEM((N_LAYER - 1, RB_DEV, BS), jnp.float32)],
        compiler_params=pltpu.CompilerParams(vmem_limit_bytes=6 * 2**20),
        cost_estimate=pl.CostEstimate(flops=10**9, bytes_accessed=2**20, transcendentals=0),
        name=name,
    )(*parts)


def prepare_kernel(
    a_ref, rows_ref, ks_ref, live_ref, b_ref, cols_ref, a_out, zero_out, one_out, a_in, b_in, zero_in, one_in, sems
):
    load_b = pltpu.make_async_copy(b_ref, b_in, sems.at[0])
    load_a = pltpu.make_async_copy(a_ref, a_in.at[pl.ds(0, A_ROWS)], sems.at[1])
    load_b.start()
    load_a.start()
    lane = lax.broadcasted_iota(jnp.int32, (POS_ROWS, BS), 1)
    found = jnp.zeros((POS_ROWS, BS), jnp.int32)
    for s in range(SA):
        target = jnp.where(s < live_ref[0, 0, 0], rows_ref[s], RB_DEV)
        found = jnp.where(lane == s, target, found)
        found = jnp.where(lane == SA + s, ks_ref[s], found)
    a_in[pl.ds(A_ROWS, POS_ROWS), :] = found.astype(jnp.float32).astype(jnp.bfloat16)
    stores = [
        pltpu.make_async_copy(held, out, sems.at[2 + at])
        for at, (held, out) in enumerate(((zero_in, zero_out), (one_in, one_out), (a_in, a_out)))
    ]
    load_b.wait()
    for n in range(K_DEV):
        zero_in[n] = b_in[n, cols_ref[0, n]]
    stores[0].start()
    load_a.wait()
    stores[2].start()
    for n in range(K_DEV):
        one_in[n] = b_in[n, 1 - cols_ref[0, n]]
    stores[1].start()
    for store in stores:
        store.wait()


def prepare(a_vals, a_rows, a_ks, a_live, b_vals, b_cols):
    smem = pl.BlockSpec(memory_space=pltpu.SMEM)
    any_spec = pl.BlockSpec(memory_space=pl.ANY)
    a_send = jax.ShapeDtypeStruct((A_ROWS + POS_ROWS, BS), jnp.bfloat16)
    chunk = jax.ShapeDtypeStruct((K_DEV, BS, BS), jnp.bfloat16)
    return pl.pallas_call(
        prepare_kernel,
        out_shape=[a_send, chunk, chunk],
        in_specs=[any_spec, smem, smem, smem, any_spec, smem],
        out_specs=[any_spec] * 3,
        scratch_shapes=[
            pltpu.VMEM(a_send.shape, a_send.dtype),
            pltpu.VMEM((K_DEV, PB, BS, BS), jnp.bfloat16),
            pltpu.VMEM(chunk.shape, chunk.dtype),
            pltpu.VMEM(chunk.shape, chunk.dtype),
            pltpu.SemaphoreType.DMA((5,)),
        ],
        compiler_params=pltpu.CompilerParams(vmem_limit_bytes=60 * 2**20),
        name="prepare",
    )(
        a_vals.reshape(A_ROWS, BS),
        a_rows.reshape(SA),
        a_ks.reshape(SA),
        a_live,
        b_vals.reshape(K_DEV, PB, BS, BS),
        jnp.transpose(b_cols, (1, 2, 0)).reshape(PB, K_DEV),
    )


def shifted(value, axis, size, by):
    return lax.ppermute(value, axis, [(i, (i + by) % size) for i in range(size)])


def up(value):
    return shifted(value, "row", N_ROW, 1)


def down(value):
    return shifted(value, "row", N_ROW, -1)


def around(b_zero, b_one, hold, early, middle):
    zero, one = {0: b_zero}, {0: b_one}
    zero[7], one[1] = up(zero[0]), down(one[0])
    one[7], zero[1] = up(one[0]), down(zero[0])
    zero[6], one[2] = up(zero[7]), down(one[1])
    one[6], zero[2] = up(one[7]), down(zero[1])
    zero[5], one[3] = up(zero[6]), down(one[2])
    (zero[2],) = hold(zero[2])
    zero[3] = down(zero[2])
    sums = early(zero, one)
    zero[5], *sums = lax.optimization_barrier((zero[5], *sums))
    zero[4] = up(zero[5])
    sums = middle(zero, one, sums)
    one[3], one[6], *sums = lax.optimization_barrier((one[3], one[6], *sums))
    one[4], one[5] = down(one[3]), up(one[6])
    return zero, one, sums


def send_sums(parts):
    own, msgs = parts[0], parts[1:]
    sent = {q: shifted(msgs[q - 1], "layer", N_LAYER, q) for q in (2, 1, 3)}
    return [own, *sent.values()]


def body(a_vals, a_rows, a_ks, a_live, b_vals, b_cols):
    a_send, b_zero, b_one = prepare(a_vals, a_rows, a_ks, a_live, b_vals, b_cols)
    a_all = lax.all_gather(a_send, "col", axis=0)
    where = [positions(a_all), a_all]

    def hold(*behind):
        *behind, where[0] = lax.optimization_barrier((*behind, where[0]))
        return behind

    def early(zero, one):
        return open_sums(where, (zero, one), (7, 1), ((), ()))

    def middle(zero, one, sums):
        return open_sums(where, (zero, one), (6, 2, 0), ((5,), (3,)), sums)

    zero, one, sums = around(b_zero, b_one, hold, early, middle)
    before = open_sums(where, (zero,), (), ((3,),), sums[:1])
    parts = send_sums(close_sums(where, zero, (4,), before[0], 2 * 10**10))
    first = combine(first_combine_kernel, (RB_DEV, XQ, BS), parts, "first_combine")
    parts = send_sums(close_sums(where, one, (4, 5), sums[1], 10**11))
    rows = XQ * RB_DEV * CB_DEV
    product = combine(last_combine_kernel, (rows, BS), [first] + parts, "last_combine")
    return product.reshape(XQ, RB_DEV, CB_DEV, BS)


def solution(mesh):
    return jax.shard_map(
        body,
        mesh=mesh,
        in_specs=(
            P("layer", "row", "col", None, None, None),
            P("layer", "row", "col", None),
            P("layer", "row", "col", None),
            P("layer", "row", "col"),
            P(("layer", "row"), "col", None, None, None),
            P(("layer", "row"), "col", None),
        ),
        out_specs=P("layer", "row", "col", None),
        check_vma=False,
    )
```

```python
import functools

import jax
import jax.numpy as jnp
from jax import lax
from jax.experimental import pallas as pl
from jax.experimental.pallas import tpu as pltpu
from jax.sharding import PartitionSpec as P

BS = 128
BLK_DEV = 8
SA = 12
PB = 2
RB_DEV = 32
CB_DEV = 2
N_LAYER = 4
N_ROW = 8
N_COL = 16
K_DEV = 16
XQ = BS // N_LAYER
A_ROWS = SA * BS
POS_ROWS = 16
MSG_ROWS = RB_DEV * XQ + RB_DEV
BITS = 13.0
LN2 = 0.6931471805599453


def piece_of(me, place):
    return lax.rem(me + place, N_ROW)


def add_products(place_ref, a_ref, places, acc, b_refs):
    row = lax.axis_index("row")
    for place, b_ref in zip(places, b_refs):

        def half(h, carry):
            col = 2 * piece_of(row, place) + h
            for s in range(SA):
                target = place_ref[col, s]
                k = place_ref[col, SA + s]
                acc[target] += jnp.dot(
                    a_ref[col, pl.ds(s * BS, BS), :],
                    b_ref[h * BLK_DEV + k],
                    preferred_element_type=jnp.float32,
                )
            return carry

        lax.fori_loop(0, 2, half, 0)


def add_both(place_ref, a_ref, places, accs, b_refs):
    row = lax.axis_index("row")
    for place, pair in zip(places, b_refs):

        def half(h, carry):
            col = 2 * piece_of(row, place) + h
            for s in range(SA):
                target = place_ref[col, s]
                k = place_ref[col, SA + s]
                block = a_ref[col, pl.ds(s * BS, BS), :]
                for acc, b_ref in zip(accs, pair):
                    acc[target] += jnp.dot(
                        block, b_ref[h * BLK_DEV + k], preferred_element_type=jnp.float32
                    )
            return carry

        lax.fori_loop(0, 2, half, 0)


def open_kernel(both, alone, resumed, place_ref, a_ref, *refs):
    width = len(alone)
    outs = refs[-width:]
    refs = list(refs[:-width])

    pairs = [[refs.pop(0) for _ in range(width)] for _ in both]
    singles = [[refs.pop(0) for _ in places] for places in alone]

    def load(i, carry):
        for c in range(width):
            outs[c][i] = refs[c][i] if resumed else jnp.zeros((BS, BS), jnp.float32)
        return carry

    lax.fori_loop(0, RB_DEV, load, 0)
    add_both(place_ref, a_ref, both, outs, pairs)
    for c in range(width):
        add_products(place_ref, a_ref, alone[c], outs[c], singles[c])


def close_kernel(places, place_ref, a_ref, *refs):
    count = len(places)
    before_ref, own_ref = refs[count : count + 2]
    msg_refs = refs[count + 2 : -2]
    acc, top = refs[-2:]
    layer = lax.axis_index("layer")

    def load(i, carry):
        acc[i] = before_ref[i]
        return carry

    lax.fori_loop(0, RB_DEV, load, 0)
    add_products(place_ref, a_ref, places, acc, refs[:count])

    def keep(i, carry):
        own_ref[i] = acc[i, pl.ds(layer * XQ, XQ), :]
        for q in range(1, N_LAYER):
            start = lax.rem(layer + q, N_LAYER) * XQ
            part = acc[i, pl.ds(start, XQ), :]
            top[q - 1, pl.ds(i, 1), :] = jnp.max(jnp.abs(part), axis=0, keepdims=True)
        return carry

    lax.fori_loop(0, RB_DEV, keep, 0)
    for q in range(1, N_LAYER):
        power = jnp.floor(jnp.log(jnp.maximum(top[q - 1], 1e-30)) * (1.0 / LN2))
        msg_refs[q - 1][pl.ds(RB_DEV * XQ, RB_DEV), :] = power.astype(jnp.int32).astype(jnp.int16)
        top[q - 1] = jnp.exp((BITS - power) * LN2)

    def pack(i, carry):
        for q in range(1, N_LAYER):
            start = lax.rem(layer + q, N_LAYER) * XQ
            part = acc[i, pl.ds(start, XQ), :] * top[q - 1, pl.ds(i, 1), :]
            msg_refs[q - 1][pl.ds(pl.multiple_of(i * XQ, XQ), XQ), :] = (
                jnp.round(part).astype(jnp.int32).astype(jnp.int16)
            )
        return carry

    lax.fori_loop(0, RB_DEV, pack, 0)


def positions_kernel(a_ref, place_ref, held, place, sem):
    copy = pltpu.make_async_copy(a_ref.at[:, pl.ds(A_ROWS, POS_ROWS)], held, sem)
    copy.start()
    copy.wait()
    for col in range(N_COL):
        place[pl.ds(col, 1), :] = held[col].astype(jnp.float32)[:1].astype(jnp.int32)
    copy = pltpu.make_async_copy(place, place_ref, sem)
    copy.start()
    copy.wait()


def positions(a_all):
    shape = (N_COL, BS)
    return pl.pallas_call(
        positions_kernel,
        out_shape=jax.ShapeDtypeStruct(shape, jnp.int32),
        in_specs=[pl.BlockSpec(memory_space=pl.ANY)],
        out_specs=pl.BlockSpec(memory_space=pltpu.SMEM),
        scratch_shapes=[
            pltpu.VMEM((N_COL, POS_ROWS, BS), jnp.bfloat16),
            pltpu.VMEM(shape, jnp.int32),
            pltpu.SemaphoreType.DMA(()),
        ],
        compiler_params=pltpu.CompilerParams(vmem_limit_bytes=50 * 2**20),
        cost_estimate=pl.CostEstimate(flops=5 * 10**9, bytes_accessed=2**20, transcendentals=0),
        name="positions",
    )(a_all)


def call_products(kernel, name, out_shape, scratch, operands, flops):
    smem = pl.BlockSpec(memory_space=pltpu.SMEM)
    vmem = pl.BlockSpec(memory_space=pltpu.VMEM)
    return pl.pallas_call(
        kernel,
        out_shape=out_shape,
        in_specs=[smem] + [vmem] * (len(operands) - 1),
        out_specs=[vmem] * len(out_shape),
        scratch_shapes=scratch,
        compiler_params=pltpu.CompilerParams(vmem_limit_bytes=6 * 2**20),
        cost_estimate=pl.CostEstimate(flops=flops, bytes_accessed=2**20, transcendentals=0),
        name=name,
    )(*operands)


def open_sums(where, chunks, both, alone, before=()):
    sums = jax.ShapeDtypeStruct((RB_DEV + 1, BS, BS), jnp.float32)
    blocks = [chunk[place] for place in both for chunk in chunks]
    blocks += [chunk[place] for chunk, places in zip(chunks, alone) for place in places]
    return call_products(
        functools.partial(open_kernel, both, alone, bool(before)),
        "open_sums",
        [sums] * len(chunks),
        [],
        [*where, *blocks, *before],
        5 * 10**9,
    )


def close_sums(where, chunk, places, before, flops):
    return call_products(
        functools.partial(close_kernel, places),
        "close_sums",
        [jax.ShapeDtypeStruct((RB_DEV, XQ, BS), jnp.float32)]
        + [jax.ShapeDtypeStruct((MSG_ROWS, BS), jnp.int16)] * (N_LAYER - 1),
        [
            pltpu.VMEM((RB_DEV + 1, BS, BS), jnp.float32),
            pltpu.VMEM((N_LAYER - 1, RB_DEV, BS), jnp.float32),
        ],
        [*where, *(chunk[place] for place in places), before],
        flops,
    )


def add_messages(own_ref, msgs, scale, i):
    total = own_ref[i]
    for q in range(N_LAYER - 1):
        part = msgs[q][pl.ds(pl.multiple_of(i * XQ, XQ), XQ), :]
        total = total + part.astype(jnp.int32).astype(jnp.float32) * scale[q, pl.ds(i, 1), :]
    return total


def load_scales(msgs, scale):
    for q in range(N_LAYER - 1):
        power = msgs[q][pl.ds(RB_DEV * XQ, RB_DEV), :].astype(jnp.int32).astype(jnp.float32)
        scale[q] = jnp.exp((power - BITS) * LN2)


def first_combine_kernel(own_ref, *refs):
    msgs, (out_ref, scale) = refs[: N_LAYER - 1], refs[N_LAYER - 1 :]
    load_scales(msgs, scale)

    def step(i, carry):
        out_ref[i] = add_messages(own_ref, msgs, scale, i)
        return carry

    lax.fori_loop(0, RB_DEV, step, 0)


def last_combine_kernel(first_ref, own_ref, *refs):
    msgs, (out_ref, scale) = refs[: N_LAYER - 1], refs[N_LAYER - 1 :]
    load_scales(msgs, scale)

    def step(i, carry):
        out_ref[pl.ds(CB_DEV * i, XQ, stride=RB_DEV * CB_DEV), :] = first_ref[i]
        out_ref[pl.ds(CB_DEV * i + 1, XQ, stride=RB_DEV * CB_DEV), :] = add_messages(own_ref, msgs, scale, i)
        return carry

    lax.fori_loop(0, RB_DEV, step, 0)


def combine(kernel, shape, parts, name):
    vmem = pl.BlockSpec(memory_space=pltpu.VMEM)
    return pl.pallas_call(
        kernel,
        out_shape=jax.ShapeDtypeStruct(shape, jnp.float32),
        in_specs=[vmem] * len(parts),
        out_specs=vmem,
        scratch_shapes=[pltpu.VMEM((N_LAYER - 1, RB_DEV, BS), jnp.float32)],
        compiler_params=pltpu.CompilerParams(vmem_limit_bytes=6 * 2**20),
        cost_estimate=pl.CostEstimate(flops=10**9, bytes_accessed=2**20, transcendentals=0),
        name=name,
    )(*parts)


def prepare_kernel(
    a_ref, rows_ref, ks_ref, live_ref, b_ref, cols_ref, a_out, zero_out, one_out, a_in, b_in, zero_in, one_in, sems
):
    load_b = pltpu.make_async_copy(b_ref, b_in, sems.at[0])
    load_a = pltpu.make_async_copy(a_ref, a_in.at[pl.ds(0, A_ROWS)], sems.at[1])
    load_b.start()
    load_a.start()
    lane = lax.broadcasted_iota(jnp.int32, (POS_ROWS, BS), 1)
    found = jnp.zeros((POS_ROWS, BS), jnp.int32)
    for s in range(SA):
        target = jnp.where(s < live_ref[0, 0, 0], rows_ref[s], RB_DEV)
        found = jnp.where(lane == s, target, found)
        found = jnp.where(lane == SA + s, ks_ref[s], found)
    a_in[pl.ds(A_ROWS, POS_ROWS), :] = found.astype(jnp.float32).astype(jnp.bfloat16)
    stores = [
        pltpu.make_async_copy(held, out, sems.at[2 + at])
        for at, (held, out) in enumerate(((zero_in, zero_out), (one_in, one_out), (a_in, a_out)))
    ]
    load_b.wait()
    for n in range(K_DEV):
        zero_in[n] = b_in[n, cols_ref[0, n]]
    stores[0].start()
    load_a.wait()
    stores[2].start()
    for n in range(K_DEV):
        one_in[n] = b_in[n, 1 - cols_ref[0, n]]
    stores[1].start()
    for store in stores:
        store.wait()


def prepare(a_vals, a_rows, a_ks, a_live, b_vals, b_cols):
    smem = pl.BlockSpec(memory_space=pltpu.SMEM)
    any_spec = pl.BlockSpec(memory_space=pl.ANY)
    a_send = jax.ShapeDtypeStruct((A_ROWS + POS_ROWS, BS), jnp.bfloat16)
    chunk = jax.ShapeDtypeStruct((K_DEV, BS, BS), jnp.bfloat16)
    return pl.pallas_call(
        prepare_kernel,
        out_shape=[a_send, chunk, chunk],
        in_specs=[any_spec, smem, smem, smem, any_spec, smem],
        out_specs=[any_spec] * 3,
        scratch_shapes=[
            pltpu.VMEM(a_send.shape, a_send.dtype),
            pltpu.VMEM((K_DEV, PB, BS, BS), jnp.bfloat16),
            pltpu.VMEM(chunk.shape, chunk.dtype),
            pltpu.VMEM(chunk.shape, chunk.dtype),
            pltpu.SemaphoreType.DMA((5,)),
        ],
        compiler_params=pltpu.CompilerParams(vmem_limit_bytes=60 * 2**20),
        name="prepare",
    )(
        a_vals.reshape(A_ROWS, BS),
        a_rows.reshape(SA),
        a_ks.reshape(SA),
        a_live,
        b_vals.reshape(K_DEV, PB, BS, BS),
        jnp.transpose(b_cols, (1, 2, 0)).reshape(PB, K_DEV),
    )


def shifted(value, axis, size, by):
    return lax.ppermute(value, axis, [(i, (i + by) % size) for i in range(size)])


def up(value):
    return shifted(value, "row", N_ROW, 1)


def down(value):
    return shifted(value, "row", N_ROW, -1)


def around(b_zero, b_one, hold, early, middle):
    zero, one = {0: b_zero}, {0: b_one}
    zero[7], one[1] = up(zero[0]), down(one[0])
    one[7], zero[1] = up(one[0]), down(zero[0])
    zero[6], one[2] = up(zero[7]), down(one[1])
    one[6], zero[2] = up(one[7]), down(zero[1])
    zero[5], one[3] = up(zero[6]), down(one[2])
    one[6], zero[2] = hold(one[6], zero[2])
    zero[3] = down(zero[2])
    sums = early(zero, one)
    zero[5], *sums = lax.optimization_barrier((zero[5], *sums))
    zero[4] = up(zero[5])
    sums = middle(zero, one, sums)
    one[3], one[6], *sums = lax.optimization_barrier((one[3], one[6], *sums))
    one[4], one[5] = down(one[3]), up(one[6])
    return zero, one, sums


def send_sums(parts):
    own, msgs = parts[0], parts[1:]
    sent = {q: shifted(msgs[q - 1], "layer", N_LAYER, q) for q in (2, 1, 3)}
    return [own, *sent.values()]


def body(a_vals, a_rows, a_ks, a_live, b_vals, b_cols):
    a_send, b_zero, b_one = prepare(a_vals, a_rows, a_ks, a_live, b_vals, b_cols)
    a_all = lax.all_gather(a_send, "col", axis=0)
    where = [positions(a_all), a_all]

    def hold(*behind):
        *behind, where[0] = lax.optimization_barrier((*behind, where[0]))
        return behind

    def early(zero, one):
        return open_sums(where, (zero, one), (7, 1), ((), ()))

    def middle(zero, one, sums):
        return open_sums(where, (zero, one), (6, 2, 0), ((5,), (3,)), sums)

    zero, one, sums = around(b_zero, b_one, hold, early, middle)
    before = open_sums(where, (zero,), (), ((3,),), sums[:1])
    parts = send_sums(close_sums(where, zero, (4,), before[0], 2 * 10**10))
    first = combine(first_combine_kernel, (RB_DEV, XQ, BS), parts, "first_combine")
    parts = send_sums(close_sums(where, one, (4, 5), sums[1], 10**11))
    rows = XQ * RB_DEV * CB_DEV
    product = combine(last_combine_kernel, (rows, BS), [first] + parts, "last_combine")
    return product.reshape(XQ, RB_DEV, CB_DEV, BS)


def solution(mesh):
    return jax.shard_map(
        body,
        mesh=mesh,
        in_specs=(
            P("layer", "row", "col", None, None, None),
            P("layer", "row", "col", None),
            P("layer", "row", "col", None),
            P("layer", "row", "col"),
            P(("layer", "row"), "col", None, None, None),
            P(("layer", "row"), "col", None),
        ),
        out_specs=P("layer", "row", "col", None),
        check_vma=False,
    )
```

```python
import functools

import jax
import jax.numpy as jnp
from jax import lax
from jax.experimental import pallas as pl
from jax.experimental.pallas import tpu as pltpu
from jax.sharding import PartitionSpec as P

BS = 128
BLK_DEV = 8
SA = 12
PB = 2
RB_DEV = 32
CB_DEV = 2
N_LAYER = 4
N_ROW = 8
N_COL = 16
K_DEV = 16
XQ = BS // N_LAYER
A_ROWS = SA * BS
POS_ROWS = 16
MSG_ROWS = RB_DEV * XQ + RB_DEV
BITS = 13.0
LN2 = 0.6931471805599453


def piece_of(me, place):
    return lax.rem(me + place, N_ROW)


def add_products(place_ref, a_ref, places, acc, b_refs):
    row = lax.axis_index("row")
    for place, b_ref in zip(places, b_refs):

        def half(h, carry):
            col = 2 * piece_of(row, place) + h
            for s in range(SA):
                target = place_ref[col, s]
                k = place_ref[col, SA + s]
                acc[target] += jnp.dot(
                    a_ref[col, pl.ds(s * BS, BS), :],
                    b_ref[h * BLK_DEV + k],
                    preferred_element_type=jnp.float32,
                )
            return carry

        lax.fori_loop(0, 2, half, 0)


def add_both(place_ref, a_ref, places, accs, b_refs):
    row = lax.axis_index("row")
    for place, pair in zip(places, b_refs):

        def half(h, carry):
            col = 2 * piece_of(row, place) + h
            for s in range(SA):
                target = place_ref[col, s]
                k = place_ref[col, SA + s]
                block = a_ref[col, pl.ds(s * BS, BS), :]
                for acc, b_ref in zip(accs, pair):
                    acc[target] += jnp.dot(
                        block, b_ref[h * BLK_DEV + k], preferred_element_type=jnp.float32
                    )
            return carry

        lax.fori_loop(0, 2, half, 0)


def open_kernel(both, alone, resumed, place_ref, a_ref, *refs):
    width = len(alone)
    outs = refs[-width:]
    refs = list(refs[:-width])

    pairs = [[refs.pop(0) for _ in range(width)] for _ in both]
    singles = [[refs.pop(0) for _ in places] for places in alone]

    def load(i, carry):
        for c in range(width):
            outs[c][i] = refs[c][i] if resumed else jnp.zeros((BS, BS), jnp.float32)
        return carry

    lax.fori_loop(0, RB_DEV, load, 0)
    add_both(place_ref, a_ref, both, outs, pairs)
    for c in range(width):
        add_products(place_ref, a_ref, alone[c], outs[c], singles[c])


def close_kernel(places, place_ref, a_ref, *refs):
    count = len(places)
    before_ref, own_ref = refs[count : count + 2]
    msg_refs = refs[count + 2 : -2]
    acc, top = refs[-2:]
    layer = lax.axis_index("layer")

    def load(i, carry):
        acc[i] = before_ref[i]
        return carry

    lax.fori_loop(0, RB_DEV, load, 0)
    add_products(place_ref, a_ref, places, acc, refs[:count])

    def keep(i, carry):
        own_ref[i] = acc[i, pl.ds(layer * XQ, XQ), :]
        for q in range(1, N_LAYER):
            start = lax.rem(layer + q, N_LAYER) * XQ
            part = acc[i, pl.ds(start, XQ), :]
            top[q - 1, pl.ds(i, 1), :] = jnp.max(jnp.abs(part), axis=0, keepdims=True)
        return carry

    lax.fori_loop(0, RB_DEV, keep, 0)
    for q in range(1, N_LAYER):
        power = jnp.floor(jnp.log(jnp.maximum(top[q - 1], 1e-30)) * (1.0 / LN2))
        msg_refs[q - 1][pl.ds(RB_DEV * XQ, RB_DEV), :] = power.astype(jnp.int32).astype(jnp.int16)
        top[q - 1] = jnp.exp((BITS - power) * LN2)

    def pack(i, carry):
        for q in range(1, N_LAYER):
            start = lax.rem(layer + q, N_LAYER) * XQ
            part = acc[i, pl.ds(start, XQ), :] * top[q - 1, pl.ds(i, 1), :]
            msg_refs[q - 1][pl.ds(pl.multiple_of(i * XQ, XQ), XQ), :] = (
                jnp.round(part).astype(jnp.int32).astype(jnp.int16)
            )
        return carry

    lax.fori_loop(0, RB_DEV, pack, 0)


def positions_kernel(a_ref, place_ref, held, place, sem):
    copy = pltpu.make_async_copy(a_ref.at[:, pl.ds(A_ROWS, POS_ROWS)], held, sem)
    copy.start()
    copy.wait()
    for col in range(N_COL):
        place[pl.ds(col, 1), :] = held[col].astype(jnp.float32)[:1].astype(jnp.int32)
    copy = pltpu.make_async_copy(place, place_ref, sem)
    copy.start()
    copy.wait()


def positions(a_all):
    shape = (N_COL, BS)
    return pl.pallas_call(
        positions_kernel,
        out_shape=jax.ShapeDtypeStruct(shape, jnp.int32),
        in_specs=[pl.BlockSpec(memory_space=pl.ANY)],
        out_specs=pl.BlockSpec(memory_space=pltpu.SMEM),
        scratch_shapes=[
            pltpu.VMEM((N_COL, POS_ROWS, BS), jnp.bfloat16),
            pltpu.VMEM(shape, jnp.int32),
            pltpu.SemaphoreType.DMA(()),
        ],
        compiler_params=pltpu.CompilerParams(vmem_limit_bytes=50 * 2**20),
        cost_estimate=pl.CostEstimate(flops=5 * 10**9, bytes_accessed=2**20, transcendentals=0),
        name="positions",
    )(a_all)


def call_products(kernel, name, out_shape, scratch, operands, flops):
    smem = pl.BlockSpec(memory_space=pltpu.SMEM)
    vmem = pl.BlockSpec(memory_space=pltpu.VMEM)
    return pl.pallas_call(
        kernel,
        out_shape=out_shape,
        in_specs=[smem] + [vmem] * (len(operands) - 1),
        out_specs=[vmem] * len(out_shape),
        scratch_shapes=scratch,
        compiler_params=pltpu.CompilerParams(vmem_limit_bytes=6 * 2**20),
        cost_estimate=pl.CostEstimate(flops=flops, bytes_accessed=2**20, transcendentals=0),
        name=name,
    )(*operands)


def open_sums(where, chunks, both, alone, before=()):
    sums = jax.ShapeDtypeStruct((RB_DEV + 1, BS, BS), jnp.float32)
    blocks = [chunk[place] for place in both for chunk in chunks]
    blocks += [chunk[place] for chunk, places in zip(chunks, alone) for place in places]
    return call_products(
        functools.partial(open_kernel, both, alone, bool(before)),
        "open_sums",
        [sums] * len(chunks),
        [],
        [*where, *blocks, *before],
        5 * 10**9,
    )


def close_sums(where, chunk, places, before, flops):
    return call_products(
        functools.partial(close_kernel, places),
        "close_sums",
        [jax.ShapeDtypeStruct((RB_DEV, XQ, BS), jnp.float32)]
        + [jax.ShapeDtypeStruct((MSG_ROWS, BS), jnp.int16)] * (N_LAYER - 1),
        [
            pltpu.VMEM((RB_DEV + 1, BS, BS), jnp.float32),
            pltpu.VMEM((N_LAYER - 1, RB_DEV, BS), jnp.float32),
        ],
        [*where, *(chunk[place] for place in places), before],
        flops,
    )


def add_messages(own_ref, msgs, scale, i):
    total = own_ref[i]
    for q in range(N_LAYER - 1):
        part = msgs[q][pl.ds(pl.multiple_of(i * XQ, XQ), XQ), :]
        total = total + part.astype(jnp.int32).astype(jnp.float32) * scale[q, pl.ds(i, 1), :]
    return total


def load_scales(msgs, scale):
    for q in range(N_LAYER - 1):
        power = msgs[q][pl.ds(RB_DEV * XQ, RB_DEV), :].astype(jnp.int32).astype(jnp.float32)
        scale[q] = jnp.exp((power - BITS) * LN2)


def first_combine_kernel(own_ref, *refs):
    msgs, (out_ref, scale) = refs[: N_LAYER - 1], refs[N_LAYER - 1 :]
    load_scales(msgs, scale)

    def step(i, carry):
        out_ref[i] = add_messages(own_ref, msgs, scale, i)
        return carry

    lax.fori_loop(0, RB_DEV, step, 0)


def last_combine_kernel(first_ref, own_ref, *refs):
    msgs, (out_ref, scale) = refs[: N_LAYER - 1], refs[N_LAYER - 1 :]
    load_scales(msgs, scale)

    def step(i, carry):
        out_ref[pl.ds(CB_DEV * i, XQ, stride=RB_DEV * CB_DEV), :] = first_ref[i]
        out_ref[pl.ds(CB_DEV * i + 1, XQ, stride=RB_DEV * CB_DEV), :] = add_messages(own_ref, msgs, scale, i)
        return carry

    lax.fori_loop(0, RB_DEV, step, 0)


def combine(kernel, shape, parts, name):
    vmem = pl.BlockSpec(memory_space=pltpu.VMEM)
    return pl.pallas_call(
        kernel,
        out_shape=jax.ShapeDtypeStruct(shape, jnp.float32),
        in_specs=[vmem] * len(parts),
        out_specs=vmem,
        scratch_shapes=[pltpu.VMEM((N_LAYER - 1, RB_DEV, BS), jnp.float32)],
        compiler_params=pltpu.CompilerParams(vmem_limit_bytes=6 * 2**20),
        cost_estimate=pl.CostEstimate(flops=10**9, bytes_accessed=2**20, transcendentals=0),
        name=name,
    )(*parts)


def prepare_kernel(
    a_ref, rows_ref, ks_ref, live_ref, b_ref, cols_ref, a_out, zero_out, one_out, a_in, b_in, zero_in, one_in, sems
):
    load_b = pltpu.make_async_copy(b_ref, b_in, sems.at[0])
    load_a = pltpu.make_async_copy(a_ref, a_in.at[pl.ds(0, A_ROWS)], sems.at[1])
    load_b.start()
    load_a.start()
    lane = lax.broadcasted_iota(jnp.int32, (POS_ROWS, BS), 1)
    found = jnp.zeros((POS_ROWS, BS), jnp.int32)
    for s in range(SA):
        target = jnp.where(s < live_ref[0, 0, 0], rows_ref[s], RB_DEV)
        found = jnp.where(lane == s, target, found)
        found = jnp.where(lane == SA + s, ks_ref[s], found)
    a_in[pl.ds(A_ROWS, POS_ROWS), :] = found.astype(jnp.float32).astype(jnp.bfloat16)
    stores = [
        pltpu.make_async_copy(held, out, sems.at[2 + at])
        for at, (held, out) in enumerate(((zero_in, zero_out), (one_in, one_out), (a_in, a_out)))
    ]
    load_b.wait()
    for n in range(K_DEV):
        zero_in[n] = b_in[n, cols_ref[0, n]]
    stores[0].start()
    load_a.wait()
    stores[2].start()
    for n in range(K_DEV):
        one_in[n] = b_in[n, 1 - cols_ref[0, n]]
    stores[1].start()
    for store in stores:
        store.wait()


def prepare(a_vals, a_rows, a_ks, a_live, b_vals, b_cols):
    smem = pl.BlockSpec(memory_space=pltpu.SMEM)
    any_spec = pl.BlockSpec(memory_space=pl.ANY)
    a_send = jax.ShapeDtypeStruct((A_ROWS + POS_ROWS, BS), jnp.bfloat16)
    chunk = jax.ShapeDtypeStruct((K_DEV, BS, BS), jnp.bfloat16)
    return pl.pallas_call(
        prepare_kernel,
        out_shape=[a_send, chunk, chunk],
        in_specs=[any_spec, smem, smem, smem, any_spec, smem],
        out_specs=[any_spec] * 3,
        scratch_shapes=[
            pltpu.VMEM(a_send.shape, a_send.dtype),
            pltpu.VMEM((K_DEV, PB, BS, BS), jnp.bfloat16),
            pltpu.VMEM(chunk.shape, chunk.dtype),
            pltpu.VMEM(chunk.shape, chunk.dtype),
            pltpu.SemaphoreType.DMA((5,)),
        ],
        compiler_params=pltpu.CompilerParams(vmem_limit_bytes=60 * 2**20),
        name="prepare",
    )(
        a_vals.reshape(A_ROWS, BS),
        a_rows.reshape(SA),
        a_ks.reshape(SA),
        a_live,
        b_vals.reshape(K_DEV, PB, BS, BS),
        jnp.transpose(b_cols, (1, 2, 0)).reshape(PB, K_DEV),
    )


def shifted(value, axis, size, by):
    return lax.ppermute(value, axis, [(i, (i + by) % size) for i in range(size)])


def up(value):
    return shifted(value, "row", N_ROW, 1)


def down(value):
    return shifted(value, "row", N_ROW, -1)


def around(b_zero, b_one, hold, early, middle):
    zero, one = {0: b_zero}, {0: b_one}
    zero[7], one[1] = up(zero[0]), down(one[0])
    one[7], zero[1] = up(one[0]), down(zero[0])
    zero[6], one[2] = up(zero[7]), down(one[1])
    one[6], zero[2] = up(one[7]), down(zero[1])
    zero[5], one[3] = up(zero[6]), down(one[2])
    zero[2], *sums = hold(zero, one)
    zero[3] = down(zero[2])
    sums = early(zero, one, sums)
    zero[5], *sums = lax.optimization_barrier((zero[5], *sums))
    zero[4] = up(zero[5])
    sums = middle(zero, one, sums)
    one[3], one[6], *sums = lax.optimization_barrier((one[3], one[6], *sums))
    one[4], one[5] = down(one[3]), up(one[6])
    return zero, one, sums


def send_sums(parts):
    own, msgs = parts[0], parts[1:]
    sent = {q: shifted(msgs[q - 1], "layer", N_LAYER, q) for q in (2, 1, 3)}
    return [own, *sent.values()]


def body(a_vals, a_rows, a_ks, a_live, b_vals, b_cols):
    a_send, b_zero, b_one = prepare(a_vals, a_rows, a_ks, a_live, b_vals, b_cols)
    a_all = lax.all_gather(a_send, "col", axis=0)
    where = [positions(a_all), a_all]

    def hold(zero, one):
        sums = open_sums(where, (zero, one), (7, 1), ((), ()))
        return lax.optimization_barrier((zero[2], *sums))

    def early(zero, one, sums):
        return open_sums(where, (zero, one), (6, 2), ((), ()), sums)

    def middle(zero, one, sums):
        return open_sums(where, (zero, one), (0,), ((5,), (3,)), sums)

    zero, one, sums = around(b_zero, b_one, hold, early, middle)
    before = open_sums(where, (zero,), (), ((3,),), sums[:1])
    parts = send_sums(close_sums(where, zero, (4,), before[0], 2 * 10**10))
    first = combine(first_combine_kernel, (RB_DEV, XQ, BS), parts, "first_combine")
    parts = send_sums(close_sums(where, one, (4, 5), sums[1], 10**11))
    rows = XQ * RB_DEV * CB_DEV
    product = combine(last_combine_kernel, (rows, BS), [first] + parts, "last_combine")
    return product.reshape(XQ, RB_DEV, CB_DEV, BS)


def solution(mesh):
    return jax.shard_map(
        body,
        mesh=mesh,
        in_specs=(
            P("layer", "row", "col", None, None, None),
            P("layer", "row", "col", None),
            P("layer", "row", "col", None),
            P("layer", "row", "col"),
            P(("layer", "row"), "col", None, None, None),
            P(("layer", "row"), "col", None),
        ),
        out_specs=P("layer", "row", "col", None),
        check_vma=False,
    )
```

```python
import functools

import jax
import jax.numpy as jnp
from jax import lax
from jax.experimental import pallas as pl
from jax.experimental.pallas import tpu as pltpu
from jax.sharding import PartitionSpec as P

BS = 128
BLK_DEV = 8
SA = 12
PB = 2
RB_DEV = 32
CB_DEV = 2
N_LAYER = 4
N_ROW = 8
N_COL = 16
K_DEV = 16
XQ = BS // N_LAYER
A_ROWS = SA * BS
POS_ROWS = 16
MSG_ROWS = RB_DEV * XQ + RB_DEV
BITS = 13.0
LN2 = 0.6931471805599453


def piece_of(me, place):
    return lax.rem(me + place, N_ROW)


def add_products(place_ref, a_ref, places, acc, b_refs):
    row = lax.axis_index("row")
    for place, b_ref in zip(places, b_refs):

        def half(h, carry):
            col = 2 * piece_of(row, place) + h
            for s in range(SA):
                target = place_ref[col, s]
                k = place_ref[col, SA + s]
                acc[target] += jnp.dot(
                    a_ref[col, pl.ds(s * BS, BS), :],
                    b_ref[h * BLK_DEV + k],
                    preferred_element_type=jnp.float32,
                )
            return carry

        lax.fori_loop(0, 2, half, 0)


def add_both(place_ref, a_ref, places, accs, b_refs):
    row = lax.axis_index("row")
    for place, pair in zip(places, b_refs):

        def half(h, carry):
            col = 2 * piece_of(row, place) + h
            for s in range(SA):
                target = place_ref[col, s]
                k = place_ref[col, SA + s]
                block = a_ref[col, pl.ds(s * BS, BS), :]
                for acc, b_ref in zip(accs, pair):
                    acc[target] += jnp.dot(
                        block, b_ref[h * BLK_DEV + k], preferred_element_type=jnp.float32
                    )
            return carry

        lax.fori_loop(0, 2, half, 0)


def open_kernel(both, alone, resumed, place_ref, a_ref, *refs):
    width = len(alone)
    outs = refs[-width:]
    refs = list(refs[:-width])

    pairs = [[refs.pop(0) for _ in range(width)] for _ in both]
    singles = [[refs.pop(0) for _ in places] for places in alone]

    def load(i, carry):
        for c in range(width):
            outs[c][i] = refs[c][i] if resumed else jnp.zeros((BS, BS), jnp.float32)
        return carry

    lax.fori_loop(0, RB_DEV, load, 0)
    add_both(place_ref, a_ref, both, outs, pairs)
    for c in range(width):
        add_products(place_ref, a_ref, alone[c], outs[c], singles[c])


def close_kernel(places, place_ref, a_ref, *refs):
    count = len(places)
    before_ref, own_ref = refs[count : count + 2]
    msg_refs = refs[count + 2 : -2]
    acc, top = refs[-2:]
    layer = lax.axis_index("layer")

    def load(i, carry):
        acc[i] = before_ref[i]
        return carry

    lax.fori_loop(0, RB_DEV, load, 0)
    add_products(place_ref, a_ref, places, acc, refs[:count])

    def keep(i, carry):
        own_ref[i] = acc[i, pl.ds(layer * XQ, XQ), :]
        for q in range(1, N_LAYER):
            start = lax.rem(layer + q, N_LAYER) * XQ
            part = acc[i, pl.ds(start, XQ), :]
            top[q - 1, pl.ds(i, 1), :] = jnp.max(jnp.abs(part), axis=0, keepdims=True)
        return carry

    lax.fori_loop(0, RB_DEV, keep, 0)
    for q in range(1, N_LAYER):
        power = jnp.floor(jnp.log(jnp.maximum(top[q - 1], 1e-30)) * (1.0 / LN2))
        msg_refs[q - 1][pl.ds(RB_DEV * XQ, RB_DEV), :] = power.astype(jnp.int32).astype(jnp.int16)
        top[q - 1] = jnp.exp((BITS - power) * LN2)

    def pack(i, carry):
        for q in range(1, N_LAYER):
            start = lax.rem(layer + q, N_LAYER) * XQ
            part = acc[i, pl.ds(start, XQ), :] * top[q - 1, pl.ds(i, 1), :]
            msg_refs[q - 1][pl.ds(pl.multiple_of(i * XQ, XQ), XQ), :] = (
                jnp.round(part).astype(jnp.int32).astype(jnp.int16)
            )
        return carry

    lax.fori_loop(0, RB_DEV, pack, 0)


def positions_kernel(a_ref, place_ref, held, place, sem):
    copy = pltpu.make_async_copy(a_ref.at[:, pl.ds(A_ROWS, POS_ROWS)], held, sem)
    copy.start()
    copy.wait()
    for col in range(N_COL):
        place[pl.ds(col, 1), :] = held[col].astype(jnp.float32)[:1].astype(jnp.int32)
    copy = pltpu.make_async_copy(place, place_ref, sem)
    copy.start()
    copy.wait()


def positions(a_all):
    shape = (N_COL, BS)
    return pl.pallas_call(
        positions_kernel,
        out_shape=jax.ShapeDtypeStruct(shape, jnp.int32),
        in_specs=[pl.BlockSpec(memory_space=pl.ANY)],
        out_specs=pl.BlockSpec(memory_space=pltpu.SMEM),
        scratch_shapes=[
            pltpu.VMEM((N_COL, POS_ROWS, BS), jnp.bfloat16),
            pltpu.VMEM(shape, jnp.int32),
            pltpu.SemaphoreType.DMA(()),
        ],
        compiler_params=pltpu.CompilerParams(vmem_limit_bytes=50 * 2**20),
        cost_estimate=pl.CostEstimate(flops=5 * 10**9, bytes_accessed=2**20, transcendentals=0),
        name="positions",
    )(a_all)


def call_products(kernel, name, out_shape, scratch, operands, flops):
    smem = pl.BlockSpec(memory_space=pltpu.SMEM)
    vmem = pl.BlockSpec(memory_space=pltpu.VMEM)
    return pl.pallas_call(
        kernel,
        out_shape=out_shape,
        in_specs=[smem] + [vmem] * (len(operands) - 1),
        out_specs=[vmem] * len(out_shape),
        scratch_shapes=scratch,
        compiler_params=pltpu.CompilerParams(vmem_limit_bytes=6 * 2**20),
        cost_estimate=pl.CostEstimate(flops=flops, bytes_accessed=2**20, transcendentals=0),
        name=name,
    )(*operands)


def open_sums(where, chunks, both, alone, before=()):
    sums = jax.ShapeDtypeStruct((RB_DEV + 1, BS, BS), jnp.float32)
    blocks = [chunk[place] for place in both for chunk in chunks]
    blocks += [chunk[place] for chunk, places in zip(chunks, alone) for place in places]
    return call_products(
        functools.partial(open_kernel, both, alone, bool(before)),
        "open_sums",
        [sums] * len(chunks),
        [],
        [*where, *blocks, *before],
        5 * 10**9,
    )


def close_sums(where, chunk, places, before, flops):
    return call_products(
        functools.partial(close_kernel, places),
        "close_sums",
        [jax.ShapeDtypeStruct((RB_DEV, XQ, BS), jnp.float32)]
        + [jax.ShapeDtypeStruct((MSG_ROWS, BS), jnp.int16)] * (N_LAYER - 1),
        [
            pltpu.VMEM((RB_DEV + 1, BS, BS), jnp.float32),
            pltpu.VMEM((N_LAYER - 1, RB_DEV, BS), jnp.float32),
        ],
        [*where, *(chunk[place] for place in places), before],
        flops,
    )


def add_messages(own_ref, msgs, scale, i):
    total = own_ref[i]
    for q in range(N_LAYER - 1):
        part = msgs[q][pl.ds(pl.multiple_of(i * XQ, XQ), XQ), :]
        total = total + part.astype(jnp.int32).astype(jnp.float32) * scale[q, pl.ds(i, 1), :]
    return total


def load_scales(msgs, scale):
    for q in range(N_LAYER - 1):
        power = msgs[q][pl.ds(RB_DEV * XQ, RB_DEV), :].astype(jnp.int32).astype(jnp.float32)
        scale[q] = jnp.exp((power - BITS) * LN2)


def first_combine_kernel(own_ref, *refs):
    msgs, (out_ref, scale) = refs[: N_LAYER - 1], refs[N_LAYER - 1 :]
    load_scales(msgs, scale)

    def step(i, carry):
        out_ref[i] = add_messages(own_ref, msgs, scale, i)
        return carry

    lax.fori_loop(0, RB_DEV, step, 0)


def last_combine_kernel(first_ref, own_ref, *refs):
    msgs, (out_ref, scale) = refs[: N_LAYER - 1], refs[N_LAYER - 1 :]
    load_scales(msgs, scale)

    def step(i, carry):
        out_ref[pl.ds(CB_DEV * i, XQ, stride=RB_DEV * CB_DEV), :] = first_ref[i]
        out_ref[pl.ds(CB_DEV * i + 1, XQ, stride=RB_DEV * CB_DEV), :] = add_messages(own_ref, msgs, scale, i)
        return carry

    lax.fori_loop(0, RB_DEV, step, 0)


def combine(kernel, shape, parts, name):
    vmem = pl.BlockSpec(memory_space=pltpu.VMEM)
    return pl.pallas_call(
        kernel,
        out_shape=jax.ShapeDtypeStruct(shape, jnp.float32),
        in_specs=[vmem] * len(parts),
        out_specs=vmem,
        scratch_shapes=[pltpu.VMEM((N_LAYER - 1, RB_DEV, BS), jnp.float32)],
        compiler_params=pltpu.CompilerParams(vmem_limit_bytes=6 * 2**20),
        cost_estimate=pl.CostEstimate(flops=10**9, bytes_accessed=2**20, transcendentals=0),
        name=name,
    )(*parts)


def prepare_kernel(
    a_ref, rows_ref, ks_ref, live_ref, b_ref, cols_ref, a_out, zero_out, one_out, a_in, b_in, zero_in, one_in, sems
):
    load_b = pltpu.make_async_copy(b_ref, b_in, sems.at[0])
    load_a = pltpu.make_async_copy(a_ref, a_in.at[pl.ds(0, A_ROWS)], sems.at[1])
    load_b.start()
    load_a.start()
    lane = lax.broadcasted_iota(jnp.int32, (POS_ROWS, BS), 1)
    found = jnp.zeros((POS_ROWS, BS), jnp.int32)
    for s in range(SA):
        target = jnp.where(s < live_ref[0, 0, 0], rows_ref[s], RB_DEV)
        found = jnp.where(lane == s, target, found)
        found = jnp.where(lane == SA + s, ks_ref[s], found)
    a_in[pl.ds(A_ROWS, POS_ROWS), :] = found.astype(jnp.float32).astype(jnp.bfloat16)
    stores = [
        pltpu.make_async_copy(held, out, sems.at[2 + at])
        for at, (held, out) in enumerate(((zero_in, zero_out), (one_in, one_out), (a_in, a_out)))
    ]
    load_b.wait()
    for n in range(K_DEV):
        zero_in[n] = b_in[n, cols_ref[0, n]]
    stores[0].start()
    load_a.wait()
    stores[2].start()
    for n in range(K_DEV):
        one_in[n] = b_in[n, 1 - cols_ref[0, n]]
    stores[1].start()
    for store in stores:
        store.wait()


def prepare(a_vals, a_rows, a_ks, a_live, b_vals, b_cols):
    smem = pl.BlockSpec(memory_space=pltpu.SMEM)
    any_spec = pl.BlockSpec(memory_space=pl.ANY)
    a_send = jax.ShapeDtypeStruct((A_ROWS + POS_ROWS, BS), jnp.bfloat16)
    chunk = jax.ShapeDtypeStruct((K_DEV, BS, BS), jnp.bfloat16)
    return pl.pallas_call(
        prepare_kernel,
        out_shape=[a_send, chunk, chunk],
        in_specs=[any_spec, smem, smem, smem, any_spec, smem],
        out_specs=[any_spec] * 3,
        scratch_shapes=[
            pltpu.VMEM(a_send.shape, a_send.dtype),
            pltpu.VMEM((K_DEV, PB, BS, BS), jnp.bfloat16),
            pltpu.VMEM(chunk.shape, chunk.dtype),
            pltpu.VMEM(chunk.shape, chunk.dtype),
            pltpu.SemaphoreType.DMA((5,)),
        ],
        compiler_params=pltpu.CompilerParams(vmem_limit_bytes=60 * 2**20),
        name="prepare",
    )(
        a_vals.reshape(A_ROWS, BS),
        a_rows.reshape(SA),
        a_ks.reshape(SA),
        a_live,
        b_vals.reshape(K_DEV, PB, BS, BS),
        jnp.transpose(b_cols, (1, 2, 0)).reshape(PB, K_DEV),
    )


def shifted(value, axis, size, by):
    return lax.ppermute(value, axis, [(i, (i + by) % size) for i in range(size)])


def up(value):
    return shifted(value, "row", N_ROW, 1)


def down(value):
    return shifted(value, "row", N_ROW, -1)


def around(b_zero, b_one, hold, early, middle):
    zero, one = {0: b_zero}, {0: b_one}
    zero[7], one[1] = up(zero[0]), down(one[0])
    one[7], zero[1] = up(one[0]), down(zero[0])
    zero[6], one[2] = up(zero[7]), down(one[1])
    one[6], zero[2] = up(one[7]), down(zero[1])
    zero[5], one[3] = up(zero[6]), down(one[2])
    (zero[2],) = hold(zero[2])
    zero[3] = down(zero[2])
    sums = early(zero, one)
    zero[5], *sums = lax.optimization_barrier((zero[5], *sums))
    zero[4] = up(zero[5])
    sums = middle(zero, one, sums)
    one[3], one[6], *sums = lax.optimization_barrier((one[3], one[6], *sums))
    one[4], one[5] = down(one[3]), up(one[6])
    return zero, one, sums


def send_sums(parts, order):
    own, msgs = parts[0], parts[1:]
    sent = {q: shifted(msgs[q - 1], "layer", N_LAYER, q) for q in order}
    return [own, *sent.values()]


def body(a_vals, a_rows, a_ks, a_live, b_vals, b_cols):
    a_send, b_zero, b_one = prepare(a_vals, a_rows, a_ks, a_live, b_vals, b_cols)
    a_all = lax.all_gather(a_send, "col", axis=0)
    where = [positions(a_all), a_all]

    def hold(*behind):
        *behind, where[0] = lax.optimization_barrier((*behind, where[0]))
        return behind

    def early(zero, one):
        return open_sums(where, (zero, one), (7, 1), ((), ()))

    def middle(zero, one, sums):
        return open_sums(where, (zero, one), (6, 2, 0), ((5,), (3,)), sums)

    zero, one, sums = around(b_zero, b_one, hold, early, middle)
    before = open_sums(where, (zero,), (), ((3,),), sums[:1])
    parts = send_sums(close_sums(where, zero, (4,), before[0], 2 * 10**10), (1, 2, 3))
    first = combine(first_combine_kernel, (RB_DEV, XQ, BS), parts, "first_combine")
    parts = send_sums(close_sums(where, one, (4, 5), sums[1], 10**11), (2, 1, 3))
    rows = XQ * RB_DEV * CB_DEV
    product = combine(last_combine_kernel, (rows, BS), [first] + parts, "last_combine")
    return product.reshape(XQ, RB_DEV, CB_DEV, BS)


def solution(mesh):
    return jax.shard_map(
        body,
        mesh=mesh,
        in_specs=(
            P("layer", "row", "col", None, None, None),
            P("layer", "row", "col", None),
            P("layer", "row", "col", None),
            P("layer", "row", "col"),
            P(("layer", "row"), "col", None, None, None),
            P(("layer", "row"), "col", None),
        ),
        out_specs=P("layer", "row", "col", None),
        check_vma=False,
    )
```

```python
import functools

import jax
import jax.numpy as jnp
from jax import lax
from jax.experimental import pallas as pl
from jax.experimental.pallas import tpu as pltpu
from jax.sharding import PartitionSpec as P

BS = 128
BLK_DEV = 8
SA = 12
PB = 2
RB_DEV = 32
CB_DEV = 2
N_LAYER = 4
N_ROW = 8
N_COL = 16
K_DEV = 16
XQ = BS // N_LAYER
A_ROWS = SA * BS
POS_ROWS = 16
MSG_ROWS = RB_DEV * XQ + RB_DEV
BITS = 13.0
LN2 = 0.6931471805599453


def piece_of(me, place):
    return lax.rem(me + place, N_ROW)


def add_products(place_ref, a_ref, places, acc, b_refs):
    row = lax.axis_index("row")
    for place, b_ref in zip(places, b_refs):

        def half(h, carry):
            col = 2 * piece_of(row, place) + h
            for s in range(SA):
                target = place_ref[col, s]
                k = place_ref[col, SA + s]
                acc[target] += jnp.dot(
                    a_ref[col, pl.ds(s * BS, BS), :],
                    b_ref[h * BLK_DEV + k],
                    preferred_element_type=jnp.float32,
                )
            return carry

        lax.fori_loop(0, 2, half, 0)


def add_both(place_ref, a_ref, places, accs, b_refs):
    row = lax.axis_index("row")
    for place, pair in zip(places, b_refs):

        def half(h, carry):
            col = 2 * piece_of(row, place) + h
            for s in range(SA):
                target = place_ref[col, s]
                k = place_ref[col, SA + s]
                block = a_ref[col, pl.ds(s * BS, BS), :]
                for acc, b_ref in zip(accs, pair):
                    acc[target] += jnp.dot(
                        block, b_ref[h * BLK_DEV + k], preferred_element_type=jnp.float32
                    )
            return carry

        lax.fori_loop(0, 2, half, 0)


def open_kernel(both, alone, resumed, place_ref, a_ref, *refs):
    width = len(alone)
    outs = refs[-width:]
    refs = list(refs[:-width])

    pairs = [[refs.pop(0) for _ in range(width)] for _ in both]
    singles = [[refs.pop(0) for _ in places] for places in alone]

    def load(i, carry):
        for c in range(width):
            outs[c][i] = refs[c][i] if resumed else jnp.zeros((BS, BS), jnp.float32)
        return carry

    lax.fori_loop(0, RB_DEV, load, 0, unroll=4)
    add_both(place_ref, a_ref, both, outs, pairs)
    for c in range(width):
        add_products(place_ref, a_ref, alone[c], outs[c], singles[c])


def close_kernel(places, place_ref, a_ref, *refs):
    count = len(places)
    before_ref, own_ref = refs[count : count + 2]
    msg_refs = refs[count + 2 : -2]
    acc, top = refs[-2:]
    layer = lax.axis_index("layer")

    def load(i, carry):
        acc[i] = before_ref[i]
        return carry

    lax.fori_loop(0, RB_DEV, load, 0, unroll=4)
    add_products(place_ref, a_ref, places, acc, refs[:count])

    def keep(i, carry):
        own_ref[i] = acc[i, pl.ds(layer * XQ, XQ), :]
        for q in range(1, N_LAYER):
            start = lax.rem(layer + q, N_LAYER) * XQ
            part = acc[i, pl.ds(start, XQ), :]
            top[q - 1, pl.ds(i, 1), :] = jnp.max(jnp.abs(part), axis=0, keepdims=True)
        return carry

    lax.fori_loop(0, RB_DEV, keep, 0, unroll=4)
    for q in range(1, N_LAYER):
        power = jnp.floor(jnp.log(jnp.maximum(top[q - 1], 1e-30)) * (1.0 / LN2))
        msg_refs[q - 1][pl.ds(RB_DEV * XQ, RB_DEV), :] = power.astype(jnp.int32).astype(jnp.int16)
        top[q - 1] = jnp.exp((BITS - power) * LN2)

    def pack(i, carry):
        for q in range(1, N_LAYER):
            start = lax.rem(layer + q, N_LAYER) * XQ
            part = acc[i, pl.ds(start, XQ), :] * top[q - 1, pl.ds(i, 1), :]
            msg_refs[q - 1][pl.ds(pl.multiple_of(i * XQ, XQ), XQ), :] = (
                jnp.round(part).astype(jnp.int32).astype(jnp.int16)
            )
        return carry

    lax.fori_loop(0, RB_DEV, pack, 0, unroll=4)


def positions_kernel(a_ref, place_ref, held, place, sem):
    copy = pltpu.make_async_copy(a_ref.at[:, pl.ds(A_ROWS, POS_ROWS)], held, sem)
    copy.start()
    copy.wait()
    for col in range(N_COL):
        place[pl.ds(col, 1), :] = held[col].astype(jnp.float32)[:1].astype(jnp.int32)
    copy = pltpu.make_async_copy(place, place_ref, sem)
    copy.start()
    copy.wait()


def positions(a_all):
    shape = (N_COL, BS)
    return pl.pallas_call(
        positions_kernel,
        out_shape=jax.ShapeDtypeStruct(shape, jnp.int32),
        in_specs=[pl.BlockSpec(memory_space=pl.ANY)],
        out_specs=pl.BlockSpec(memory_space=pltpu.SMEM),
        scratch_shapes=[
            pltpu.VMEM((N_COL, POS_ROWS, BS), jnp.bfloat16),
            pltpu.VMEM(shape, jnp.int32),
            pltpu.SemaphoreType.DMA(()),
        ],
        compiler_params=pltpu.CompilerParams(vmem_limit_bytes=50 * 2**20),
        cost_estimate=pl.CostEstimate(flops=5 * 10**9, bytes_accessed=2**20, transcendentals=0),
        name="positions",
    )(a_all)


def call_products(kernel, name, out_shape, scratch, operands, flops):
    smem = pl.BlockSpec(memory_space=pltpu.SMEM)
    vmem = pl.BlockSpec(memory_space=pltpu.VMEM)
    return pl.pallas_call(
        kernel,
        out_shape=out_shape,
        in_specs=[smem] + [vmem] * (len(operands) - 1),
        out_specs=[vmem] * len(out_shape),
        scratch_shapes=scratch,
        compiler_params=pltpu.CompilerParams(vmem_limit_bytes=6 * 2**20),
        cost_estimate=pl.CostEstimate(flops=flops, bytes_accessed=2**20, transcendentals=0),
        name=name,
    )(*operands)


def open_sums(where, chunks, both, alone, before=()):
    sums = jax.ShapeDtypeStruct((RB_DEV + 1, BS, BS), jnp.float32)
    blocks = [chunk[place] for place in both for chunk in chunks]
    blocks += [chunk[place] for chunk, places in zip(chunks, alone) for place in places]
    return call_products(
        functools.partial(open_kernel, both, alone, bool(before)),
        "open_sums",
        [sums] * len(chunks),
        [],
        [*where, *blocks, *before],
        5 * 10**9,
    )


def close_sums(where, chunk, places, before, flops):
    return call_products(
        functools.partial(close_kernel, places),
        "close_sums",
        [jax.ShapeDtypeStruct((RB_DEV, XQ, BS), jnp.float32)]
        + [jax.ShapeDtypeStruct((MSG_ROWS, BS), jnp.int16)] * (N_LAYER - 1),
        [
            pltpu.VMEM((RB_DEV + 1, BS, BS), jnp.float32),
            pltpu.VMEM((N_LAYER - 1, RB_DEV, BS), jnp.float32),
        ],
        [*where, *(chunk[place] for place in places), before],
        flops,
    )


def add_messages(own_ref, msgs, scale, i):
    total = own_ref[i]
    for q in range(N_LAYER - 1):
        part = msgs[q][pl.ds(pl.multiple_of(i * XQ, XQ), XQ), :]
        total = total + part.astype(jnp.int32).astype(jnp.float32) * scale[q, pl.ds(i, 1), :]
    return total


def load_scales(msgs, scale):
    for q in range(N_LAYER - 1):
        power = msgs[q][pl.ds(RB_DEV * XQ, RB_DEV), :].astype(jnp.int32).astype(jnp.float32)
        scale[q] = jnp.exp((power - BITS) * LN2)


def first_combine_kernel(own_ref, *refs):
    msgs, (out_ref, scale) = refs[: N_LAYER - 1], refs[N_LAYER - 1 :]
    load_scales(msgs, scale)

    def step(i, carry):
        out_ref[i] = add_messages(own_ref, msgs, scale, i)
        return carry

    lax.fori_loop(0, RB_DEV, step, 0, unroll=4)


def last_combine_kernel(first_ref, own_ref, *refs):
    msgs, (out_ref, scale) = refs[: N_LAYER - 1], refs[N_LAYER - 1 :]
    load_scales(msgs, scale)

    def step(i, carry):
        out_ref[pl.ds(CB_DEV * i, XQ, stride=RB_DEV * CB_DEV), :] = first_ref[i]
        out_ref[pl.ds(CB_DEV * i + 1, XQ, stride=RB_DEV * CB_DEV), :] = add_messages(own_ref, msgs, scale, i)
        return carry

    lax.fori_loop(0, RB_DEV, step, 0, unroll=4)


def combine(kernel, shape, parts, name):
    vmem = pl.BlockSpec(memory_space=pltpu.VMEM)
    return pl.pallas_call(
        kernel,
        out_shape=jax.ShapeDtypeStruct(shape, jnp.float32),
        in_specs=[vmem] * len(parts),
        out_specs=vmem,
        scratch_shapes=[pltpu.VMEM((N_LAYER - 1, RB_DEV, BS), jnp.float32)],
        compiler_params=pltpu.CompilerParams(vmem_limit_bytes=6 * 2**20),
        cost_estimate=pl.CostEstimate(flops=10**9, bytes_accessed=2**20, transcendentals=0),
        name=name,
    )(*parts)


def prepare_kernel(
    a_ref, rows_ref, ks_ref, live_ref, b_ref, cols_ref, a_out, zero_out, one_out, a_in, b_in, zero_in, one_in, sems
):
    load_b = pltpu.make_async_copy(b_ref, b_in, sems.at[0])
    load_a = pltpu.make_async_copy(a_ref, a_in.at[pl.ds(0, A_ROWS)], sems.at[1])
    load_b.start()
    load_a.start()
    lane = lax.broadcasted_iota(jnp.int32, (POS_ROWS, BS), 1)
    found = jnp.zeros((POS_ROWS, BS), jnp.int32)
    for s in range(SA):
        target = jnp.where(s < live_ref[0, 0, 0], rows_ref[s], RB_DEV)
        found = jnp.where(lane == s, target, found)
        found = jnp.where(lane == SA + s, ks_ref[s], found)
    a_in[pl.ds(A_ROWS, POS_ROWS), :] = found.astype(jnp.float32).astype(jnp.bfloat16)
    stores = [
        pltpu.make_async_copy(held, out, sems.at[2 + at])
        for at, (held, out) in enumerate(((zero_in, zero_out), (one_in, one_out), (a_in, a_out)))
    ]
    load_b.wait()
    for n in range(K_DEV):
        zero_in[n] = b_in[n, cols_ref[0, n]]
    stores[0].start()
    load_a.wait()
    stores[2].start()
    for n in range(K_DEV):
        one_in[n] = b_in[n, 1 - cols_ref[0, n]]
    stores[1].start()
    for store in stores:
        store.wait()


def prepare(a_vals, a_rows, a_ks, a_live, b_vals, b_cols):
    smem = pl.BlockSpec(memory_space=pltpu.SMEM)
    any_spec = pl.BlockSpec(memory_space=pl.ANY)
    a_send = jax.ShapeDtypeStruct((A_ROWS + POS_ROWS, BS), jnp.bfloat16)
    chunk = jax.ShapeDtypeStruct((K_DEV, BS, BS), jnp.bfloat16)
    return pl.pallas_call(
        prepare_kernel,
        out_shape=[a_send, chunk, chunk],
        in_specs=[any_spec, smem, smem, smem, any_spec, smem],
        out_specs=[any_spec] * 3,
        scratch_shapes=[
            pltpu.VMEM(a_send.shape, a_send.dtype),
            pltpu.VMEM((K_DEV, PB, BS, BS), jnp.bfloat16),
            pltpu.VMEM(chunk.shape, chunk.dtype),
            pltpu.VMEM(chunk.shape, chunk.dtype),
            pltpu.SemaphoreType.DMA((5,)),
        ],
        compiler_params=pltpu.CompilerParams(vmem_limit_bytes=60 * 2**20),
        name="prepare",
    )(
        a_vals.reshape(A_ROWS, BS),
        a_rows.reshape(SA),
        a_ks.reshape(SA),
        a_live,
        b_vals.reshape(K_DEV, PB, BS, BS),
        jnp.transpose(b_cols, (1, 2, 0)).reshape(PB, K_DEV),
    )


def shifted(value, axis, size, by):
    return lax.ppermute(value, axis, [(i, (i + by) % size) for i in range(size)])


def up(value):
    return shifted(value, "row", N_ROW, 1)


def down(value):
    return shifted(value, "row", N_ROW, -1)


def around(b_zero, b_one, hold, early, middle):
    zero, one = {0: b_zero}, {0: b_one}
    zero[7], one[1] = up(zero[0]), down(one[0])
    one[7], zero[1] = up(one[0]), down(zero[0])
    zero[6], one[2] = up(zero[7]), down(one[1])
    one[6], zero[2] = up(one[7]), down(zero[1])
    zero[5], one[3] = up(zero[6]), down(one[2])
    (zero[2],) = hold(zero[2])
    zero[3] = down(zero[2])
    sums = early(zero, one)
    zero[5], *sums = lax.optimization_barrier((zero[5], *sums))
    zero[4] = up(zero[5])
    sums = middle(zero, one, sums)
    one[3], one[6], *sums = lax.optimization_barrier((one[3], one[6], *sums))
    one[4], one[5] = down(one[3]), up(one[6])
    return zero, one, sums


def send_sums(parts):
    own, msgs = parts[0], parts[1:]
    sent = {q: shifted(msgs[q - 1], "layer", N_LAYER, q) for q in (2, 1, 3)}
    return [own, *sent.values()]


def body(a_vals, a_rows, a_ks, a_live, b_vals, b_cols):
    a_send, b_zero, b_one = prepare(a_vals, a_rows, a_ks, a_live, b_vals, b_cols)
    a_all = lax.all_gather(a_send, "col", axis=0)
    where = [positions(a_all), a_all]

    def hold(*behind):
        *behind, where[0] = lax.optimization_barrier((*behind, where[0]))
        return behind

    def early(zero, one):
        return open_sums(where, (zero, one), (7, 1), ((), ()))

    def middle(zero, one, sums):
        return open_sums(where, (zero, one), (6, 2, 0), ((5,), (3,)), sums)

    zero, one, sums = around(b_zero, b_one, hold, early, middle)
    before = open_sums(where, (zero,), (), ((3,),), sums[:1])
    parts = send_sums(close_sums(where, zero, (4,), before[0], 2 * 10**10))
    first = combine(first_combine_kernel, (RB_DEV, XQ, BS), parts, "first_combine")
    parts = send_sums(close_sums(where, one, (4, 5), sums[1], 10**11))
    rows = XQ * RB_DEV * CB_DEV
    product = combine(last_combine_kernel, (rows, BS), [first] + parts, "last_combine")
    return product.reshape(XQ, RB_DEV, CB_DEV, BS)


def solution(mesh):
    return jax.shard_map(
        body,
        mesh=mesh,
        in_specs=(
            P("layer", "row", "col", None, None, None),
            P("layer", "row", "col", None),
            P("layer", "row", "col", None),
            P("layer", "row", "col"),
            P(("layer", "row"), "col", None, None, None),
            P(("layer", "row"), "col", None),
        ),
        out_specs=P("layer", "row", "col", None),
        check_vma=False,
    )
```
